256 devices in a mesh: seq: 16 (over z, core), fsdp: 16 (over x, y).
Axes of the slice: x: 4, y: 4, z: 8, core: 2. Of those that a mesh axis runs over, the one named last changes fastest.
Arguments:
- tokens: bfloat16 [2048, 8192], P('seq', 'fsdp'), may hold values from -6 to 6
- norm_gain: float32 [8192], replicated, may hold values from 0.25 to 1.75
- gate_proj: bfloat16 [8192, 8192], P('seq', 'fsdp'), may hold values from -0.0625 to 0.0625
- value_proj: bfloat16 [8192, 8192], P('seq', 'fsdp'), may hold values from -0.0625 to 0.0625
- step_proj: bfloat16 [8192, 128], P('seq', 'fsdp'), may hold values from -0.0625 to 0.0625
- state_proj: bfloat16 [8192, 4, 256], P('seq'), may hold values from -0.0625 to 0.0625
- conv_value: float32 [4, 8192], P(None, 'fsdp'), may hold values from -3 to 3
- conv_state: float32 [4, 4, 256], replicated, may hold values from -3 to 3
- step_bias: float32 [128], P('fsdp'), may hold values from -1 to 1
- decay_rate: float32 [128], P('fsdp'), may hold values from 0.00024414062 to 0.1
- skip_gain: float32 [128], P('fsdp'), may hold values from 0.5 to 1.5
- mix_gain: float32 [8192], P('fsdp'), may hold values from 0.25 to 1.75
- out_proj: bfloat16 [8192, 8192], P('fsdp', 'seq'), may hold values from -0.09375 to 0.09375
- doc_lengths: int32 [32], replicated, may hold values from 1 to 1024, 2048 in all
Outputs:
- layer_out: bfloat16 [2048, 8192], P('seq', 'fsdp')
The draws below stay inside these ranges and needn't reach their ends.
Inputs may be any that keep to these rules, and one draw needn't show every extreme that they name: `doc_lengths`: the longest document has exactly 1024 tokens, so it spans many stretches; the lengths sum to 2048.
All inputs are finite; a program needn't handle non-finite values.
Results may differ from the reference program's by a relative error of at most 0.014.
Values may be sent and summed in bfloat16 or wider, within the bound.
A program may use at most 128 MiB of HBM per device.

```python
import math
import jax
import jax.numpy as jnp
import numpy as np
from jax import lax

D = 8192
H = 128
HEAD_DIM = 64
N = 128
G = 4
TOKENS = 2048
DOCS = 32


def spiked(entries, own_key, source, target, blocks, factor):
    def block_of(position):
        return (jnp.arange(entries.shape[position]) // (entries.shape[position] // blocks)).reshape((-1,) + (1,) * (entries.ndim - 1 - position))

    one_side = jax.random.permutation(own_key, blocks)[block_of(target)]
    far = (block_of(target) + blocks // 2) % blocks
    return jnp.where((block_of(source) == one_side) | (block_of(source) == far), factor * entries, entries)


def block_scale(own_key, extent, split, smallest, largest):
    factor_of = 1.0
    for axis_at, shards_of in split:
        heights = jax.random.uniform(jax.random.fold_in(jax.random.fold_in(own_key, 6), axis_at), (shards_of,), jnp.float32, smallest / len(split), largest / len(split))
        factor_of = factor_of * jnp.repeat(jnp.exp(heights), extent[axis_at] // shards_of).reshape((-1,) + (1,) * (len(extent) - 1 - axis_at))
    return factor_of


def length_profile(count, total, limit, skew):
    portions = [(1 << 20) // math.isqrt(standing ** skew) + 1 for standing in range(2, count + 1)]
    rest, holding = total - limit - (count - 1), [1] * (count - 1)
    while rest > 0:
        free = [i for i in range(count - 1) if holding[i] < limit]
        pool, left = sum([portions[i] for i in free]), rest
        for i in free:
            more = min(limit - holding[i], max(1, left * portions[i] // pool), rest)
            holding[i] = holding[i] + more
            rest = rest - more
    return np.array([limit] + holding)


def ragged_sizes(rng, amount, total, reach, skew):
    if amount == 2:
        one = jax.random.randint(rng, (), max(1, total - reach), min(reach, total - 1) + 1)
        return jnp.stack([one, total - one])
    lengths = jnp.asarray(length_profile(amount, total, reach, skew), jnp.int32)
    couples = (amount - 1) // 2
    source_of, sink = lengths[1:1 + 2 * couples:2], lengths[2:2 + 2 * couples:2]
    room = jnp.minimum(source_of - 1, reach - sink)
    moved = jax.random.randint(jax.random.fold_in(rng, 1), (couples,), 0, 1 << 20) % (room + 1)
    lengths = lengths.at[1:1 + 2 * couples:2].set(source_of - moved).at[2:2 + 2 * couples:2].set(sink + moved)
    return lengths[jax.random.permutation(jax.random.fold_in(rng, 2), amount)]


def scatter_about(key, dims, scale, bound, split=(), kind=jnp.bfloat16):
    level = block_scale(key, dims, split, -0.22, 0.18) if split else 1.0
    drawn = jax.random.normal(key, dims, jnp.float32) * scale * level
    return jnp.minimum(jnp.maximum(drawn, -bound), bound).astype(kind)


def gaussian_with(rng, extent, scale, bound, cuts, heavy, held_as=jnp.bfloat16):
    drawn = scale * jax.random.normal(rng, extent, jnp.float32)
    if cuts:
        drawn = drawn * block_scale(rng, extent, cuts, -0.22, 0.18)
    return jnp.clip(spiked(drawn, jax.random.fold_in(rng, 3), *heavy), -bound, bound).astype(held_as)


def setup_inputs(seed: int = 0) -> dict:
    key_list = jax.random.split(jax.random.key(seed), 15)
    return {
        "tokens": scatter_about(key_list[0], (TOKENS, D), 1.0, 6.0, ((0, 16), (1, 16))),
        "norm_gain": jnp.clip(1.0 + 0.15 * jax.random.normal(key_list[1], (D,), jnp.float32), 0.25, 1.75),
        "gate_proj": scatter_about(key_list[2], (D, H * HEAD_DIM), D ** -0.5, 0.0625, ((0, 16), (1, 16))),
        "value_proj": scatter_about(key_list[3], (D, H * HEAD_DIM), D ** -0.5, 0.0625, ((0, 16), (1, 16))),
        "step_proj": scatter_about(key_list[4], (D, H), D ** -0.5, 0.0625, ((0, 16), (1, 16))),
        "state_proj": scatter_about(key_list[5], (D, G, 2 * N), D ** -0.5, 0.0625, ((0, 16),)),
        "conv_value": scatter_about(key_list[6], (4, H * HEAD_DIM), 4 ** -0.5, 3.0, ((1, 16),), jnp.float32),
        "conv_state": scatter_about(key_list[7], (4, G, 2 * N), 4 ** -0.5, 3.0, (), jnp.float32),
        "step_bias": jnp.clip(jax.random.uniform(key_list[8], (H,), jnp.float32, -1.0, 1.0) * block_scale(key_list[8], (H,), ((0, 16),), -0.4, 0.0), -1.0, 1.0),
        "decay_rate": jnp.clip(jnp.exp(math.log(0.1) - 6.015181 * jax.random.uniform(key_list[9], (H,), jnp.float32) ** block_scale(key_list[9], (H,), ((0, 16),), -0.2, 0.2)), 0.00024414062, 0.1),
        "skip_gain": jnp.clip(0.5 + 1.0 * jax.random.uniform(key_list[10], (H,), jnp.float32) ** block_scale(key_list[10], (H,), ((0, 16),), -0.2, 0.2), 0.5, 1.5),
        "mix_gain": jnp.clip(1.0 + 0.15 * jax.random.normal(key_list[11], (H * HEAD_DIM,), jnp.float32), 0.25, 1.75),
        "out_proj": gaussian_with(key_list[12], (H * HEAD_DIM, D), (H * HEAD_DIM) ** -0.5, 0.09375, ((0, 16), (1, 16)), (0, 1, 16, 2.0)),
        "doc_lengths": ragged_sizes(key_list[13], DOCS, TOKENS, TOKENS // 2, 2).astype(jnp.int32),
    }


EPSILON = 1e-05
PRECISE = lax.Precision.HIGHEST

def reference(tokens, norm_gain, gate_proj, value_proj, step_proj, state_proj, conv_value, conv_state, step_bias, decay_rate, skip_gain, mix_gain, out_proj, doc_lengths):
    as_float = tokens.astype(jnp.float32)
    normed = (as_float * lax.rsqrt(lax.optimization_barrier(jnp.mean(as_float * as_float, axis=1, keepdims=True)) + EPSILON) * norm_gain).astype(jnp.bfloat16)
    gate = jnp.dot(normed, gate_proj, preferred_element_type=jnp.float32)
    raw_step = jnp.dot(normed, step_proj, preferred_element_type=jnp.float32)
    raw_values = jnp.dot(normed, value_proj, preferred_element_type=jnp.float32).astype(jnp.bfloat16)
    raw_states = jnp.dot(normed, state_proj.reshape(D, G * 2 * N), preferred_element_type=jnp.float32).astype(jnp.bfloat16).reshape(TOKENS, G, 2 * N)
    starts = (jnp.cumsum(doc_lengths) - doc_lengths).astype(jnp.int32)
    positions = jnp.arange(-3, TOKENS, dtype=jnp.int32)
    segment_ext = lax.optimization_barrier(jnp.sum(starts[None, :] <= positions[:, None], axis=1)).astype(jnp.int32) - 1
    segment = segment_ext[3:]
    padded_values = jnp.concatenate([jnp.zeros((3, H * HEAD_DIM), jnp.bfloat16), raw_values], axis=0)
    padded_states = jnp.concatenate([jnp.zeros((3, G, 2 * N), jnp.bfloat16), raw_states], axis=0)
    conv_values = jnp.zeros((TOKENS, H * HEAD_DIM), jnp.float32)
    conv_states = jnp.zeros((TOKENS, G, 2 * N), jnp.float32)
    for offset in range(4):
        same_doc = segment_ext[offset:offset + TOKENS] == segment
        conv_values = conv_values + jnp.where(same_doc[:, None], padded_values[offset:offset + TOKENS].astype(jnp.float32), 0.0) * conv_value[offset]
        conv_states = conv_states + jnp.where(same_doc[:, None, None], padded_states[offset:offset + TOKENS].astype(jnp.float32), 0.0) * conv_state[offset]
    rounded_values = lax.optimization_barrier(jax.nn.silu(conv_values).astype(jnp.bfloat16))
    rounded_states = lax.optimization_barrier(jax.nn.silu(conv_states).astype(jnp.bfloat16))
    inputs = rounded_values.astype(jnp.float32).reshape(TOKENS, H, HEAD_DIM)
    maps = rounded_states.astype(jnp.float32)
    in_map = maps[:, :, :N]
    out_map = maps[:, :, N:]
    step_size = jax.nn.softplus(raw_step + step_bias)
    log_decay = -decay_rate * step_size
    is_start = jnp.any(positions[3:, None] == starts[None, :], axis=1)
    per_group = H // G

    def advance(state, column):
        value_now, in_now, out_now, size_now, decay_now, start_now = column
        in_heads = jnp.repeat(in_now, per_group, axis=0)
        out_heads = jnp.repeat(out_now, per_group, axis=0)
        keep = jnp.where(start_now, 0.0, jnp.exp(decay_now))
        state = keep[:, None, None] * state + (size_now[:, None] * value_now)[:, :, None] * in_heads[:, None, :]
        return (state, jnp.einsum('hpn,hn->hp', state, out_heads, precision=PRECISE))
    initial = jnp.zeros((H, HEAD_DIM, N), jnp.float32)
    _, history = lax.scan(advance, initial, (inputs, in_map, out_map, step_size, log_decay, is_start))
    outputs = history + skip_gain[None, :, None] * inputs
    gated = outputs.reshape(TOKENS, H * HEAD_DIM) * jax.nn.silu(gate)
    grouped = gated.reshape(TOKENS, G, H * HEAD_DIM // G)
    mean_square = lax.optimization_barrier(jnp.mean(grouped * grouped, axis=2, keepdims=True))
    scaled = ((grouped * lax.rsqrt(mean_square + EPSILON)).reshape(TOKENS, H * HEAD_DIM) * mix_gain).astype(jnp.bfloat16)
    mixed = jnp.dot(scaled, out_proj, preferred_element_type=jnp.float32)
    return (as_float + mixed).astype(jnp.bfloat16)
```

```python
import jax
import jax.numpy as jnp
from jax import lax
from jax.experimental import pallas as pl
from jax.experimental.pallas import tpu as pltpu
from jax.sharding import PartitionSpec as P

N = 128
EPSILON = 1e-05
PRECISE = lax.Precision.HIGHEST
MESH = pl.DeviceIdType.MESH
F32 = jnp.float32
BF16 = jnp.bfloat16
WIDE = 640
STEP0 = 32
SQ = 36
SENDS = 200


def dot(a, b, precision=None):
    return jnp.dot(a, b, preferred_element_type=F32, precision=precision)


def body(
    tok, gain, gate_w, value_w, extra_w, conv_v, conv_s, mix_gain, out_w,
    bias, rate, skip, docs,
    out,
    X, W, WS, PS, SL, SS, RL, RS, R, HS, HR, EXT, BC, ST, SR, SO, SI, GS, SQB, GZ, T, Q, A1, B1, C1, RA1, RB1, RC1,
    A2, B2, C2, RA2, RB2, RC2, FO, FR,
    sem_send, sem_a, sem_y, sem_x, sem_s, sem_w, sem_l, sem_sh, sem_h, sem_bc, sem_st, sem_in, sem_sq, sem_g, sem_gs,
    sem_1, sem_2, sem_f, sem_loc,
):
    s = lax.axis_index("seq")
    f = lax.axis_index("fsdp")
    z, c = lax.div(s, 2), lax.rem(s, 2)
    x, y = lax.div(f, 4), lax.rem(f, 4)
    sg = 1 - 2 * c

    def m4(v):
        return lax.rem(v + 8, 4)

    def m8(v):
        return lax.rem(v + 16, 8)

    def dev(z_=z, c_=c, x_=x, y_=y):
        return (2 * z_ + c_, 4 * x_ + y_)

    sibling = dev(c_=1 - c)
    started = []

    def send(src, dst, sem, to):
        copy = pltpu.make_async_remote_copy(
            src_ref=src, dst_ref=dst, send_sem=sem_send.at[len(started)], recv_sem=sem,
            device_id=to, device_id_type=MESH,
        )
        copy.start()
        started.append((copy, None))

    def arrived(dst, sem):
        pltpu.make_async_remote_copy(
            src_ref=dst, dst_ref=dst, send_sem=sem_send.at[0], recv_sem=sem,
            device_id=sibling, device_id_type=MESH,
        ).wait_recv()

    def send_or_keep(own, src, dst, sem, to):
        copy = pltpu.make_async_remote_copy(
            src_ref=src, dst_ref=dst, send_sem=sem_send.at[len(started)], recv_sem=sem,
            device_id=to, device_id_type=MESH,
        )
        away = jnp.logical_not(own)

        @pl.when(away)
        def _():
            copy.start()

        @pl.when(own)
        def _():
            pltpu.make_async_copy(src, dst, sem).start()

        started.append((copy, away))

    for i in range(8):
        px, py = 2 * c + i // 4, i % 4
        own = (f == s) & (f == 8 * c + i)
        send_or_keep(
            own, tok.at[pl.ds(16 * i, 16)], X.at[lax.rem(f, 2), px, py, z], sem_a.at[z], (f, 4 * px + py)
        )

    gain_col = jnp.transpose(
        jnp.broadcast_to(gain[0:1, pl.ds(pl.multiple_of(512 * s, 512), 512)], (128, 512))
    )[:, 0:1]

    def rows_of(half, ref):
        cols = pl.ds(pl.multiple_of(256 * half, 256), 256)
        ref[:, 0:256] = (gate_w[:, cols].astype(F32) * gain_col).astype(BF16)
        ref[:, 256:512] = (value_w[:, cols].astype(F32) * gain_col).astype(BF16)
        ref[:, 512:640] = (extra_w[half].astype(F32) * gain_col).astype(BF16)

    rows_of(1 - c, WS)
    send(WS, W.at[c], sem_w, sibling)
    rows_of(c, W.at[c])

    lane8 = lax.broadcasted_iota(jnp.int32, (8, 128), 1)
    starts = jnp.full((8, 128), 1 << 20, jnp.int32)
    total = jnp.int32(0)
    for i in range(32):
        starts = jnp.where(lane8 == i, total, starts)
        total = total + docs[i]
    starts = starts.astype(F32)[0:1]
    first = (256 * z).astype(F32)
    t_wide = first + lax.broadcasted_iota(jnp.int32, (256, 128), 0).astype(F32)
    start_of = jnp.max(jnp.where(starts <= t_wide, starts, 0.0), axis=1, keepdims=True)
    t_col = t_wide[:, 0:1]
    into = t_col - start_of
    row8 = lane8
    bias_row = jnp.zeros((8, 128), F32)
    rate_row = jnp.zeros((8, 128), F32)
    lane_256 = lax.broadcasted_iota(jnp.int32, (8, 256), 1)
    skip_row = jnp.zeros((8, 256), F32)
    for i in range(4):
        bias_row = jnp.where(row8 == STEP0 + i, bias[4 * c + i], bias_row)
        rate_row = jnp.where(row8 == STEP0 + i, rate[4 * c + i], rate_row)
        skip_row = jnp.where(lax.div(lane_256, 64) == i, skip[4 * c + i], skip_row)
    bias_row, rate_row, skip_row = bias_row[0:1], rate_row[0:1], skip_row[0:1]

    for zt in range(8):
        arrived(X.at[c, x, y, zt], sem_a.at[zt])
    mine = X.at[c, x, y]
    send(mine, mine, sem_y.at[y], dev(y_=m4(y + 1)))
    send(mine, mine, sem_y.at[y], dev(y_=m4(y - 1)))
    near = X.at[c, x, m4(y - sg)]
    arrived(near, sem_y.at[m4(y - sg)])
    send(near, near, sem_y.at[m4(y - sg)], dev(y_=m4(y + sg)))
    arrived(X.at[c, x, m4(y + sg)], sem_y.at[m4(y + sg)])
    arrived(X.at[c, x, m4(y + 2)], sem_y.at[m4(y + 2)])
    mine = X.at[c, x]
    send(mine, mine, sem_s.at[x], sibling)
    send(mine, mine, sem_x.at[x], dev(x_=m4(x + 1)))
    send(mine, mine, sem_x.at[x], dev(x_=m4(x - 1)))
    arrived(W.at[1 - c], sem_w)

    lane_e = lax.broadcasted_iota(jnp.int32, (256, 128), 1)

    def product(g, xg):
        other = X.at[1 - c, xg]
        arrived(other, sem_s.at[xg])

        def half(i, carry):
            a = X[0, xg, pl.ds(2 * i, 2)].reshape(256, 512)
            b = X[1, xg, pl.ds(2 * i, 2)].reshape(256, 512)
            p = dot(a, W[0]) + dot(b, W[1])
            a, b = a.astype(F32), b.astype(F32)
            squares = jnp.sum(a * a + b * b, axis=1, keepdims=True)
            PS[g, pl.ds(2 * i, 2), :, :, 0:512] = p[:, 0:512].reshape(2, 8, 16, 512)
            PS[g, pl.ds(2 * i, 2), :, :, 512:640] = (
                p[:, 512:640] + jnp.where(lane_e == SQ, squares, 0.0)
            ).reshape(2, 8, 16, 128)
            return carry

        lax.fori_loop(0, 2, half, 0)

    def hop(g, k):
        if k:
            arrived(RL.at[g, k - 1], sem_l.at[g, k - 1])
        long = PS[g, :, m8(z + (4 - k) * sg)]
        SL[g, k] = (long + RL[g, k - 1].astype(F32) if k else long).astype(BF16)
        send(SL.at[g, k], RL.at[g, k], sem_l.at[g, k], dev(z_=m8(z + sg)))
        if k < 3:
            if k:
                arrived(RS.at[g, k - 1], sem_sh.at[g, k - 1])
            short = PS[g, :, m8(z - (3 - k) * sg)]
            SS[g, k] = (short + RS[g, k - 1].astype(F32) if k else short).astype(BF16)
            send(SS.at[g, k], RS.at[g, k], sem_sh.at[g, k], dev(z_=m8(z - sg)))

    def last(g, xg):
        arrived(RL.at[g, 3], sem_l.at[g, 3])
        arrived(RS.at[g, 2], sem_sh.at[g, 2])
        R[xg] = PS[g, :, z] + RL[g, 3].astype(F32) + RS[g, 2].astype(F32)

    groups = [x, m4(x - sg), m4(x + sg), m4(x + 2)]

    def came(j):
        got = X.at[c, groups[j]]
        arrived(got, sem_x.at[groups[j]])
        if j == 1:
            send(got, got, sem_x.at[groups[j]], dev(x_=m4(x + sg)))
        send(got, got, sem_s.at[groups[j]], sibling)

    product(0, groups[0])
    for k in range(4):
        hop(0, k)
    came(1)
    came(2)
    product(1, groups[1])
    hop(1, 0)
    last(0, groups[0])
    product(2, groups[2])
    hop(2, 0)
    hop(1, 1)
    hop(2, 1)
    hop(1, 2)
    hop(2, 2)
    hop(1, 3)
    came(3)
    product(3, groups[3])
    hop(3, 0)
    hop(2, 3)
    last(1, groups[1])
    hop(3, 1)
    last(2, groups[2])
    hop(3, 2)
    hop(3, 3)
    last(3, groups[3])

    scale = lax.rsqrt(R[:, :, :, 512:640].reshape(256, 128)[:, SQ : SQ + 1] * (1.0 / 8192) + EPSILON)
    raw = (R[:, :, :, 256:640].reshape(256, 384) * scale).astype(BF16)
    HS[...] = raw[240:256]
    send(HS, HR, sem_h, dev(z_=m8(z + 1)))
    EXT[16:272] = raw.astype(F32)
    gate = R[:, :, :, 0:256].reshape(256, 256) * scale
    GS[...] = gate * jax.nn.sigmoid(gate)

    raw_step = R[:, :, :, 512:640].reshape(256, 128) * scale + bias_row
    step = jnp.maximum(raw_step, 0.0) + jnp.log1p(jnp.exp(-jnp.abs(raw_step)))
    log_decay = -rate_row * step
    order_r = lax.broadcasted_iota(jnp.int32, (256, 256), 0)
    order_c = lax.broadcasted_iota(jnp.int32, (256, 256), 1)
    cum = dot((order_r >= order_c).astype(F32), log_decay, PRECISE)
    cum_rows = jnp.transpose(cum)
    end = cum[255:256]
    causal = (order_r >= order_c) & (first + order_c.astype(F32) >= start_of)
    start_last = start_of[255:256]
    low = lax.broadcasted_iota(jnp.int32, (1, 128), 1) < 64

    def expand(a):
        return jnp.concatenate(
            [
                jnp.where(low, a[:, STEP0 + 2 * i : STEP0 + 2 * i + 1], a[:, STEP0 + 2 * i + 1 : STEP0 + 2 * i + 2])
                for i in range(2)
            ],
            axis=1,
        )

    step_wide = expand(step)
    tail = expand(jnp.where(t_col >= start_last, jnp.exp(end - cum), 0.0))
    carried = expand(jnp.where(start_of < first, jnp.exp(cum), 0.0))
    passing = expand(jnp.where(start_last < first, jnp.exp(end), 0.0))

    arrived(HR, sem_h)
    EXT[0:16] = HR[...].astype(F32)

    def conv(lo, width, taps):
        acc = jnp.zeros((256, width), F32)
        for k in range(4):
            acc = acc + jnp.where(into >= 3 - k, EXT[13 + k : 269 + k, lo : lo + width], 0.0) * taps[k]
        return acc * jax.nn.sigmoid(acc)

    turn = lax.rem(128 - 32 * y, 128)
    maps_cols = pl.ds(pl.multiple_of(128 * c, 128), 128)
    group_row = lax.broadcasted_iota(jnp.int32, (4, 128), 0) == x
    taps_s = [
        pltpu.roll(
            jnp.broadcast_to(
                jnp.sum(jnp.where(group_row, conv_s[k, :, maps_cols], 0.0), axis=0, keepdims=True), (8, 128)
            ),
            turn,
            1,
        )[0:1]
        for k in range(4)
    ]
    maps = jnp.transpose(conv(256, 128, taps_s))[0:32].astype(BF16)
    BC[c, y] = maps
    peers = [(dc, dy) for dc in range(2) for dy in range(4) if (dc, dy) != (0, 0)]
    for dc, dy in peers:
        to_c = lax.rem(c + dc, 2)
        send(BC.at[c, y], BC.at[c, y], sem_bc.at[4 * c + y], dev(c_=to_c, y_=m4(y + dy)))

    own_cols = pl.ds(pl.multiple_of(256 * c, 256), 256)
    inputs = conv(0, 256, [conv_v[k : k + 1, own_cols] for k in range(4)]).astype(BF16).astype(F32)
    stepped = inputs * step_wide
    to_end = (stepped * tail).astype(BF16)
    stepped = stepped.astype(BF16)

    for dc, dy in peers:
        pc, py = lax.rem(c + dc, 2), m4(y + dy)
        arrived(BC.at[pc, py], sem_bc.at[4 * pc + py])
    b_rows = BC[0].reshape(128, 256)
    c_cols = jnp.transpose(BC[1].reshape(128, 256).astype(F32)).astype(BF16)

    state = dot(b_rows, to_end).astype(BF16)
    ST[:, 0:16] = state.reshape(8, 16, 256)
    ST[:, 16:32] = jnp.broadcast_to(passing.astype(BF16)[None], (8, 16, 256))
    for o in range(1, 8):
        k = m8(z + o)
        send(ST.at[k], SR.at[z], sem_st.at[z], dev(z_=k))
    SR[z] = ST[z]

    scores = dot(c_cols, b_rows)
    parts = []
    for i in range(4):
        gaps = cum[:, STEP0 + i : STEP0 + i + 1] - cum_rows[STEP0 + i : STEP0 + i + 1, :]
        mixing = (jnp.exp(jnp.where(causal, gaps, -1e30)) * scores).astype(BF16)
        parts.append(dot(mixing, stepped[:, 128 * (i // 2) : 128 * (i // 2) + 128]))
    intra = jnp.concatenate([jnp.where(low, parts[0], parts[1]), jnp.where(low, parts[2], parts[3])], axis=1)
    partly = intra + skip_row * inputs

    for o in range(1, 8):
        k = m8(z + o)
        arrived(SR.at[k], sem_st.at[k])
    incoming = jnp.zeros((16, 256), F32)
    for i in range(8):
        SO[i] = incoming.astype(BF16)
        incoming = SR[i, 16:32].astype(F32) * incoming + SR[i, 0:16].astype(F32)
    for o in range(1, 8):
        k = m8(z + o)
        send(SO.at[k], SI.at[z], sem_in.at[z], dev(z_=k))
    SI[z] = SO[z]
    for o in range(1, 8):
        k = m8(z + o)
        arrived(SI.at[k], sem_in.at[k])
    outputs = partly + dot(c_cols, SI[...].reshape(128, 256)) * carried
    gated = outputs * GS[...]

    own_sq = 2 * y + c
    SQB[own_sq] = lax.dot_general(
        jnp.ones((8, 256), F32), gated * gated, (((1,), (1,)), ((), ())), preferred_element_type=F32, precision=PRECISE
    )
    for dc, dy in peers:
        send(SQB.at[own_sq], SQB.at[own_sq], sem_sq.at[own_sq], dev(c_=lax.rem(c + dc, 2), y_=m4(y + dy)))
    for dc, dy in peers:
        k = 2 * m4(y + dy) + lax.rem(c + dc, 2)
        arrived(SQB.at[k], sem_sq.at[k])
    squares = jnp.sum(SQB[...], axis=0)
    norm = lax.rsqrt(squares * (1.0 / 2048) + EPSILON)
    norm = jnp.transpose(jnp.concatenate([norm] * 16, axis=0))[:, 0:1]
    GZ[c, z] = (gated * norm * mix_gain[0:1, own_cols]).astype(BF16)

    order = [z]
    for k in range(1, 4):
        order += [m8(z - k * sg), m8(z + k * sg)]
    order.append(m8(z + 4))
    block = GZ.at[c, z]
    send(block, block, sem_g.at[z], dev(z_=m8(z + sg)))
    send(block, block, sem_g.at[z], dev(z_=m8(z - sg)))
    send(block, block, sem_gs.at[z], sibling)

    def pass_on(o):
        zt = order[o]
        got = GZ.at[c, zt]
        arrived(got, sem_g.at[zt])
        if o in (1, 3, 5):
            send(got, got, sem_g.at[zt], dev(z_=m8(z + sg)))
        if o in (2, 4):
            send(got, got, sem_g.at[zt], dev(z_=m8(z - sg)))
        send(got, got, sem_gs.at[zt], sibling)

    def take(o):
        zt = order[o]
        if o % 2 == 1:
            pass_on(o)
            if o < 7:
                pass_on(o + 1)
        arrived(GZ.at[1 - c, zt], sem_gs.at[zt])
        T[o] = (dot(GZ[0, zt], out_w[0:256]) + dot(GZ[1, zt], out_w[256:512])).reshape(4, 4, 16, 512)

    def along(o, level):
        over_x = (o % 2 == 0) == (level == 1)
        p = x if over_x else y

        def to(q):
            return dev(x_=q) if over_x else dev(y_=q)

        return p, to

    def quarter(o, q):
        return T[o, q] if o % 2 == 0 else T[o, :, q]

    def first_out(o):
        p, to = along(o, 1)
        A1[o] = quarter(o, m4(p + 2)).astype(BF16)
        send(A1.at[o], RA1.at[o], sem_1.at[o, 0], to(m4(p + sg)))
        B1[o] = quarter(o, m4(p - sg)).astype(BF16)
        send(B1.at[o], RB1.at[o], sem_1.at[o, 1], to(m4(p - sg)))

    def first_relay(o):
        p, to = along(o, 1)
        arrived(RA1.at[o], sem_1.at[o, 0])
        C1[o] = (quarter(o, m4(p + sg)) + RA1[o].astype(F32)).astype(BF16)
        send(C1.at[o], RC1.at[o], sem_1.at[o, 2], to(m4(p + sg)))

    def second_out(o):
        p, _ = along(o, 1)
        arrived(RB1.at[o], sem_1.at[o, 1])
        arrived(RC1.at[o], sem_1.at[o, 2])
        Q[o] = quarter(o, p) + RB1[o].astype(F32) + RC1[o].astype(F32)
        p, to = along(o, 2)
        A2[o] = Q[o, m4(p + 2)].astype(BF16)
        send(A2.at[o], RA2.at[o], sem_2.at[o, 0], to(m4(p + sg)))
        B2[o] = Q[o, m4(p - sg)].astype(BF16)
        send(B2.at[o], RB2.at[o], sem_2.at[o, 1], to(m4(p - sg)))

    def second_relay(o):
        p, to = along(o, 2)
        arrived(RA2.at[o], sem_2.at[o, 0])
        C2[o] = (Q[o, m4(p + sg)] + RA2[o].astype(F32)).astype(BF16)
        send(C2.at[o], RC2.at[o], sem_2.at[o, 2], to(m4(p + sg)))

    block_at = f
    row_block = lax.rem(block_at, 8)
    to_core = lax.div(block_at, 8)

    def finish(o):
        p, _ = along(o, 2)
        arrived(RB2.at[o], sem_2.at[o, 1])
        arrived(RC2.at[o], sem_2.at[o, 2])
        FO[o] = (Q[o, p] + RB2[o].astype(F32) + RC2[o].astype(F32)).astype(BF16)
        to = (2 * order[o] + to_core, s)
        own = (to[0] == s) & (s == f) if o == 0 else None
        if own is None:
            send(FO.at[o], FR.at[row_block], sem_f.at[row_block], to)
        else:
            send_or_keep(own, FO.at[o], FR.at[row_block], sem_f.at[row_block], to)

    for tick in range(8 + 4):
        if tick < 8:
            take(tick)
            first_out(tick)
        if 0 <= tick - 1 < 8:
            first_relay(tick - 1)
        if 0 <= tick - 2 < 8:
            second_out(tick - 2)
        if 0 <= tick - 3 < 8:
            second_relay(tick - 3)
        if 0 <= tick - 4 < 8:
            finish(tick - 4)

    for i in range(8):
        arrived(FR.at[i], sem_f.at[i])
    out[...] = (tok[...].astype(F32) + FR[...].reshape(128, 512).astype(F32)).astype(BF16)

    for copy, away in started:
        if away is None:
            copy.wait_send()
        else:

            @pl.when(away)
            def _(copy=copy):
                copy.wait_send()

    assert len(started) <= SENDS


def local(
    tokens, norm_gain, gate_proj, value_proj, step_proj, state_proj, conv_value, conv_state, step_bias, decay_rate,
    skip_gain, mix_gain, out_proj, doc_lengths,
):
    f = lax.axis_index("fsdp")
    x, y = f // 4, f % 4
    rows = state_proj.shape[0]
    halves = []
    for core in range(2):
        maps = lax.dynamic_slice(state_proj, (0, x, 128 * core + 32 * y), (rows, 1, 32))[:, 0]
        halves.append(
            jnp.concatenate([maps, step_proj[:, 4 * core : 4 * core + 4], jnp.zeros((rows, 92), BF16)], axis=1)
        )
    extra = jnp.stack(halves)
    vmem = pl.BlockSpec(memory_space=pltpu.VMEM)
    smem = pl.BlockSpec(memory_space=pltpu.SMEM)

    def buf(*shape, dtype=BF16):
        return pltpu.VMEM(shape, dtype)

    def dma(*shape):
        return pltpu.SemaphoreType.DMA(shape)

    return pl.pallas_call(
        body,
        out_shape=jax.ShapeDtypeStruct((128, 512), BF16),
        in_specs=[vmem] * 9 + [smem] * 4,
        out_specs=vmem,
        scratch_shapes=[
            buf(2, 4, 4, 8, 16, 512),
            buf(2, 512, WIDE),
            buf(512, WIDE),
            buf(4, 4, 8, 16, WIDE, dtype=F32),
            buf(4, 4, 4, 16, WIDE),
            buf(4, 3, 4, 16, WIDE),
            buf(4, 4, 4, 16, WIDE),
            buf(4, 3, 4, 16, WIDE),
            buf(4, 4, 16, WIDE, dtype=F32),
            buf(16, 384),
            buf(16, 384),
            buf(272, 384, dtype=F32),
            buf(2, 4, 32, 256),
            buf(8, 32, 256),
            buf(8, 32, 256),
            buf(8, 16, 256),
            buf(8, 16, 256),
            buf(256, 256, dtype=F32),
            buf(8, 8, 256, dtype=F32),
            buf(2, 8, 256, 256),
            buf(8, 4, 4, 16, 512, dtype=F32),
            buf(8, 4, 16, 512, dtype=F32),
        ]
        + [buf(8, 4, 16, 512)] * 6
        + [buf(8, 16, 512)] * 6
        + [buf(8, 16, 512)] * 2
        + [
            dma(SENDS), dma(8), dma(4), dma(4), dma(4), dma(), dma(4, 4), dma(4, 3), dma(), dma(8), dma(8), dma(8),
            dma(8), dma(8), dma(8), dma(8, 3), dma(8, 3), dma(8), dma(),
        ],
        compiler_params=pltpu.CompilerParams(has_side_effects=True, vmem_limit_bytes=56 * 2**20),
        name="mixer",
    )(
        tokens, norm_gain.reshape(1, -1), gate_proj, value_proj, extra, conv_value, conv_state, mix_gain.reshape(1, -1),
        out_proj, step_bias, decay_rate, skip_gain, doc_lengths,
    )


def solution(mesh):
    return jax.shard_map(
        local,
        mesh=mesh,
        in_specs=(
            P("seq", "fsdp"), P(), P("seq", "fsdp"), P("seq", "fsdp"), P("seq", "fsdp"), P("seq", None, None),
            P(None, "fsdp"), P(), P("fsdp"), P("fsdp"), P("fsdp"), P("fsdp"), P("fsdp", "seq"), P(),
        ),
        out_specs=P("seq", "fsdp"),
        check_vma=False,
    )
```

```python
import jax
import jax.numpy as jnp
from jax import lax
from jax.experimental import pallas as pl
from jax.experimental.pallas import tpu as pltpu
from jax.sharding import PartitionSpec as P

N = 128
EPSILON = 1e-05
PRECISE = lax.Precision.HIGHEST
MESH = pl.DeviceIdType.MESH
F32 = jnp.float32
BF16 = jnp.bfloat16
WIDE = 640
STEP0 = 32
SQ = 40
SENDS = 260


def dot(a, b, precision=None):
    return jnp.dot(a, b, preferred_element_type=F32, precision=precision)


def body(
    tok, gain, gate_w, value_w, maps_w, step_w, conv_v, conv_s, mix_gain, out_w,
    bias, rate, skip, docs,
    out,
    XI, X, WV, WG, SV, SG, PV, PG, S0L, S0S, R0L, R0S, S1L, S1S, R1L, R1S, S2L, S2S, R2L, R2S, S3L, S3S, R3L, R3S, RV, RG,
    HS, HR, EXT, BC, ST, SR, SO, SI, SQB, NZ, GZ, T, Q, A1, B1, C1, RA1, RB1, RC1,
    A2, B2, C2, RA2, RB2, RC2, FO, FR,
    sem_send, sem_i, sem_a, sem_y, sem_x, sem_s, sem_w, sem_l, sem_sh, sem_h, sem_bc, sem_st, sem_in, sem_sq, sem_nz,
    sem_g, sem_gs, sem_1, sem_2, sem_f,
):
    s = lax.axis_index("seq")
    f = lax.axis_index("fsdp")
    z, c = lax.div(s, 2), lax.rem(s, 2)
    x, y = lax.div(f, 4), lax.rem(f, 4)
    sg = 1 - 2 * c

    def m4(v):
        return lax.rem(v + 8, 4)

    def m8(v):
        return lax.rem(v + 16, 8)

    def dev(z_=z, c_=c, x_=x, y_=y):
        return (2 * z_ + c_, 4 * x_ + y_)

    sibling = dev(c_=1 - c)
    peers = [(dc, dy) for dc in range(2) for dy in range(4) if (dc, dy) != (0, 0)]
    started = []

    def send(src, dst, sem, to):
        copy = pltpu.make_async_remote_copy(
            src_ref=src, dst_ref=dst, send_sem=sem_send.at[len(started)], recv_sem=sem,
            device_id=to, device_id_type=MESH,
        )
        copy.start()
        started.append((copy, None))

    def arrived(dst, sem):
        pltpu.make_async_remote_copy(
            src_ref=dst, dst_ref=dst, send_sem=sem_send.at[0], recv_sem=sem,
            device_id=sibling, device_id_type=MESH,
        ).wait_recv()

    def send_or_keep(own, src, dst, sem, to):
        copy = pltpu.make_async_remote_copy(
            src_ref=src, dst_ref=dst, send_sem=sem_send.at[len(started)], recv_sem=sem,
            device_id=to, device_id_type=MESH,
        )
        away = jnp.logical_not(own)

        @pl.when(away)
        def _():
            copy.start()

        @pl.when(own)
        def _():
            pltpu.make_async_copy(src, dst, sem).start()

        started.append((copy, away))

    def wrap_up():
        for copy, away in started:
            if away is None:
                copy.wait_send()
            else:

                @pl.when(away)
                def _(copy=copy):
                    copy.wait_send()

        assert len(started) <= SENDS

    barrier = pltpu.get_barrier_semaphore()
    own_leg = (lax.rem(f, 2) == c) & (lax.div(x, 2) == c)

    def greet(to):
        pl.semaphore_signal(barrier, inc=1, device_id=to, device_id_type=MESH)

    for i in range(8):
        for to, at in (((2 * z + lax.rem(f, 2), 8 * c + i), 8 * c + i), ((2 * z + lax.div(x, 2), 2 * i + c), 2 * i + c)):

            @pl.when(jnp.logical_not(own_leg & (f == at)))
            def _(to=to):
                greet(to)

    for o in range(1, 8):
        greet(dev(z_=m8(z + o)))
    for dc, dy in peers:
        greet(dev(c_=lax.rem(c + dc, 2), y_=m4(y + dy)))
    greet(dev(x_=m4(x + 1)))
    greet(dev(x_=m4(x - 1)))

    gain_col = jnp.transpose(
        jnp.broadcast_to(gain[0:1, pl.ds(pl.multiple_of(512 * s, 512), 512)], (128, 512))
    )[:, 0:1]
    lane_w = lax.broadcasted_iota(jnp.int32, (512, 128), 1)
    turn = lax.rem(128 - 32 * y, 128)

    def rows_of(half, ref_v, ref_g):
        cols = pl.ds(pl.multiple_of(256 * half, 256), 256)
        ref_v[:, 0:256] = (value_w[:, cols].astype(F32) * gain_col).astype(BF16)
        maps = pltpu.roll(maps_w[:, pl.ds(pl.multiple_of(128 * half, 128), 128)].astype(F32), turn, 1)
        steps = pltpu.roll(step_w[...].astype(F32), lax.rem(8 - 4 * half, 8), 0)
        steps = jnp.concatenate([jnp.zeros((32, 512), F32), steps, jnp.zeros((88, 512), F32)], axis=0)
        extra = jnp.where(lane_w < 32, maps, 0.0) + jnp.transpose(steps)
        ref_v[:, 256:384] = (extra * gain_col).astype(BF16)
        ref_g[...] = (gate_w[:, cols].astype(F32) * gain_col).astype(BF16)

    pl.semaphore_wait(barrier, 32 - 2 * own_leg.astype(jnp.int32))

    for i in range(8):
        send_or_keep(
            own_leg & (f == 8 * c + i),
            tok.at[pl.ds(16 * i, 16)], XI.at[lax.div(f, 2)], sem_i.at[lax.div(f, 2)],
            (2 * z + lax.rem(f, 2), 8 * c + i),
        )
    rows_of(1 - c, SV, SG)
    send(SV, WV.at[c], sem_w.at[0], sibling)
    send(SG, WG.at[c], sem_w.at[1], sibling)
    rows_of(c, WV.at[c], WG.at[c])
    upper = lax.div(z, 4)
    lead, trail = x + upper * (y - x), y + upper * (x - y)
    for o in (4, 3, 5, 2, 6, 1, 7):
        to = m8(z + o)
        arrived(XI.at[to], sem_i.at[to])
        send(XI.at[to], X.at[c, upper, lead, trail, lax.rem(z, 4)], sem_a.at[z], dev(z_=to))
    arrived(XI.at[z], sem_i.at[z])
    pltpu.make_async_copy(XI.at[z], X.at[c, upper, lead, trail, lax.rem(z, 4)], sem_a.at[z]).start()

    lane8 = lax.broadcasted_iota(jnp.int32, (8, 128), 1)
    starts = jnp.full((8, 128), 1 << 20, jnp.int32)
    total = jnp.int32(0)
    for i in range(32):
        starts = jnp.where(lane8 == i, total, starts)
        total = total + docs[i]
    starts = starts.astype(F32)[0:1]
    first = (256 * z).astype(F32)
    t_wide = first + lax.broadcasted_iota(jnp.int32, (256, 128), 0).astype(F32)
    start_of = jnp.max(jnp.where(starts <= t_wide, starts, 0.0), axis=1, keepdims=True)
    t_col = t_wide[:, 0:1]
    into = t_col - start_of
    bias_row = jnp.zeros((8, 128), F32)
    rate_row = jnp.zeros((8, 128), F32)
    lane_256 = lax.broadcasted_iota(jnp.int32, (8, 256), 1)
    skip_row = jnp.zeros((8, 256), F32)
    for i in range(4):
        bias_row = jnp.where(lane8 == STEP0 + i, bias[4 * c + i], bias_row)
        rate_row = jnp.where(lane8 == STEP0 + i, rate[4 * c + i], rate_row)
        skip_row = jnp.where(lax.div(lane_256, 64) == i, skip[4 * c + i], skip_row)
    bias_row, rate_row, skip_row = bias_row[0:1], rate_row[0:1], skip_row[0:1]

    def at_x(q):
        return dev(x_=q)

    def at_y(q):
        return dev(y_=q)

    legs = [(x, at_x, y, at_y), (y, at_y, x, at_x)]
    for h, (a, _, b, to) in enumerate(legs):
        for zt in range(4):
            arrived(X.at[c, h, a, b, zt], sem_a.at[4 * h + zt])
        mine = X.at[c, h, a, b]
        send(mine, mine, sem_y.at[h, b], to(m4(b + 1)))
        send(mine, mine, sem_y.at[h, b], to(m4(b - 1)))
    for h, (a, _, b, to) in enumerate(legs):
        near = X.at[c, h, a, m4(b - sg)]
        arrived(near, sem_y.at[h, m4(b - sg)])
        send(near, near, sem_y.at[h, m4(b - sg)], to(m4(b + sg)))
    for h, (a, to, b, _) in enumerate(legs):
        for q in (m4(b + sg), m4(b + 2)):
            arrived(X.at[c, h, a, q], sem_y.at[h, q])
        mine = X.at[c, h, a]
        send(mine, mine, sem_s.at[h, a], sibling)
        send(mine, mine, sem_x.at[h, a], to(m4(a + 1)))
        send(mine, mine, sem_x.at[h, a], to(m4(a - 1)))
    arrived(WV.at[1 - c], sem_w.at[0])
    arrived(WG.at[1 - c], sem_w.at[1])

    lane_e = lax.broadcasted_iota(jnp.int32, (256, 128), 1)
    groups = [[a, m4(a - sg), m4(a + sg), m4(a + 2)] for a, _, _, _ in legs]

    def came(j):
        for h, (a, to, _, _) in enumerate(legs):
            q = groups[h][j]
            got = X.at[c, h, q]
            arrived(got, sem_x.at[h, q])
            if j == 1:
                send(got, got, sem_x.at[h, q], to(m4(a + sg)))
            send(got, got, sem_s.at[h, q], sibling)

    def product(g):
        for h in range(2):
            arrived(X.at[1 - c, h, groups[h][g]], sem_s.at[h, groups[h][g]])
            a = X[0, h, groups[h][g]].reshape(256, 512)
            b = X[1, h, groups[h][g]].reshape(256, 512)
            p = dot(a, WV[0]) + dot(b, WV[1])
            PG[g, h] = (dot(a, WG[0]) + dot(b, WG[1])).reshape(4, 4, 16, 256)
            a, b = a.astype(F32), b.astype(F32)
            squares = jnp.sum(a * a + b * b, axis=1, keepdims=True)
            PV[g, h, :, :, :, 0:256] = p[:, 0:256].reshape(4, 4, 16, 256)
            PV[g, h, :, :, :, 256:384] = (p[:, 256:384] + jnp.where(lane_e == SQ, squares, 0.0)).reshape(4, 4, 16, 128)

    rings = [
        (0, 1, "all", S0L, S0S, R0L, R0S),
        (1, 2, "values", S1L, S1S, R1L, R1S),
        (3, 1, "values", S2L, S2S, R2L, R2S),
        (1, 3, "gate", S3L, S3S, R3L, R3S),
    ]

    def pieces(r, d):
        g, n, kind = rings[r][:3]
        d_up, d_at = lax.div(d, 4), lax.rem(d, 4)
        got = []
        if kind != "gate":
            got.append((0, 384, PV[pl.ds(g, n), d_up, :, d_at]))
        if kind != "values":
            got.append((got[0][1] if got else 0, 256, PG[pl.ds(g, n), d_up, :, d_at]))
        return got

    def hop(r, k):
        out_l, out_s, in_l, in_s = rings[r][3:]
        if k:
            arrived(in_l.at[k - 1], sem_l.at[r, k - 1])
        for lo, wide, v in pieces(r, m8(z + (4 - k) * sg)):
            if k:
                v = v + in_l[k - 1, :, :, :, lo : lo + wide].astype(F32)
            out_l[k, :, :, :, lo : lo + wide] = v.astype(BF16)
        send(out_l.at[k], in_l.at[k], sem_l.at[r, k], dev(z_=m8(z + sg)))
        if k < 3:
            if k:
                arrived(in_s.at[k - 1], sem_sh.at[r, k - 1])
            for lo, wide, v in pieces(r, m8(z - (3 - k) * sg)):
                if k:
                    v = v + in_s[k - 1, :, :, :, lo : lo + wide].astype(F32)
                out_s[k, :, :, :, lo : lo + wide] = v.astype(BF16)
            send(out_s.at[k], in_s.at[k], sem_sh.at[r, k], dev(z_=m8(z - sg)))

    def last(r):
        g, n, kind, _, _, in_l, in_s = rings[r]
        arrived(in_l.at[3], sem_l.at[r, 3])
        arrived(in_s.at[2], sem_sh.at[r, 2])
        for lo, wide, v in pieces(r, z):
            v = v + in_l[3, :, :, :, lo : lo + wide].astype(F32) + in_s[2, :, :, :, lo : lo + wide].astype(F32)
            ref = RV if wide == 384 else RG
            for j in range(n):
                a = groups[0][g + j] + upper * (groups[1][g + j] - groups[0][g + j])
                for i in range(4):
                    ref[a + upper * (i - a), i + upper * (a - i)] = v[j, i]

    product(0)
    hop(0, 0)
    hop(0, 1)
    hop(0, 2)
    came(1)
    came(2)
    product(1)
    product(2)
    hop(1, 0)
    hop(0, 3)
    hop(1, 1)
    came(3)
    product(3)
    hop(2, 0)
    hop(1, 2)
    last(0)
    hop(2, 1)
    hop(1, 3)
    hop(3, 0)
    hop(2, 2)
    last(1)
    hop(2, 3)
    hop(3, 1)
    last(2)

    scale = lax.rsqrt(RV[:, :, :, 256:384].reshape(256, 128)[:, SQ : SQ + 1] * (1.0 / 8192) + EPSILON)
    raw = (RV[...].reshape(256, 384) * scale).astype(BF16)
    HS[...] = raw[240:256]
    send(HS, HR, sem_h, dev(z_=m8(z + 1)))
    EXT[16:272] = raw.astype(F32)

    raw_step = RV[:, :, :, 256:384].reshape(256, 128) * scale + bias_row
    step = jnp.maximum(raw_step, 0.0) + jnp.log1p(jnp.exp(-jnp.abs(raw_step)))
    log_decay = -rate_row * step
    order_r = lax.broadcasted_iota(jnp.int32, (256, 256), 0)
    order_c = lax.broadcasted_iota(jnp.int32, (256, 256), 1)
    cum = dot((order_r >= order_c).astype(F32), log_decay, PRECISE)
    cum_rows = jnp.transpose(cum)
    end = cum[255:256]
    causal = (order_r >= order_c) & (first + order_c.astype(F32) >= start_of)
    start_last = start_of[255:256]
    low = lax.broadcasted_iota(jnp.int32, (1, 128), 1) < 64

    def expand(a):
        return jnp.concatenate(
            [
                jnp.where(low, a[:, STEP0 + 2 * i : STEP0 + 2 * i + 1], a[:, STEP0 + 2 * i + 1 : STEP0 + 2 * i + 2])
                for i in range(2)
            ],
            axis=1,
        )

    step_wide = expand(step)
    tail = expand(jnp.where(t_col >= start_last, jnp.exp(end - cum), 0.0))
    carried = expand(jnp.where(start_of < first, jnp.exp(cum), 0.0))
    passing = expand(jnp.where(start_last < first, jnp.exp(end), 0.0))

    arrived(HR, sem_h)
    EXT[0:16] = HR[...].astype(F32)

    def conv(lo, width, taps):
        acc = jnp.zeros((256, width), F32)
        for k in range(4):
            acc = acc + jnp.where(into >= 3 - k, EXT[13 + k : 269 + k, lo : lo + width], 0.0) * taps[k]
        return acc * jax.nn.sigmoid(acc)

    maps_cols = pl.ds(pl.multiple_of(128 * c, 128), 128)
    group_row = lax.broadcasted_iota(jnp.int32, (4, 128), 0) == x
    taps_s = [
        pltpu.roll(
            jnp.broadcast_to(
                jnp.sum(jnp.where(group_row, conv_s[k, :, maps_cols], 0.0), axis=0, keepdims=True), (8, 128)
            ),
            turn,
            1,
        )[0:1]
        for k in range(4)
    ]
    maps = jnp.transpose(conv(256, 128, taps_s))[0:32].astype(BF16)
    BC[c, y] = maps
    for dc, dy in peers:
        to_c = lax.rem(c + dc, 2)
        send(BC.at[c, y], BC.at[c, y], sem_bc.at[4 * c + y], dev(c_=to_c, y_=m4(y + dy)))

    hop(3, 2)
    own_cols = pl.ds(pl.multiple_of(256 * c, 256), 256)
    inputs = conv(0, 256, [conv_v[k : k + 1, own_cols] for k in range(4)]).astype(BF16).astype(F32)
    stepped = inputs * step_wide
    to_end = (stepped * tail).astype(BF16)
    stepped = stepped.astype(BF16)

    for dc, dy in peers:
        pc, py = lax.rem(c + dc, 2), m4(y + dy)
        arrived(BC.at[pc, py], sem_bc.at[4 * pc + py])
    b_rows = BC[0].reshape(128, 256)
    c_cols = jnp.transpose(BC[1].reshape(128, 256).astype(F32)).astype(BF16)

    state = dot(b_rows, to_end).astype(BF16)
    ST[:, 0:16] = state.reshape(8, 16, 256)
    ST[:, 16:32] = jnp.broadcast_to(passing.astype(BF16)[None], (8, 16, 256))
    for o in range(1, 8):
        k = m8(z + o)
        send(ST.at[k], SR.at[z], sem_st.at[z], dev(z_=k))
    SR[z] = ST[z]

    hop(3, 3)
    scores = dot(c_cols, b_rows)
    parts = []
    for i in range(4):
        gaps = cum[:, STEP0 + i : STEP0 + i + 1] - cum_rows[STEP0 + i : STEP0 + i + 1, :]
        mixing = (jnp.exp(jnp.where(causal, gaps, -1e30)) * scores).astype(BF16)
        parts.append(dot(mixing, stepped[:, 128 * (i // 2) : 128 * (i // 2) + 128]))
    intra = jnp.concatenate([jnp.where(low, parts[0], parts[1]), jnp.where(low, parts[2], parts[3])], axis=1)
    partly = intra + skip_row * inputs

    for o in range(1, 8):
        k = m8(z + o)
        arrived(SR.at[k], sem_st.at[k])
    incoming = jnp.zeros((16, 256), F32)
    for i in range(8):
        SO[i] = incoming.astype(BF16)
        incoming = SR[i, 16:32].astype(F32) * incoming + SR[i, 0:16].astype(F32)
    for o in range(1, 8):
        k = m8(z + o)
        send(SO.at[k], SI.at[z], sem_in.at[z], dev(z_=k))
    SI[z] = SO[z]
    for o in range(1, 8):
        k = m8(z + o)
        arrived(SI.at[k], sem_in.at[k])
    outputs = partly + dot(c_cols, SI[...].reshape(128, 256)) * carried
    last(3)
    gate = RG[...].reshape(256, 256) * scale
    gated = outputs * (gate * jax.nn.sigmoid(gate))
    GZ[c, z] = (gated * mix_gain[0:1, own_cols]).astype(BF16)

    order = [z]
    for k in range(1, 4):
        order += [m8(z - k * sg), m8(z + k * sg)]
    order.append(m8(z + 4))
    block = GZ.at[c, z]
    send(block, block, sem_g.at[z], dev(z_=m8(z + sg)))
    send(block, block, sem_g.at[z], dev(z_=m8(z - sg)))
    send(block, block, sem_gs.at[z], sibling)

    own_sq = 2 * y + c
    SQB[own_sq] = lax.dot_general(
        jnp.ones((8, 256), F32), gated * gated, (((1,), (1,)), ((), ())), preferred_element_type=F32, precision=PRECISE
    )
    for dc, dy in peers:
        send(SQB.at[own_sq], SQB.at[own_sq], sem_sq.at[own_sq], dev(c_=lax.rem(c + dc, 2), y_=m4(y + dy)))
    for dc, dy in peers:
        k = 2 * m4(y + dy) + lax.rem(c + dc, 2)
        arrived(SQB.at[k], sem_sq.at[k])
    NZ[z] = lax.rsqrt(jnp.sum(SQB[...], axis=0) * (1.0 / 2048) + EPSILON)
    for o in range(1, 8):
        send(NZ.at[z], NZ.at[z], sem_nz.at[z], dev(z_=m8(z + o)))

    def pass_on(o):
        zt = order[o]
        got = GZ.at[c, zt]
        arrived(got, sem_g.at[zt])
        if o in (1, 3, 5):
            send(got, got, sem_g.at[zt], dev(z_=m8(z + sg)))
        if o in (2, 4):
            send(got, got, sem_g.at[zt], dev(z_=m8(z - sg)))
        send(got, got, sem_gs.at[zt], sibling)

    def take(o):
        zt = order[o]
        if o % 2 == 1:
            pass_on(o)
            if o < 7:
                pass_on(o + 1)
        arrived(GZ.at[1 - c, zt], sem_gs.at[zt])
        if o:
            arrived(NZ.at[zt], sem_nz.at[zt])
        norm = jnp.transpose(jnp.concatenate([NZ[zt]] * 16, axis=0))[:, 0:1]
        T[o] = ((dot(GZ[0, zt], out_w[0:256]) + dot(GZ[1, zt], out_w[256:512])) * norm).reshape(4, 4, 16, 512)

    def along(o, level):
        over_x = (o % 2 == 0) == (level == 1)
        p = x if over_x else y

        def to(q):
            return dev(x_=q) if over_x else dev(y_=q)

        return p, to

    def quarter(o, q):
        return T[o, q] if o % 2 == 0 else T[o, :, q]

    def first_out(o):
        p, to = along(o, 1)
        A1[o] = quarter(o, m4(p + 2)).astype(BF16)
        send(A1.at[o], RA1.at[o], sem_1.at[o, 0], to(m4(p + sg)))
        B1[o] = quarter(o, m4(p - sg)).astype(BF16)
        send(B1.at[o], RB1.at[o], sem_1.at[o, 1], to(m4(p - sg)))

    def first_relay(o):
        p, to = along(o, 1)
        arrived(RA1.at[o], sem_1.at[o, 0])
        C1[o] = (quarter(o, m4(p + sg)) + RA1[o].astype(F32)).astype(BF16)
        send(C1.at[o], RC1.at[o], sem_1.at[o, 2], to(m4(p + sg)))

    def second_out(o):
        p, _ = along(o, 1)
        arrived(RB1.at[o], sem_1.at[o, 1])
        arrived(RC1.at[o], sem_1.at[o, 2])
        Q[o] = quarter(o, p) + RB1[o].astype(F32) + RC1[o].astype(F32)
        p, to = along(o, 2)
        A2[o] = Q[o, m4(p + 2)].astype(BF16)
        send(A2.at[o], RA2.at[o], sem_2.at[o, 0], to(m4(p + sg)))
        B2[o] = Q[o, m4(p - sg)].astype(BF16)
        send(B2.at[o], RB2.at[o], sem_2.at[o, 1], to(m4(p - sg)))

    def second_relay(o):
        p, to = along(o, 2)
        arrived(RA2.at[o], sem_2.at[o, 0])
        C2[o] = (Q[o, m4(p + sg)] + RA2[o].astype(F32)).astype(BF16)
        send(C2.at[o], RC2.at[o], sem_2.at[o, 2], to(m4(p + sg)))

    block_at = f
    row_block = lax.rem(block_at, 8)
    to_core = lax.div(block_at, 8)

    def finish(o):
        p, _ = along(o, 2)
        arrived(RB2.at[o], sem_2.at[o, 1])
        arrived(RC2.at[o], sem_2.at[o, 2])
        FO[o] = (Q[o, p] + RB2[o].astype(F32) + RC2[o].astype(F32)).astype(BF16)
        to = (2 * order[o] + to_core, s)
        own = (to[0] == s) & (s == f) if o == 0 else None
        if own is None:
            send(FO.at[o], FR.at[row_block], sem_f.at[row_block], to)
        else:
            send_or_keep(own, FO.at[o], FR.at[row_block], sem_f.at[row_block], to)

    for tick in range(8 + 4):
        if tick < 8:
            take(tick)
            first_out(tick)
        if 0 <= tick - 1 < 8:
            first_relay(tick - 1)
        if 0 <= tick - 2 < 8:
            second_out(tick - 2)
        if 0 <= tick - 3 < 8:
            second_relay(tick - 3)
        if 0 <= tick - 4 < 8:
            finish(tick - 4)

    for i in range(8):
        arrived(FR.at[i], sem_f.at[i])
    out[...] = (tok[...].astype(F32) + FR[...].reshape(128, 512).astype(F32)).astype(BF16)

    wrap_up()


def local(
    tokens, norm_gain, gate_proj, value_proj, step_proj, state_proj, conv_value, conv_state, step_bias, decay_rate,
    skip_gain, mix_gain, out_proj, doc_lengths,
):
    maps = lax.dynamic_index_in_dim(state_proj, lax.axis_index("fsdp") // 4, 1, keepdims=False)
    vmem = pl.BlockSpec(memory_space=pltpu.VMEM)
    smem = pl.BlockSpec(memory_space=pltpu.SMEM)

    def buf(*shape, dtype=BF16):
        return pltpu.VMEM(shape, dtype)

    def dma(*shape):
        return pltpu.SemaphoreType.DMA(shape)

    return pl.pallas_call(
        body,
        out_shape=jax.ShapeDtypeStruct((128, 512), BF16),
        in_specs=[vmem] * 10 + [smem] * 4,
        out_specs=vmem,
        scratch_shapes=[
            buf(8, 16, 512),
            buf(2, 2, 4, 4, 4, 16, 512),
            buf(2, 512, 384),
            buf(2, 512, 256),
            buf(512, 384),
            buf(512, 256),
            buf(4, 2, 4, 4, 16, 384, dtype=F32),
            buf(4, 2, 4, 4, 16, 256, dtype=F32),
        ]
        + [buf(k, n, 4, 16, w) for n, w in ((1, 640), (2, 384), (1, 384), (3, 256)) for k in (4, 3, 4, 3)]
        + [
            buf(4, 4, 16, 384, dtype=F32),
            buf(4, 4, 16, 256, dtype=F32),
            buf(16, 384),
            buf(16, 384),
            buf(272, 384, dtype=F32),
            buf(2, 4, 32, 256),
            buf(8, 32, 256),
            buf(8, 32, 256),
            buf(8, 16, 256),
            buf(8, 16, 256),
            buf(8, 8, 256, dtype=F32),
            buf(8, 8, 256, dtype=F32),
            buf(2, 8, 256, 256),
            buf(8, 4, 4, 16, 512, dtype=F32),
            buf(8, 4, 16, 512, dtype=F32),
        ]
        + [buf(8, 4, 16, 512)] * 6
        + [buf(8, 16, 512)] * 6
        + [buf(8, 16, 512)] * 2
        + [
            dma(SENDS), dma(8), dma(8), dma(2, 4), dma(2, 4), dma(2, 4), dma(2), dma(4, 4), dma(4, 3), dma(), dma(8),
            dma(8), dma(8), dma(8), dma(8), dma(8), dma(8), dma(8, 3), dma(8, 3), dma(8),
        ],
        compiler_params=pltpu.CompilerParams(collective_id=0, has_side_effects=True, vmem_limit_bytes=56 * 2**20),
        name="mixer",
    )(
        tokens, norm_gain.reshape(1, -1), gate_proj, value_proj, maps, step_proj.T, conv_value, conv_state, mix_gain.reshape(1, -1),
        out_proj, step_bias, decay_rate, skip_gain, doc_lengths,
    )


def solution(mesh):
    return jax.shard_map(
        local,
        mesh=mesh,
        in_specs=(
            P("seq", "fsdp"), P(), P("seq", "fsdp"), P("seq", "fsdp"), P("seq", "fsdp"), P("seq", None, None),
            P(None, "fsdp"), P(), P("fsdp"), P("fsdp"), P("fsdp"), P("fsdp"), P("fsdp", "seq"), P(),
        ),
        out_specs=P("seq", "fsdp"),
        check_vma=False,
    )
```

```python
import jax
import jax.numpy as jnp
from jax import lax
from jax.experimental import pallas as pl
from jax.experimental.pallas import tpu as pltpu
from jax.sharding import PartitionSpec as P

N = 128
EPSILON = 1e-05
PRECISE = lax.Precision.HIGHEST
MESH = pl.DeviceIdType.MESH
F32 = jnp.float32
BF16 = jnp.bfloat16
WIDE = 640
STEP0 = 32
SQ = 40
SENDS = 320


def dot(a, b, precision=None):
    return jnp.dot(a, b, preferred_element_type=F32, precision=precision)


def body(
    tok_h, gain_h, gate_h, value_h, maps_h, step_h, conv_v_h, conv_s_h, mix_gain_h, out_w_h,
    bias, rate, skip, docs,
    out,
    tok, gain, gate_w, value_w, maps_w, step_w, conv_v, conv_s, mix_gain, out_w,
    XI, X, WV, WG, SV, SG, PV, PG, S0L, S0S, R0L, R0S, S1L, S1S, R1L, R1S, S2L, S2S, R2L, R2S, S3L, S3S, R3L, R3S, RV, RG,
    HS, HR, EXT, BC, ST, SR, SO, SI, SQB, NZ, GZ, T, Q, A1, B1, C1, RA1, RB1, RC1,
    A2, B2, C2, RA2, RB2, RC2, FO, FR,
    sem_load, sem_send, sem_i, sem_a, sem_y, sem_x, sem_s, sem_w, sem_l, sem_sh, sem_h, sem_bc, sem_st, sem_in, sem_sq,
    sem_nz, sem_g, sem_gs, sem_1, sem_2, sem_f,
):
    s = lax.axis_index("seq")
    f = lax.axis_index("fsdp")
    z, c = lax.div(s, 2), lax.rem(s, 2)
    x, y = lax.div(f, 4), lax.rem(f, 4)
    sg = 1 - 2 * c

    def m4(v):
        return lax.rem(v + 8, 4)

    def m8(v):
        return lax.rem(v + 16, 8)

    def dev(z_=z, c_=c, x_=x, y_=y):
        return (2 * z_ + c_, 4 * x_ + y_)

    sibling = dev(c_=1 - c)
    peers = [(dc, dy) for dc in range(2) for dy in range(4) if (dc, dy) != (0, 0)]
    started = []

    def send(src, dst, sem, to):
        copy = pltpu.make_async_remote_copy(
            src_ref=src, dst_ref=dst, send_sem=sem_send.at[len(started)], recv_sem=sem,
            device_id=to, device_id_type=MESH,
        )
        copy.start()
        started.append((copy, None))

    def arrived(dst, sem):
        pltpu.make_async_remote_copy(
            src_ref=dst, dst_ref=dst, send_sem=sem_send.at[0], recv_sem=sem,
            device_id=sibling, device_id_type=MESH,
        ).wait_recv()

    def send_or_keep(own, src, dst, sem, to):
        copy = pltpu.make_async_remote_copy(
            src_ref=src, dst_ref=dst, send_sem=sem_send.at[len(started)], recv_sem=sem,
            device_id=to, device_id_type=MESH,
        )
        away = jnp.logical_not(own)

        @pl.when(away)
        def _():
            copy.start()

        @pl.when(own)
        def _():
            pltpu.make_async_copy(src, dst, sem).start()

        started.append((copy, away))

    def wrap_up():
        for copy, away in started:
            if away is None:
                copy.wait_send()
            else:

                @pl.when(away)
                def _(copy=copy):
                    copy.wait_send()

        assert len(started) <= SENDS

    barrier = pltpu.get_barrier_semaphore()
    own_leg = (lax.rem(f, 2) == c) & (lax.div(x, 2) == c)

    def greet(to):
        pl.semaphore_signal(barrier, inc=1, device_id=to, device_id_type=MESH)

    for i in range(8):
        for to, at in (((2 * z + lax.rem(f, 2), 8 * c + i), 8 * c + i), ((2 * z + lax.div(x, 2), 2 * i + c), 2 * i + c)):

            @pl.when(jnp.logical_not(own_leg & (f == at)))
            def _(to=to):
                greet(to)

    for o in range(1, 8):
        greet(dev(z_=m8(z + o)))
    for dc, dy in peers:
        greet(dev(c_=lax.rem(c + dc, 2), y_=m4(y + dy)))
    greet(dev(x_=m4(x + 1)))
    greet(dev(x_=m4(x - 1)))

    loads = [
        pltpu.make_async_copy(src, dst, sem_load.at[i])
        for i, (src, dst) in enumerate(
            (
                (tok_h, tok), (gain_h, gain), (value_h, value_w), (maps_h, maps_w), (step_h, step_w), (gate_h, gate_w),
                (conv_v_h, conv_v), (conv_s_h, conv_s), (mix_gain_h, mix_gain), (out_w_h, out_w),
            )
        )
    ]
    for load in loads:
        load.start()
    loads[1].wait()

    gain_col = jnp.transpose(
        jnp.broadcast_to(gain[0:1, pl.ds(pl.multiple_of(512 * s, 512), 512)], (128, 512))
    )[:, 0:1]
    lane_w = lax.broadcasted_iota(jnp.int32, (512, 128), 1)
    turn = lax.rem(128 - 32 * y, 128)

    def rows_of(half, ref_v, ref_g):
        cols = pl.ds(pl.multiple_of(256 * half, 256), 256)
        ref_v[:, 0:256] = (value_w[:, cols].astype(F32) * gain_col).astype(BF16)
        maps = pltpu.roll(maps_w[:, pl.ds(pl.multiple_of(128 * half, 128), 128)].astype(F32), turn, 1)
        steps = pltpu.roll(step_w[...].astype(F32), lax.rem(8 - 4 * half, 8), 0)
        steps = jnp.concatenate([jnp.zeros((32, 512), F32), steps, jnp.zeros((88, 512), F32)], axis=0)
        extra = jnp.where(lane_w < 32, maps, 0.0) + jnp.transpose(steps)
        ref_v[:, 256:384] = (extra * gain_col).astype(BF16)
        ref_g[...] = (gate_w[:, cols].astype(F32) * gain_col).astype(BF16)

    for load in (loads[0], *loads[2:]):
        load.wait()
    pl.semaphore_wait(barrier, 32 - 2 * own_leg.astype(jnp.int32))

    for i in range(8):
        send_or_keep(
            own_leg & (f == 8 * c + i),
            tok.at[pl.ds(16 * i, 16)], XI.at[lax.div(f, 2)], sem_i.at[lax.div(f, 2)],
            (2 * z + lax.rem(f, 2), 8 * c + i),
        )
    rows_of(1 - c, SV, SG)
    send(SV, WV.at[c], sem_w.at[0], sibling)
    send(SG, WG.at[c], sem_w.at[1], sibling)
    rows_of(c, WV.at[c], WG.at[c])
    upper = lax.div(z, 4)
    lead, trail = x + upper * (y - x), y + upper * (x - y)
    for o in (4, 3, 5, 2, 6, 1, 7):
        to = m8(z + o)
        arrived(XI.at[to], sem_i.at[to])
        send(XI.at[to], X.at[c, upper, lead, trail, lax.rem(z, 4)], sem_a.at[z], dev(z_=to))
    arrived(XI.at[z], sem_i.at[z])
    pltpu.make_async_copy(XI.at[z], X.at[c, upper, lead, trail, lax.rem(z, 4)], sem_a.at[z]).start()

    lane8 = lax.broadcasted_iota(jnp.int32, (8, 128), 1)
    starts = jnp.full((8, 128), 1 << 20, jnp.int32)
    total = jnp.int32(0)
    for i in range(32):
        starts = jnp.where(lane8 == i, total, starts)
        total = total + docs[i]
    starts = starts.astype(F32)[0:1]
    first = (256 * z).astype(F32)
    t_wide = first + lax.broadcasted_iota(jnp.int32, (256, 128), 0).astype(F32)
    start_of = jnp.max(jnp.where(starts <= t_wide, starts, 0.0), axis=1, keepdims=True)
    t_col = t_wide[:, 0:1]
    into = t_col - start_of
    bias_row = jnp.zeros((8, 128), F32)
    rate_row = jnp.zeros((8, 128), F32)
    lane_256 = lax.broadcasted_iota(jnp.int32, (8, 256), 1)
    skip_row = jnp.zeros((8, 256), F32)
    for i in range(4):
        bias_row = jnp.where(lane8 == STEP0 + i, bias[4 * c + i], bias_row)
        rate_row = jnp.where(lane8 == STEP0 + i, rate[4 * c + i], rate_row)
        skip_row = jnp.where(lax.div(lane_256, 64) == i, skip[4 * c + i], skip_row)
    bias_row, rate_row, skip_row = bias_row[0:1], rate_row[0:1], skip_row[0:1]

    def at_x(q):
        return dev(x_=q)

    def at_y(q):
        return dev(y_=q)

    legs = [(x, at_x, y, at_y), (y, at_y, x, at_x)]
    def spread(h, q):
        a, to, _, _ = legs[h]
        mine = X.at[c, h, a, q]
        send(mine, mine, sem_x.at[h, a, q], to(m4(a + 1)))
        send(mine, mine, sem_x.at[h, a, q], to(m4(a - 1)))

    def relay(h, q):
        a, to, _, _ = legs[h]
        near = m4(a - sg)
        got = X.at[c, h, near, q]
        arrived(got, sem_x.at[h, near, q])
        send(got, got, sem_x.at[h, near, q], to(m4(a + sg)))

    def trailing(h, q):
        arrived(X.at[c, h, legs[h][0], q], sem_y.at[h, q])

    for h, (a, _, b, to) in enumerate(legs):
        for zt in range(4):
            arrived(X.at[c, h, a, b, zt], sem_a.at[4 * h + zt])
        mine = X.at[c, h, a, b]
        send(mine, mine, sem_y.at[h, b], to(m4(b + 1)))
        send(mine, mine, sem_y.at[h, b], to(m4(b - 1)))
        spread(h, b)
    for h, (a, _, b, to) in enumerate(legs):
        near = X.at[c, h, a, m4(b - sg)]
        trailing(h, m4(b - sg))
        send(near, near, sem_y.at[h, m4(b - sg)], to(m4(b + sg)))
        spread(h, m4(b - sg))
        trailing(h, m4(b + sg))
        spread(h, m4(b + sg))
    for h, (_, _, b, _) in enumerate(legs):
        relay(h, b)
    for h, (a, _, b, _) in enumerate(legs):
        trailing(h, m4(b + 2))
        spread(h, m4(b + 2))
        send(X.at[c, h, a], X.at[c, h, a], sem_s.at[h, a], sibling)
    arrived(WV.at[1 - c], sem_w.at[0])
    arrived(WG.at[1 - c], sem_w.at[1])

    lane_e = lax.broadcasted_iota(jnp.int32, (256, 128), 1)
    groups = [[a, m4(a - sg), m4(a + sg), m4(a + 2)] for a, _, _, _ in legs]

    def came(j):
        for h, (_, _, b, _) in enumerate(legs):
            q = groups[h][j]
            for at in range(4):
                if j > 1:
                    arrived(X.at[c, h, q, at], sem_x.at[h, q, at])
            send(X.at[c, h, q], X.at[c, h, q], sem_s.at[h, q], sibling)

    def product(g):
        for h in range(2):
            arrived(X.at[1 - c, h, groups[h][g]], sem_s.at[h, groups[h][g]])
            a = X[0, h, groups[h][g]].reshape(256, 512)
            b = X[1, h, groups[h][g]].reshape(256, 512)
            p = dot(a, WV[0]) + dot(b, WV[1])
            PG[g, h] = (dot(a, WG[0]) + dot(b, WG[1])).reshape(4, 4, 16, 256)
            a, b = a.astype(F32), b.astype(F32)
            squares = jnp.sum(a * a + b * b, axis=1, keepdims=True)
            PV[g, h, :, :, :, 0:256] = p[:, 0:256].reshape(4, 4, 16, 256)
            PV[g, h, :, :, :, 256:384] = (p[:, 256:384] + jnp.where(lane_e == SQ, squares, 0.0)).reshape(4, 4, 16, 128)

    rings = [
        (0, 1, "all", S0L, S0S, R0L, R0S),
        (1, 2, "values", S1L, S1S, R1L, R1S),
        (3, 1, "values", S2L, S2S, R2L, R2S),
        (1, 3, "gate", S3L, S3S, R3L, R3S),
    ]

    def pieces(r, d):
        g, n, kind = rings[r][:3]
        d_up, d_at = lax.div(d, 4), lax.rem(d, 4)
        got = []
        if kind != "gate":
            got.append((0, 384, PV[pl.ds(g, n), d_up, :, d_at]))
        if kind != "values":
            got.append((got[0][1] if got else 0, 256, PG[pl.ds(g, n), d_up, :, d_at]))
        return got

    def hop(r, k):
        out_l, out_s, in_l, in_s = rings[r][3:]
        if k:
            arrived(in_l.at[k - 1], sem_l.at[r, k - 1])
        for lo, wide, v in pieces(r, m8(z + (4 - k) * sg)):
            if k:
                v = v + in_l[k - 1, :, :, :, lo : lo + wide].astype(F32)
            out_l[k, :, :, :, lo : lo + wide] = v.astype(BF16)
        send(out_l.at[k], in_l.at[k], sem_l.at[r, k], dev(z_=m8(z + sg)))
        if k < 3:
            if k:
                arrived(in_s.at[k - 1], sem_sh.at[r, k - 1])
            for lo, wide, v in pieces(r, m8(z - (3 - k) * sg)):
                if k:
                    v = v + in_s[k - 1, :, :, :, lo : lo + wide].astype(F32)
                out_s[k, :, :, :, lo : lo + wide] = v.astype(BF16)
            send(out_s.at[k], in_s.at[k], sem_sh.at[r, k], dev(z_=m8(z - sg)))

    def last(r):
        g, n, kind, _, _, in_l, in_s = rings[r]
        arrived(in_l.at[3], sem_l.at[r, 3])
        arrived(in_s.at[2], sem_sh.at[r, 2])
        for lo, wide, v in pieces(r, z):
            v = v + in_l[3, :, :, :, lo : lo + wide].astype(F32) + in_s[2, :, :, :, lo : lo + wide].astype(F32)
            ref = RV if wide == 384 else RG
            for j in range(n):
                a = groups[0][g + j] + upper * (groups[1][g + j] - groups[0][g + j])
                for i in range(4):
                    ref[a + upper * (i - a), i + upper * (a - i)] = v[j, i]

    product(0)
    hop(0, 0)
    for at in (-1, 1):
        for h in range(2):
            relay(h, m4(legs[h][2] + at * sg))
    hop(0, 1)
    for h in range(2):
        relay(h, m4(legs[h][2] + 2))
    came(1)
    came(2)
    product(1)
    product(2)
    hop(1, 0)
    hop(0, 2)
    came(3)
    product(3)
    hop(2, 0)
    hop(1, 1)
    hop(0, 3)
    hop(2, 1)
    hop(1, 2)
    last(0)
    hop(2, 2)
    hop(1, 3)
    hop(2, 3)
    hop(3, 0)
    last(1)
    last(2)

    scale = lax.rsqrt(RV[:, :, :, 256:384].reshape(256, 128)[:, SQ : SQ + 1] * (1.0 / 8192) + EPSILON)
    raw = (RV[...].reshape(256, 384) * scale).astype(BF16)
    HS[...] = raw[240:256]
    send(HS, HR, sem_h, dev(z_=m8(z + 1)))
    EXT[16:272] = raw.astype(F32)

    raw_step = RV[:, :, :, 256:384].reshape(256, 128) * scale + bias_row
    step = jnp.maximum(raw_step, 0.0) + jnp.log1p(jnp.exp(-jnp.abs(raw_step)))
    log_decay = -rate_row * step
    order_r = lax.broadcasted_iota(jnp.int32, (256, 256), 0)
    order_c = lax.broadcasted_iota(jnp.int32, (256, 256), 1)
    cum = dot((order_r >= order_c).astype(F32), log_decay, PRECISE)
    cum_rows = jnp.transpose(cum)
    end = cum[255:256]
    causal = (order_r >= order_c) & (first + order_c.astype(F32) >= start_of)
    start_last = start_of[255:256]
    low = lax.broadcasted_iota(jnp.int32, (1, 128), 1) < 64

    def expand(a):
        return jnp.concatenate(
            [
                jnp.where(low, a[:, STEP0 + 2 * i : STEP0 + 2 * i + 1], a[:, STEP0 + 2 * i + 1 : STEP0 + 2 * i + 2])
                for i in range(2)
            ],
            axis=1,
        )

    step_wide = expand(step)
    tail = expand(jnp.where(t_col >= start_last, jnp.exp(end - cum), 0.0))
    carried = expand(jnp.where(start_of < first, jnp.exp(cum), 0.0))
    passing = expand(jnp.where(start_last < first, jnp.exp(end), 0.0))

    arrived(HR, sem_h)
    EXT[0:16] = HR[...].astype(F32)
    hop(3, 1)

    def conv(lo, width, taps):
        acc = jnp.zeros((256, width), F32)
        for k in range(4):
            acc = acc + jnp.where(into >= 3 - k, EXT[13 + k : 269 + k, lo : lo + width], 0.0) * taps[k]
        return acc * jax.nn.sigmoid(acc)

    maps_cols = pl.ds(pl.multiple_of(128 * c, 128), 128)
    group_row = lax.broadcasted_iota(jnp.int32, (4, 128), 0) == x
    taps_s = [
        pltpu.roll(
            jnp.broadcast_to(
                jnp.sum(jnp.where(group_row, conv_s[k, :, maps_cols], 0.0), axis=0, keepdims=True), (8, 128)
            ),
            turn,
            1,
        )[0:1]
        for k in range(4)
    ]
    maps = jnp.transpose(conv(256, 128, taps_s))[0:32].astype(BF16)
    BC[c, y] = maps
    for dc, dy in peers:
        to_c = lax.rem(c + dc, 2)
        send(BC.at[c, y], BC.at[c, y], sem_bc.at[4 * c + y], dev(c_=to_c, y_=m4(y + dy)))

    own_cols = pl.ds(pl.multiple_of(256 * c, 256), 256)
    inputs = conv(0, 256, [conv_v[k : k + 1, own_cols] for k in range(4)]).astype(BF16).astype(F32)
    stepped = inputs * step_wide
    to_end = (stepped * tail).astype(BF16)
    stepped = stepped.astype(BF16)

    for dc, dy in peers:
        pc, py = lax.rem(c + dc, 2), m4(y + dy)
        arrived(BC.at[pc, py], sem_bc.at[4 * pc + py])
    hop(3, 2)
    b_rows = BC[0].reshape(128, 256)
    c_cols = jnp.transpose(BC[1].reshape(128, 256).astype(F32)).astype(BF16)

    state = dot(b_rows, to_end).astype(BF16)
    ST[:, 0:16] = state.reshape(8, 16, 256)
    ST[:, 16:32] = jnp.broadcast_to(passing.astype(BF16)[None], (8, 16, 256))
    for o in range(1, 8):
        k = m8(z + o)
        send(ST.at[k], SR.at[z], sem_st.at[z], dev(z_=k))
    SR[z] = ST[z]

    scores = dot(c_cols, b_rows)
    parts = []
    for i in range(4):
        gaps = cum[:, STEP0 + i : STEP0 + i + 1] - cum_rows[STEP0 + i : STEP0 + i + 1, :]
        mixing = (jnp.exp(jnp.where(causal, gaps, -1e30)) * scores).astype(BF16)
        parts.append(dot(mixing, stepped[:, 128 * (i // 2) : 128 * (i // 2) + 128]))
    intra = jnp.concatenate([jnp.where(low, parts[0], parts[1]), jnp.where(low, parts[2], parts[3])], axis=1)
    partly = intra + skip_row * inputs

    for o in range(1, 8):
        k = m8(z + o)
        arrived(SR.at[k], sem_st.at[k])
    incoming = jnp.zeros((16, 256), F32)
    for i in range(8):
        SO[i] = incoming.astype(BF16)
        incoming = SR[i, 16:32].astype(F32) * incoming + SR[i, 0:16].astype(F32)
    for o in range(1, 8):
        k = m8(z + o)
        send(SO.at[k], SI.at[z], sem_in.at[z], dev(z_=k))
    SI[z] = SO[z]
    hop(3, 3)
    for o in range(1, 8):
        k = m8(z + o)
        arrived(SI.at[k], sem_in.at[k])
    outputs = partly + dot(c_cols, SI[...].reshape(128, 256)) * carried
    last(3)
    gate = RG[...].reshape(256, 256) * scale
    gated = outputs * (gate * jax.nn.sigmoid(gate))
    GZ[c, z] = (gated * mix_gain[0:1, own_cols]).astype(BF16).reshape(2, 128, 256)

    order = [z]
    for k in range(1, 4):
        order += [m8(z - k * sg), m8(z + k * sg)]
    order.append(m8(z + 4))
    for i in range(2):
        block = GZ.at[c, z, i]
        send(block, block, sem_g.at[z, i], dev(z_=m8(z + sg)))
        send(block, block, sem_g.at[z, i], dev(z_=m8(z - sg)))
        send(block, block, sem_gs.at[z, i], sibling)

    own_sq = 2 * y + c
    SQB[own_sq] = lax.dot_general(
        jnp.ones((8, 256), F32), gated * gated, (((1,), (1,)), ((), ())), preferred_element_type=F32, precision=PRECISE
    )
    for dc, dy in peers:
        send(SQB.at[own_sq], SQB.at[own_sq], sem_sq.at[own_sq], dev(c_=lax.rem(c + dc, 2), y_=m4(y + dy)))
    for dc, dy in peers:
        k = 2 * m4(y + dy) + lax.rem(c + dc, 2)
        arrived(SQB.at[k], sem_sq.at[k])
    NZ[z] = lax.rsqrt(jnp.sum(SQB[...], axis=0) * (1.0 / 2048) + EPSILON)
    for o in range(1, 8):
        send(NZ.at[z], NZ.at[z], sem_nz.at[z], dev(z_=m8(z + o)))

    def pass_on(o, i):
        zt = order[o]
        got = GZ.at[c, zt, i]
        arrived(got, sem_g.at[zt, i])
        if o in (1, 3, 5):
            send(got, got, sem_g.at[zt, i], dev(z_=m8(z + sg)))
        if o in (2, 4):
            send(got, got, sem_g.at[zt, i], dev(z_=m8(z - sg)))
        send(got, got, sem_gs.at[zt, i], sibling)

    def take(o):
        zt = order[o]
        if o % 2 == 1:
            for i in range(2):
                pass_on(o, i)
                if o < 7:
                    pass_on(o + 1, i)
        for i in range(2):
            arrived(GZ.at[1 - c, zt, i], sem_gs.at[zt, i])
        if o:
            arrived(NZ.at[zt], sem_nz.at[zt])
        norm = jnp.transpose(jnp.concatenate([NZ[zt]] * 16, axis=0))[:, 0:1]
        T[o] = ((dot(GZ[0, zt].reshape(256, 256), out_w[0:256]) + dot(GZ[1, zt].reshape(256, 256), out_w[256:512])) * norm).reshape(4, 4, 16, 512)

    def along(o, level):
        over_x = (o % 2 == 0) == (level == 1)
        p = x if over_x else y

        def to(q):
            return dev(x_=q) if over_x else dev(y_=q)

        return p, to

    def quarter(o, q):
        return T[o, q] if o % 2 == 0 else T[o, :, q]

    straight = (6, 7)

    def first_out(o):
        p, to = along(o, 1)
        A1[o] = quarter(o, m4(p + 2)).astype(BF16)
        send(A1.at[o], RA1.at[o], sem_1.at[o, 0], to(m4(p + 2) if o in straight else m4(p + sg)))
        B1[o] = quarter(o, m4(p - sg)).astype(BF16)
        send(B1.at[o], RB1.at[o], sem_1.at[o, 1], to(m4(p - sg)))
        if o in straight:
            C1[o] = quarter(o, m4(p + sg)).astype(BF16)
            send(C1.at[o], RC1.at[o], sem_1.at[o, 2], to(m4(p + sg)))

    def first_relay(o):
        p, to = along(o, 1)
        arrived(RA1.at[o], sem_1.at[o, 0])
        C1[o] = (quarter(o, m4(p + sg)) + RA1[o].astype(F32)).astype(BF16)
        send(C1.at[o], RC1.at[o], sem_1.at[o, 2], to(m4(p + sg)))

    def second_out(o):
        p, _ = along(o, 1)
        arrived(RB1.at[o], sem_1.at[o, 1])
        arrived(RC1.at[o], sem_1.at[o, 2])
        summed = quarter(o, p) + RB1[o].astype(F32) + RC1[o].astype(F32)
        if o in straight:
            arrived(RA1.at[o], sem_1.at[o, 0])
            summed = summed + RA1[o].astype(F32)
        Q[o] = summed
        p, to = along(o, 2)
        for i, (out_b, in_b, q) in enumerate(((A2, RA2, m4(p + 2)), (B2, RB2, m4(p - sg)), (C2, RC2, m4(p + sg)))):
            out_b[o] = Q[o, q].astype(BF16)
            send(out_b.at[o], in_b.at[o], sem_2.at[o, i], to(q))

    block_at = f
    row_block = lax.rem(block_at, 8)
    to_core = lax.div(block_at, 8)

    def finish(o):
        p, _ = along(o, 2)
        for i, in_b in enumerate((RA2, RB2, RC2)):
            arrived(in_b.at[o], sem_2.at[o, i])
        FO[o] = (Q[o, p] + RA2[o].astype(F32) + RB2[o].astype(F32) + RC2[o].astype(F32)).astype(BF16)
        to = (2 * order[o] + to_core, s)
        own = (to[0] == s) & (s == f) if o == 0 else None
        if own is None:
            send(FO.at[o], FR.at[row_block], sem_f.at[row_block], to)
        else:
            send_or_keep(own, FO.at[o], FR.at[row_block], sem_f.at[row_block], to)

    for tick in range(8 + 2):
        if tick < 8:
            take(tick)
            first_out(tick)
        if 0 <= tick - 1 < 8 and tick - 1 not in straight:
            first_relay(tick - 1)
        if 2 <= tick < 9:
            second_out(tick - 2)
        if tick == 8:
            second_out(7)
        if 0 <= tick - 3 < 8:
            finish(tick - 3)
    finish(7)

    for i in range(8):
        arrived(FR.at[i], sem_f.at[i])
    out[...] = (tok[...].astype(F32) + FR[...].reshape(128, 512).astype(F32)).astype(BF16)

    wrap_up()


def local(
    tokens, norm_gain, gate_proj, value_proj, step_proj, state_proj, conv_value, conv_state, step_bias, decay_rate,
    skip_gain, mix_gain, out_proj, doc_lengths,
):
    maps = lax.dynamic_index_in_dim(state_proj, lax.axis_index("fsdp") // 4, 1, keepdims=False)
    vmem = pl.BlockSpec(memory_space=pltpu.VMEM)
    smem = pl.BlockSpec(memory_space=pltpu.SMEM)

    def buf(*shape, dtype=BF16):
        return pltpu.VMEM(shape, dtype)

    def dma(*shape):
        return pltpu.SemaphoreType.DMA(shape)

    return pl.pallas_call(
        body,
        out_shape=jax.ShapeDtypeStruct((128, 512), BF16),
        in_specs=[pl.BlockSpec(memory_space=pl.ANY)] * 10 + [smem] * 4,
        out_specs=vmem,
        scratch_shapes=[
            buf(128, 512),
            buf(1, 8192, dtype=F32),
            buf(512, 512),
            buf(512, 512),
            buf(512, 256),
            buf(8, 512),
            buf(4, 512, dtype=F32),
            buf(4, 4, 256, dtype=F32),
            buf(1, 512, dtype=F32),
            buf(512, 512),
            buf(8, 16, 512),
            buf(2, 2, 4, 4, 4, 16, 512),
            buf(2, 512, 384),
            buf(2, 512, 256),
            buf(512, 384),
            buf(512, 256),
            buf(4, 2, 4, 4, 16, 384, dtype=F32),
            buf(4, 2, 4, 4, 16, 256, dtype=F32),
        ]
        + [buf(k, n, 4, 16, w) for n, w in ((1, 640), (2, 384), (1, 384), (3, 256)) for k in (4, 3, 4, 3)]
        + [
            buf(4, 4, 16, 384, dtype=F32),
            buf(4, 4, 16, 256, dtype=F32),
            buf(16, 384),
            buf(16, 384),
            buf(272, 384, dtype=F32),
            buf(2, 4, 32, 256),
            buf(8, 32, 256),
            buf(8, 32, 256),
            buf(8, 16, 256),
            buf(8, 16, 256),
            buf(8, 8, 256, dtype=F32),
            buf(8, 8, 256, dtype=F32),
            buf(2, 8, 2, 128, 256),
            buf(8, 4, 4, 16, 512, dtype=F32),
            buf(8, 4, 16, 512, dtype=F32),
        ]
        + [buf(8, 4, 16, 512)] * 6
        + [buf(8, 16, 512)] * 6
        + [buf(8, 16, 512)] * 2
        + [
            dma(10), dma(SENDS), dma(8), dma(8), dma(2, 4), dma(2, 4, 4), dma(2, 4), dma(2), dma(4, 4), dma(4, 3), dma(), dma(8),
            dma(8), dma(8), dma(8), dma(8), dma(8, 2), dma(8, 2), dma(8, 3), dma(8, 3), dma(8),
        ],
        compiler_params=pltpu.CompilerParams(collective_id=0, has_side_effects=True, vmem_limit_bytes=56 * 2**20),
        name="mixer",
    )(
        tokens, norm_gain.reshape(1, -1), gate_proj, value_proj, maps, step_proj.T, conv_value, conv_state, mix_gain.reshape(1, -1),
        out_proj, step_bias, decay_rate, skip_gain, doc_lengths,
    )


def solution(mesh):
    return jax.shard_map(
        local,
        mesh=mesh,
        in_specs=(
            P("seq", "fsdp"), P(), P("seq", "fsdp"), P("seq", "fsdp"), P("seq", "fsdp"), P("seq", None, None),
            P(None, "fsdp"), P(), P("fsdp"), P("fsdp"), P("fsdp"), P("fsdp"), P("fsdp", "seq"), P(),
        ),
        out_specs=P("seq", "fsdp"),
        check_vma=False,
    )
```

```python
import jax
import jax.numpy as jnp
from jax import lax
from jax.experimental import pallas as pl
from jax.experimental.pallas import tpu as pltpu
from jax.sharding import PartitionSpec as P

N = 128
EPSILON = 1e-05
PRECISE = lax.Precision.HIGHEST
MESH = pl.DeviceIdType.MESH
F32 = jnp.float32
BF16 = jnp.bfloat16
WIDE = 640
STEP0 = 32
SQ = 40
SENDS = 320


def dot(a, b, precision=None):
    return jnp.dot(a, b, preferred_element_type=F32, precision=precision)


def body(
    tok_h, gain_h, gate_h, value_h, maps_h, step_h, conv_v_h, conv_s_h, mix_gain_h, out_w_h,
    bias, rate, skip, docs,
    out,
    tok, gain, gate_w, value_w, all_maps, step_w, conv_v, conv_s, mix_gain, out_w, maps_w,
    XI, X, WV, WG, SV, SG, PV, PG, S0L, S0S, R0L, R0S, S1L, S1S, R1L, R1S, S2L, S2S, R2L, R2S, S3L, S3S, R3L, R3S, RV, RG,
    HS, HR, EXT, BC, ST, SR, SO, SI, SQB, NZ, GZ, T, Q, A1, B1, C1, RA1, RB1, RC1,
    A2, B2, C2, RA2, RB2, RC2, FO, FR,
    sem_load, sem_send, sem_i, sem_a, sem_y, sem_x, sem_s, sem_w, sem_l, sem_sh, sem_h, sem_bc, sem_st, sem_in, sem_sq,
    sem_nz, sem_g, sem_gs, sem_1, sem_2, sem_f,
):
    s = lax.axis_index("seq")
    f = lax.axis_index("fsdp")
    z, c = lax.div(s, 2), lax.rem(s, 2)
    x, y = lax.div(f, 4), lax.rem(f, 4)
    sg = 1 - 2 * c

    def m4(v):
        return lax.rem(v + 8, 4)

    def m8(v):
        return lax.rem(v + 16, 8)

    def dev(z_=z, c_=c, x_=x, y_=y):
        return (2 * z_ + c_, 4 * x_ + y_)

    sibling = dev(c_=1 - c)
    peers = [(dc, dy) for dc in range(2) for dy in range(4) if (dc, dy) != (0, 0)]
    started = []

    def send(src, dst, sem, to):
        copy = pltpu.make_async_remote_copy(
            src_ref=src, dst_ref=dst, send_sem=sem_send.at[len(started)], recv_sem=sem,
            device_id=to, device_id_type=MESH,
        )
        copy.start()
        started.append((copy, None))

    def arrived(dst, sem):
        pltpu.make_async_remote_copy(
            src_ref=dst, dst_ref=dst, send_sem=sem_send.at[0], recv_sem=sem,
            device_id=sibling, device_id_type=MESH,
        ).wait_recv()

    def send_or_keep(own, src, dst, sem, to):
        copy = pltpu.make_async_remote_copy(
            src_ref=src, dst_ref=dst, send_sem=sem_send.at[len(started)], recv_sem=sem,
            device_id=to, device_id_type=MESH,
        )
        away = jnp.logical_not(own)

        @pl.when(away)
        def _():
            copy.start()

        @pl.when(own)
        def _():
            pltpu.make_async_copy(src, dst, sem).start()

        started.append((copy, away))

    def wrap_up():
        for copy, away in started:
            if away is None:
                copy.wait_send()
            else:

                @pl.when(away)
                def _(copy=copy):
                    copy.wait_send()

        assert len(started) <= SENDS

    barrier = pltpu.get_barrier_semaphore()
    own_leg = (lax.rem(f, 2) == c) & (lax.div(x, 2) == c)

    def greet(to):
        pl.semaphore_signal(barrier, inc=1, device_id=to, device_id_type=MESH)

    for i in range(8):
        for to, at in (((2 * z + lax.rem(f, 2), 8 * c + i), 8 * c + i), ((2 * z + lax.div(x, 2), 2 * i + c), 2 * i + c)):

            @pl.when(jnp.logical_not(own_leg & (f == at)))
            def _(to=to):
                greet(to)

    for o in range(1, 8):
        greet(dev(z_=m8(z + o)))
    for dc, dy in peers:
        greet(dev(c_=lax.rem(c + dc, 2), y_=m4(y + dy)))
    greet(dev(x_=m4(x + 1)))
    greet(dev(x_=m4(x - 1)))

    loads = [
        pltpu.make_async_copy(src, dst, sem_load.at[i])
        for i, (src, dst) in enumerate(
            (
                (tok_h, tok), (gain_h, gain), (value_h, value_w), (maps_h, all_maps), (step_h, step_w), (gate_h, gate_w),
                (conv_v_h, conv_v), (conv_s_h, conv_s), (mix_gain_h, mix_gain), (out_w_h, out_w),
            )
        )
    ]
    for load in loads:
        load.start()
    loads[1].wait()

    gain_col = jnp.transpose(
        jnp.broadcast_to(gain[0:1, pl.ds(pl.multiple_of(512 * s, 512), 512)], (128, 512))
    )[:, 0:1]
    lane_w = lax.broadcasted_iota(jnp.int32, (512, 128), 1)
    turn = lax.rem(128 - 32 * y, 128)

    def rows_of(half, ref_v, ref_g):
        cols = pl.ds(pl.multiple_of(256 * half, 256), 256)
        ref_v[:, 0:256] = (value_w[:, cols].astype(F32) * gain_col).astype(BF16)
        maps = pltpu.roll(maps_w[:, pl.ds(pl.multiple_of(128 * half, 128), 128)].astype(F32), turn, 1)
        steps = pltpu.roll(step_w[...].astype(F32), lax.rem(8 - 4 * half, 8), 0)
        steps = jnp.concatenate([jnp.zeros((32, 512), F32), steps, jnp.zeros((88, 512), F32)], axis=0)
        extra = jnp.where(lane_w < 32, maps, 0.0) + jnp.transpose(steps)
        ref_v[:, 256:384] = (extra * gain_col).astype(BF16)
        ref_g[...] = (gate_w[:, cols].astype(F32) * gain_col).astype(BF16)

    for load in (loads[0], *loads[2:]):
        load.wait()
    for k in range(4):

        @pl.when(x == k)
        def _(k=k):
            maps_w[...] = all_maps[:, k, :]

    pl.semaphore_wait(barrier, 32 - 2 * own_leg.astype(jnp.int32))

    for i in range(8):
        send_or_keep(
            own_leg & (f == 8 * c + i),
            tok.at[pl.ds(16 * i, 16)], XI.at[lax.div(f, 2)], sem_i.at[lax.div(f, 2)],
            (2 * z + lax.rem(f, 2), 8 * c + i),
        )
    rows_of(1 - c, SV, SG)
    send(SV, WV.at[c], sem_w.at[0], sibling)
    send(SG, WG.at[c], sem_w.at[1], sibling)
    rows_of(c, WV.at[c], WG.at[c])
    upper = lax.div(z, 4)
    lead, trail = x + upper * (y - x), y + upper * (x - y)
    for o in (4, 3, 5, 2, 6, 1, 7):
        to = m8(z + o)
        arrived(XI.at[to], sem_i.at[to])
        send(XI.at[to], X.at[c, upper, lead, trail, lax.rem(z, 4)], sem_a.at[z], dev(z_=to))
    arrived(XI.at[z], sem_i.at[z])
    pltpu.make_async_copy(XI.at[z], X.at[c, upper, lead, trail, lax.rem(z, 4)], sem_a.at[z]).start()

    lane8 = lax.broadcasted_iota(jnp.int32, (8, 128), 1)
    starts = jnp.full((8, 128), 1 << 20, jnp.int32)
    total = jnp.int32(0)
    for i in range(32):
        starts = jnp.where(lane8 == i, total, starts)
        total = total + docs[i]
    starts = starts.astype(F32)[0:1]
    first = (256 * z).astype(F32)
    t_wide = first + lax.broadcasted_iota(jnp.int32, (256, 128), 0).astype(F32)
    start_of = jnp.max(jnp.where(starts <= t_wide, starts, 0.0), axis=1, keepdims=True)
    t_col = t_wide[:, 0:1]
    into = t_col - start_of
    bias_row = jnp.zeros((8, 128), F32)
    rate_row = jnp.zeros((8, 128), F32)
    lane_256 = lax.broadcasted_iota(jnp.int32, (8, 256), 1)
    skip_row = jnp.zeros((8, 256), F32)
    for i in range(4):
        bias_row = jnp.where(lane8 == STEP0 + i, bias[4 * c + i], bias_row)
        rate_row = jnp.where(lane8 == STEP0 + i, rate[4 * c + i], rate_row)
        skip_row = jnp.where(lax.div(lane_256, 64) == i, skip[4 * c + i], skip_row)
    bias_row, rate_row, skip_row = bias_row[0:1], rate_row[0:1], skip_row[0:1]

    def at_x(q):
        return dev(x_=q)

    def at_y(q):
        return dev(y_=q)

    legs = [(x, at_x, y, at_y), (y, at_y, x, at_x)]
    def spread(h, q):
        a, to, _, _ = legs[h]
        mine = X.at[c, h, a, q]
        send(mine, mine, sem_x.at[h, a, q], to(m4(a + 1)))
        send(mine, mine, sem_x.at[h, a, q], to(m4(a - 1)))

    def relay(h, q):
        a, to, _, _ = legs[h]
        near = m4(a - sg)
        got = X.at[c, h, near, q]
        arrived(got, sem_x.at[h, near, q])
        send(got, got, sem_x.at[h, near, q], to(m4(a + sg)))

    def trailing(h, q):
        arrived(X.at[c, h, legs[h][0], q], sem_y.at[h, q])

    for h, (a, _, b, to) in enumerate(legs):
        for zt in range(4):
            arrived(X.at[c, h, a, b, zt], sem_a.at[4 * h + zt])
        mine = X.at[c, h, a, b]
        send(mine, mine, sem_y.at[h, b], to(m4(b + 1)))
        send(mine, mine, sem_y.at[h, b], to(m4(b - 1)))
        spread(h, b)
    for h, (a, _, b, to) in enumerate(legs):
        near = X.at[c, h, a, m4(b - sg)]
        trailing(h, m4(b - sg))
        send(near, near, sem_y.at[h, m4(b - sg)], to(m4(b + sg)))
        spread(h, m4(b - sg))
        trailing(h, m4(b + sg))
        spread(h, m4(b + sg))
    for h, (_, _, b, _) in enumerate(legs):
        relay(h, b)
    for h, (a, _, b, _) in enumerate(legs):
        trailing(h, m4(b + 2))
        spread(h, m4(b + 2))
        send(X.at[c, h, a], X.at[c, h, a], sem_s.at[h, a], sibling)
    arrived(WV.at[1 - c], sem_w.at[0])
    arrived(WG.at[1 - c], sem_w.at[1])

    lane_e = lax.broadcasted_iota(jnp.int32, (256, 128), 1)
    groups = [[a, m4(a - sg), m4(a + sg), m4(a + 2)] for a, _, _, _ in legs]

    def came(j):
        for h, (_, _, b, _) in enumerate(legs):
            q = groups[h][j]
            for at in range(4):
                if j > 1:
                    arrived(X.at[c, h, q, at], sem_x.at[h, q, at])
            send(X.at[c, h, q], X.at[c, h, q], sem_s.at[h, q], sibling)

    def product(g):
        for h in range(2):
            arrived(X.at[1 - c, h, groups[h][g]], sem_s.at[h, groups[h][g]])
            a = X[0, h, groups[h][g]].reshape(256, 512)
            b = X[1, h, groups[h][g]].reshape(256, 512)
            p = dot(a, WV[0]) + dot(b, WV[1])
            PG[g, h] = (dot(a, WG[0]) + dot(b, WG[1])).reshape(4, 4, 16, 256)
            a, b = a.astype(F32), b.astype(F32)
            squares = jnp.sum(a * a + b * b, axis=1, keepdims=True)
            PV[g, h, :, :, :, 0:256] = p[:, 0:256].reshape(4, 4, 16, 256)
            PV[g, h, :, :, :, 256:384] = (p[:, 256:384] + jnp.where(lane_e == SQ, squares, 0.0)).reshape(4, 4, 16, 128)

    rings = [
        (0, 1, "all", S0L, S0S, R0L, R0S),
        (1, 2, "values", S1L, S1S, R1L, R1S),
        (3, 1, "values", S2L, S2S, R2L, R2S),
        (1, 3, "gate", S3L, S3S, R3L, R3S),
    ]

    def pieces(r, d):
        g, n, kind = rings[r][:3]
        d_up, d_at = lax.div(d, 4), lax.rem(d, 4)
        got = []
        if kind != "gate":
            got.append((0, 384, PV[pl.ds(g, n), d_up, :, d_at]))
        if kind != "values":
            got.append((got[0][1] if got else 0, 256, PG[pl.ds(g, n), d_up, :, d_at]))
        return got

    def hop(r, k):
        out_l, out_s, in_l, in_s = rings[r][3:]
        if k:
            arrived(in_l.at[k - 1], sem_l.at[r, k - 1])
        for lo, wide, v in pieces(r, m8(z + (4 - k) * sg)):
            if k:
                v = v + in_l[k - 1, :, :, :, lo : lo + wide].astype(F32)
            out_l[k, :, :, :, lo : lo + wide] = v.astype(BF16)
        send(out_l.at[k], in_l.at[k], sem_l.at[r, k], dev(z_=m8(z + sg)))
        if k < 3:
            if k:
                arrived(in_s.at[k - 1], sem_sh.at[r, k - 1])
            for lo, wide, v in pieces(r, m8(z - (3 - k) * sg)):
                if k:
                    v = v + in_s[k - 1, :, :, :, lo : lo + wide].astype(F32)
                out_s[k, :, :, :, lo : lo + wide] = v.astype(BF16)
            send(out_s.at[k], in_s.at[k], sem_sh.at[r, k], dev(z_=m8(z - sg)))

    def last(r):
        g, n, kind, _, _, in_l, in_s = rings[r]
        arrived(in_l.at[3], sem_l.at[r, 3])
        arrived(in_s.at[2], sem_sh.at[r, 2])
        for lo, wide, v in pieces(r, z):
            v = v + in_l[3, :, :, :, lo : lo + wide].astype(F32) + in_s[2, :, :, :, lo : lo + wide].astype(F32)
            ref = RV if wide == 384 else RG
            for j in range(n):
                a = groups[0][g + j] + upper * (groups[1][g + j] - groups[0][g + j])
                for i in range(4):
                    ref[a + upper * (i - a), i + upper * (a - i)] = v[j, i]

    product(0)
    hop(0, 0)
    for at in (-1, 1):
        for h in range(2):
            relay(h, m4(legs[h][2] + at * sg))
    hop(0, 1)
    for h in range(2):
        relay(h, m4(legs[h][2] + 2))
    came(1)
    came(2)
    product(1)
    product(2)
    hop(1, 0)
    hop(0, 2)
    hop(1, 1)
    hop(0, 3)
    came(3)
    product(3)
    hop(2, 0)
    hop(1, 2)
    last(0)
    hop(2, 1)
    hop(1, 3)
    hop(2, 2)
    last(1)
    hop(2, 3)
    hop(3, 0)
    last(2)

    scale = lax.rsqrt(RV[:, :, :, 256:384].reshape(256, 128)[:, SQ : SQ + 1] * (1.0 / 8192) + EPSILON)
    raw = (RV[...].reshape(256, 384) * scale).astype(BF16)
    HS[...] = raw[240:256]
    send(HS, HR, sem_h, dev(z_=m8(z + 1)))
    EXT[16:272] = raw.astype(F32)

    raw_step = RV[:, :, :, 256:384].reshape(256, 128) * scale + bias_row
    step = jnp.maximum(raw_step, 0.0) + jnp.log1p(jnp.exp(-jnp.abs(raw_step)))
    log_decay = -rate_row * step
    order_r = lax.broadcasted_iota(jnp.int32, (256, 256), 0)
    order_c = lax.broadcasted_iota(jnp.int32, (256, 256), 1)
    cum = dot((order_r >= order_c).astype(F32), log_decay, PRECISE)
    cum_rows = jnp.transpose(cum)
    end = cum[255:256]
    causal = (order_r >= order_c) & (first + order_c.astype(F32) >= start_of)
    start_last = start_of[255:256]
    low = lax.broadcasted_iota(jnp.int32, (1, 128), 1) < 64

    def expand(a):
        return jnp.concatenate(
            [
                jnp.where(low, a[:, STEP0 + 2 * i : STEP0 + 2 * i + 1], a[:, STEP0 + 2 * i + 1 : STEP0 + 2 * i + 2])
                for i in range(2)
            ],
            axis=1,
        )

    step_wide = expand(step)
    tail = expand(jnp.where(t_col >= start_last, jnp.exp(end - cum), 0.0))
    carried = expand(jnp.where(start_of < first, jnp.exp(cum), 0.0))
    passing = expand(jnp.where(start_last < first, jnp.exp(end), 0.0))

    arrived(HR, sem_h)
    EXT[0:16] = HR[...].astype(F32)
    hop(3, 1)

    def conv(lo, width, taps):
        acc = jnp.zeros((256, width), F32)
        for k in range(4):
            acc = acc + jnp.where(into >= 3 - k, EXT[13 + k : 269 + k, lo : lo + width], 0.0) * taps[k]
        return acc * jax.nn.sigmoid(acc)

    maps_cols = pl.ds(pl.multiple_of(128 * c, 128), 128)
    group_row = lax.broadcasted_iota(jnp.int32, (4, 128), 0) == x
    taps_s = [
        pltpu.roll(
            jnp.broadcast_to(
                jnp.sum(jnp.where(group_row, conv_s[k, :, maps_cols], 0.0), axis=0, keepdims=True), (8, 128)
            ),
            turn,
            1,
        )[0:1]
        for k in range(4)
    ]
    maps = jnp.transpose(conv(256, 128, taps_s))[0:32].astype(BF16)
    BC[c, y] = maps
    for dc, dy in peers:
        to_c = lax.rem(c + dc, 2)
        send(BC.at[c, y], BC.at[c, y], sem_bc.at[4 * c + y], dev(c_=to_c, y_=m4(y + dy)))

    own_cols = pl.ds(pl.multiple_of(256 * c, 256), 256)
    inputs = conv(0, 256, [conv_v[k : k + 1, own_cols] for k in range(4)]).astype(BF16).astype(F32)
    stepped = inputs * step_wide
    to_end = (stepped * tail).astype(BF16)
    stepped = stepped.astype(BF16)

    for dc, dy in peers:
        pc, py = lax.rem(c + dc, 2), m4(y + dy)
        arrived(BC.at[pc, py], sem_bc.at[4 * pc + py])
    hop(3, 2)
    b_rows = BC[0].reshape(128, 256)
    c_cols = jnp.transpose(BC[1].reshape(128, 256).astype(F32)).astype(BF16)

    state = dot(b_rows, to_end).astype(BF16)
    ST[:, 0:16] = state.reshape(8, 16, 256)
    ST[:, 16:32] = jnp.broadcast_to(passing.astype(BF16)[None], (8, 16, 256))
    for o in range(1, 8):
        k = m8(z + o)
        send(ST.at[k], SR.at[z], sem_st.at[z], dev(z_=k))
    SR[z] = ST[z]

    scores = dot(c_cols, b_rows)
    parts = []
    for i in range(4):
        gaps = cum[:, STEP0 + i : STEP0 + i + 1] - cum_rows[STEP0 + i : STEP0 + i + 1, :]
        mixing = (jnp.exp(jnp.where(causal, gaps, -1e30)) * scores).astype(BF16)
        parts.append(dot(mixing, stepped[:, 128 * (i // 2) : 128 * (i // 2) + 128]))
    intra = jnp.concatenate([jnp.where(low, parts[0], parts[1]), jnp.where(low, parts[2], parts[3])], axis=1)
    partly = intra + skip_row * inputs

    for o in range(1, 8):
        k = m8(z + o)
        arrived(SR.at[k], sem_st.at[k])
    incoming = jnp.zeros((16, 256), F32)
    for i in range(8):
        SO[i] = incoming.astype(BF16)
        incoming = SR[i, 16:32].astype(F32) * incoming + SR[i, 0:16].astype(F32)
    for o in range(1, 8):
        k = m8(z + o)
        send(SO.at[k], SI.at[z], sem_in.at[z], dev(z_=k))
    SI[z] = SO[z]
    hop(3, 3)
    last(3)
    gate = RG[...].reshape(256, 256) * scale
    gate = gate * jax.nn.sigmoid(gate)
    partly = partly * gate
    carried = carried * gate
    for o in range(1, 8):
        k = m8(z + o)
        arrived(SI.at[k], sem_in.at[k])
    gated = partly + dot(c_cols, SI[...].reshape(128, 256)) * carried
    GZ[c, z] = (gated * mix_gain[0:1, own_cols]).astype(BF16).reshape(2, 128, 256)

    order = [z]
    for k in range(1, 4):
        order += [m8(z - k * sg), m8(z + k * sg)]
    order.append(m8(z + 4))
    for i in range(2):
        block = GZ.at[c, z, i]
        send(block, block, sem_g.at[z, i], dev(z_=m8(z + sg)))
        send(block, block, sem_g.at[z, i], dev(z_=m8(z - sg)))
        send(block, block, sem_gs.at[z, i], sibling)

    own_sq = 2 * y + c
    SQB[own_sq] = lax.dot_general(
        jnp.ones((8, 256), F32), gated * gated, (((1,), (1,)), ((), ())), preferred_element_type=F32, precision=PRECISE
    )
    for dc, dy in peers:
        send(SQB.at[own_sq], SQB.at[own_sq], sem_sq.at[own_sq], dev(c_=lax.rem(c + dc, 2), y_=m4(y + dy)))
    def pass_on(o, i):
        zt = order[o]
        got = GZ.at[c, zt, i]
        arrived(got, sem_g.at[zt, i])
        if o in (1, 3, 5):
            send(got, got, sem_g.at[zt, i], dev(z_=m8(z + sg)))
        if o in (2, 4):
            send(got, got, sem_g.at[zt, i], dev(z_=m8(z - sg)))
        send(got, got, sem_gs.at[zt, i], sibling)

    def forward(o):
        for i in range(2):
            pass_on(o, i)
            if o < 7:
                pass_on(o + 1, i)

    def take(o):
        zt = order[o]
        for i in range(2):
            arrived(GZ.at[1 - c, zt, i], sem_gs.at[zt, i])
        if o:
            arrived(NZ.at[zt], sem_nz.at[zt])
        norm = jnp.transpose(jnp.concatenate([NZ[zt]] * 16, axis=0))[:, 0:1]
        T[o] = ((dot(GZ[0, zt].reshape(256, 256), out_w[0:256]) + dot(GZ[1, zt].reshape(256, 256), out_w[256:512])) * norm).reshape(4, 4, 16, 512)

    def along(o, level):
        over_x = (o % 2 == 0) == (level == 1)
        p = x if over_x else y

        def to(q):
            return dev(x_=q) if over_x else dev(y_=q)

        return p, to

    def quarter(o, q):
        return T[o, q] if o % 2 == 0 else T[o, :, q]

    straight = (6, 7)

    def first_out(o):
        p, to = along(o, 1)
        A1[o] = quarter(o, m4(p + 2)).astype(BF16)
        send(A1.at[o], RA1.at[o], sem_1.at[o, 0], to(m4(p + 2) if o in straight else m4(p + sg)))
        B1[o] = quarter(o, m4(p - sg)).astype(BF16)
        send(B1.at[o], RB1.at[o], sem_1.at[o, 1], to(m4(p - sg)))
        if o in straight:
            C1[o] = quarter(o, m4(p + sg)).astype(BF16)
            send(C1.at[o], RC1.at[o], sem_1.at[o, 2], to(m4(p + sg)))

    def first_relay(o):
        p, to = along(o, 1)
        arrived(RA1.at[o], sem_1.at[o, 0])
        C1[o] = (quarter(o, m4(p + sg)) + RA1[o].astype(F32)).astype(BF16)
        send(C1.at[o], RC1.at[o], sem_1.at[o, 2], to(m4(p + sg)))

    def second_out(o):
        p, _ = along(o, 1)
        arrived(RB1.at[o], sem_1.at[o, 1])
        arrived(RC1.at[o], sem_1.at[o, 2])
        summed = quarter(o, p) + RB1[o].astype(F32) + RC1[o].astype(F32)
        if o in straight:
            arrived(RA1.at[o], sem_1.at[o, 0])
            summed = summed + RA1[o].astype(F32)
        Q[o] = summed
        p, to = along(o, 2)
        for i, (out_b, in_b, q) in enumerate(((A2, RA2, m4(p + 2)), (B2, RB2, m4(p - sg)), (C2, RC2, m4(p + sg)))):
            out_b[o] = Q[o, q].astype(BF16)
            send(out_b.at[o], in_b.at[o], sem_2.at[o, i], to(q))

    block_at = f
    row_block = lax.rem(block_at, 8)
    to_core = lax.div(block_at, 8)

    def finish(o):
        p, _ = along(o, 2)
        for i, in_b in enumerate((RA2, RB2, RC2)):
            arrived(in_b.at[o], sem_2.at[o, i])
        FO[o] = (Q[o, p] + RA2[o].astype(F32) + RB2[o].astype(F32) + RC2[o].astype(F32)).astype(BF16)
        to = (2 * order[o] + to_core, s)
        own = (to[0] == s) & (s == f) if o == 0 else None
        if own is None:
            send(FO.at[o], FR.at[row_block], sem_f.at[row_block], to)
        else:
            send_or_keep(own, FO.at[o], FR.at[row_block], sem_f.at[row_block], to)

    forward(1)
    for dc, dy in peers:
        k = 2 * m4(y + dy) + lax.rem(c + dc, 2)
        arrived(SQB.at[k], sem_sq.at[k])
    NZ[z] = lax.rsqrt(jnp.sum(SQB[...], axis=0) * (1.0 / 2048) + EPSILON)
    for o in range(1, 8):
        send(NZ.at[z], NZ.at[z], sem_nz.at[z], dev(z_=m8(z + o)))
    take(0)
    first_out(0)
    forward(3)
    for o in (1, 2):
        take(o)
        first_out(o)
    first_relay(0)
    forward(5)
    for o in (3, 4):
        take(o)
        first_out(o)
    first_relay(1)
    first_relay(2)
    second_out(0)
    forward(7)
    for o in (5, 6):
        take(o)
        first_out(o)
    first_relay(3)
    first_relay(4)
    take(7)
    first_out(7)
    second_out(1)
    second_out(2)
    first_relay(5)
    second_out(3)
    second_out(4)
    for o in range(3):
        finish(o)
    second_out(6)
    second_out(5)
    second_out(7)
    for o in (3, 4, 6, 5, 7):
        finish(o)

    for i in range(8):
        arrived(FR.at[i], sem_f.at[i])
    out[...] = (tok[...].astype(F32) + FR[...].reshape(128, 512).astype(F32)).astype(BF16)

    wrap_up()


def local(
    tokens, norm_gain, gate_proj, value_proj, step_proj, state_proj, conv_value, conv_state, step_bias, decay_rate,
    skip_gain, mix_gain, out_proj, doc_lengths,
):
    vmem = pl.BlockSpec(memory_space=pltpu.VMEM)
    smem = pl.BlockSpec(memory_space=pltpu.SMEM)

    def buf(*shape, dtype=BF16):
        return pltpu.VMEM(shape, dtype)

    def dma(*shape):
        return pltpu.SemaphoreType.DMA(shape)

    return pl.pallas_call(
        body,
        out_shape=jax.ShapeDtypeStruct((128, 512), BF16),
        in_specs=[pl.BlockSpec(memory_space=pl.ANY)] * 10 + [smem] * 4,
        out_specs=vmem,
        scratch_shapes=[
            buf(128, 512),
            buf(1, 8192, dtype=F32),
            buf(512, 512),
            buf(512, 512),
            buf(512, 4, 256),
            buf(8, 512),
            buf(4, 512, dtype=F32),
            buf(4, 4, 256, dtype=F32),
            buf(1, 512, dtype=F32),
            buf(512, 512),
            buf(512, 256),
            buf(8, 16, 512),
            buf(2, 2, 4, 4, 4, 16, 512),
            buf(2, 512, 384),
            buf(2, 512, 256),
            buf(512, 384),
            buf(512, 256),
            buf(4, 2, 4, 4, 16, 384, dtype=F32),
            buf(4, 2, 4, 4, 16, 256, dtype=F32),
        ]
        + [buf(k, n, 4, 16, w) for n, w in ((1, 640), (2, 384), (1, 384), (3, 256)) for k in (4, 3, 4, 3)]
        + [
            buf(4, 4, 16, 384, dtype=F32),
            buf(4, 4, 16, 256, dtype=F32),
            buf(16, 384),
            buf(16, 384),
            buf(272, 384, dtype=F32),
            buf(2, 4, 32, 256),
            buf(8, 32, 256),
            buf(8, 32, 256),
            buf(8, 16, 256),
            buf(8, 16, 256),
            buf(8, 8, 256, dtype=F32),
            buf(8, 8, 256, dtype=F32),
            buf(2, 8, 2, 128, 256),
            buf(8, 4, 4, 16, 512, dtype=F32),
            buf(8, 4, 16, 512, dtype=F32),
        ]
        + [buf(8, 4, 16, 512)] * 6
        + [buf(8, 16, 512)] * 6
        + [buf(8, 16, 512)] * 2
        + [
            dma(10), dma(SENDS), dma(8), dma(8), dma(2, 4), dma(2, 4, 4), dma(2, 4), dma(2), dma(4, 4), dma(4, 3), dma(), dma(8),
            dma(8), dma(8), dma(8), dma(8), dma(8, 2), dma(8, 2), dma(8, 3), dma(8, 3), dma(8),
        ],
        compiler_params=pltpu.CompilerParams(collective_id=0, has_side_effects=True, vmem_limit_bytes=56 * 2**20),
        name="mixer",
    )(
        tokens, norm_gain.reshape(1, -1), gate_proj, value_proj, state_proj, step_proj.T, conv_value, conv_state, mix_gain.reshape(1, -1),
        out_proj, step_bias, decay_rate, skip_gain, doc_lengths,
    )


def solution(mesh):
    return jax.shard_map(
        local,
        mesh=mesh,
        in_specs=(
            P("seq", "fsdp"), P(), P("seq", "fsdp"), P("seq", "fsdp"), P("seq", "fsdp"), P("seq", None, None),
            P(None, "fsdp"), P(), P("fsdp"), P("fsdp"), P("fsdp"), P("fsdp"), P("fsdp", "seq"), P(),
        ),
        out_specs=P("seq", "fsdp"),
        check_vma=False,
    )
```

```python
import jax
import jax.numpy as jnp
from jax import lax
from jax.experimental import pallas as pl
from jax.experimental.pallas import tpu as pltpu
from jax.sharding import PartitionSpec as P

N = 128
EPSILON = 1e-05
PRECISE = lax.Precision.HIGHEST
MESH = pl.DeviceIdType.MESH
F32 = jnp.float32
BF16 = jnp.bfloat16
WIDE = 640
STEP0 = 32
SQ = 40
SENDS = 400
PIECES = 4


def dot(a, b, precision=None):
    return jnp.dot(a, b, preferred_element_type=F32, precision=precision)


def body(
    tok_h, gain_h, gate_h, value_h, maps_h, step_h, conv_v_h, conv_s_h, mix_gain_h, out_w_h,
    bias, rate, skip, docs,
    out,
    tok, gain, gate_w, value_w, all_maps, step_w, conv_v, conv_s, mix_gain, out_w, maps_w,
    XI, X, WV, WG, SV, SG, PV, PG, S0L, S0S, R0L, R0S, S1L, S1S, R1L, R1S, S2L, S2S, R2L, R2S, S3L, S3S, R3L, R3S, S4L, S4S, R4L, R4S, RV, RG,
    HS, HR, EXT, BC, ST, SR, SO, SI, SQB, NZ, GZ, T, Q, A1, B1, C1, RA1, RB1, RC1,
    A2, B2, C2, RA2, RB2, RC2, FO, FR,
    sem_load, sem_send, sem_i, sem_a, sem_y, sem_x, sem_s, sem_w, sem_l, sem_sh, sem_h, sem_bc, sem_st, sem_in, sem_sq,
    sem_nz, sem_g, sem_gs, sem_1, sem_2, sem_f,
):
    s = lax.axis_index("seq")
    f = lax.axis_index("fsdp")
    z, c = lax.div(s, 2), lax.rem(s, 2)
    x, y = lax.div(f, 4), lax.rem(f, 4)
    sg = 1 - 2 * c

    def m4(v):
        return lax.rem(v + 8, 4)

    def m8(v):
        return lax.rem(v + 16, 8)

    def dev(z_=z, c_=c, x_=x, y_=y):
        return (2 * z_ + c_, 4 * x_ + y_)

    sibling = dev(c_=1 - c)
    peers = [(dc, dy) for dc in range(2) for dy in range(4) if (dc, dy) != (0, 0)]
    started = []

    def send(src, dst, sem, to):
        copy = pltpu.make_async_remote_copy(
            src_ref=src, dst_ref=dst, send_sem=sem_send.at[len(started)], recv_sem=sem,
            device_id=to, device_id_type=MESH,
        )
        copy.start()
        started.append((copy, None))

    def arrived(dst, sem):
        pltpu.make_async_remote_copy(
            src_ref=dst, dst_ref=dst, send_sem=sem_send.at[0], recv_sem=sem,
            device_id=sibling, device_id_type=MESH,
        ).wait_recv()

    def send_or_keep(own, src, dst, sem, to):
        copy = pltpu.make_async_remote_copy(
            src_ref=src, dst_ref=dst, send_sem=sem_send.at[len(started)], recv_sem=sem,
            device_id=to, device_id_type=MESH,
        )
        away = jnp.logical_not(own)

        @pl.when(away)
        def _():
            copy.start()

        @pl.when(own)
        def _():
            pltpu.make_async_copy(src, dst, sem).start()

        started.append((copy, away))

    def wrap_up():
        for copy, away in started:
            if away is None:
                copy.wait_send()
            else:

                @pl.when(away)
                def _(copy=copy):
                    copy.wait_send()

        assert len(started) <= SENDS

    barrier = pltpu.get_barrier_semaphore()
    own_leg = (lax.rem(f, 2) == c) & (lax.div(x, 2) == c)

    def greet(to):
        pl.semaphore_signal(barrier, inc=1, device_id=to, device_id_type=MESH)

    for i in range(8):
        for to, at in (((2 * z + lax.rem(f, 2), 8 * c + i), 8 * c + i), ((2 * z + lax.div(x, 2), 2 * i + c), 2 * i + c)):

            @pl.when(jnp.logical_not(own_leg & (f == at)))
            def _(to=to):
                greet(to)

    for o in range(1, 8):
        greet(dev(z_=m8(z + o)))
    for dc, dy in peers:
        greet(dev(c_=lax.rem(c + dc, 2), y_=m4(y + dy)))
    greet(dev(x_=m4(x + 1)))
    greet(dev(x_=m4(x - 1)))

    loads = [
        pltpu.make_async_copy(src, dst, sem_load.at[i])
        for i, (src, dst) in enumerate(
            (
                (tok_h, tok), (gain_h, gain), (value_h, value_w), (maps_h, all_maps), (step_h, step_w), (gate_h, gate_w),
                (conv_v_h, conv_v), (conv_s_h, conv_s), (mix_gain_h, mix_gain), (out_w_h, out_w),
            )
        )
    ]
    for load in loads:
        load.start()
    loads[1].wait()

    gain_col = jnp.transpose(
        jnp.broadcast_to(gain[0:1, pl.ds(pl.multiple_of(512 * s, 512), 512)], (128, 512))
    )[:, 0:1]
    lane_w = lax.broadcasted_iota(jnp.int32, (512, 128), 1)
    turn = lax.rem(128 - 32 * y, 128)

    def rows_of(half, ref_v, ref_g):
        cols = pl.ds(pl.multiple_of(256 * half, 256), 256)
        ref_v[:, 0:256] = (value_w[:, cols].astype(F32) * gain_col).astype(BF16)
        maps = pltpu.roll(maps_w[:, pl.ds(pl.multiple_of(128 * half, 128), 128)].astype(F32), turn, 1)
        steps = pltpu.roll(step_w[...].astype(F32), lax.rem(8 - 4 * half, 8), 0)
        steps = jnp.concatenate([jnp.zeros((32, 512), F32), steps, jnp.zeros((88, 512), F32)], axis=0)
        extra = jnp.where(lane_w < 32, maps, 0.0) + jnp.transpose(steps)
        ref_v[:, 256:384] = (extra * gain_col).astype(BF16)
        ref_g[...] = (gate_w[:, cols].astype(F32) * gain_col).astype(BF16)

    for load in (loads[0], *loads[2:]):
        load.wait()
    for k in range(4):

        @pl.when(x == k)
        def _(k=k):
            maps_w[...] = all_maps[:, k, :]

    pl.semaphore_wait(barrier, 32 - 2 * own_leg.astype(jnp.int32))

    for i in range(8):
        send_or_keep(
            own_leg & (f == 8 * c + i),
            tok.at[pl.ds(16 * i, 16)], XI.at[lax.div(f, 2)], sem_i.at[lax.div(f, 2)],
            (2 * z + lax.rem(f, 2), 8 * c + i),
        )
    rows_of(1 - c, SV, SG)
    send(SV, WV.at[c], sem_w.at[0], sibling)
    send(SG, WG.at[c], sem_w.at[1], sibling)
    rows_of(c, WV.at[c], WG.at[c])
    upper = lax.div(z, 4)
    lead, trail = x + upper * (y - x), y + upper * (x - y)
    for o in (4, 3, 5, 2, 6, 1, 7):
        to = m8(z + o)
        arrived(XI.at[to], sem_i.at[to])
        send(XI.at[to], X.at[c, upper, lead, trail, lax.rem(z, 4)], sem_a.at[z], dev(z_=to))
    arrived(XI.at[z], sem_i.at[z])
    pltpu.make_async_copy(XI.at[z], X.at[c, upper, lead, trail, lax.rem(z, 4)], sem_a.at[z]).start()

    lane8 = lax.broadcasted_iota(jnp.int32, (8, 128), 1)
    starts = jnp.full((8, 128), 1 << 20, jnp.int32)
    total = jnp.int32(0)
    for i in range(32):
        starts = jnp.where(lane8 == i, total, starts)
        total = total + docs[i]
    starts = starts.astype(F32)[0:1]
    first = (256 * z).astype(F32)
    t_wide = first + lax.broadcasted_iota(jnp.int32, (256, 128), 0).astype(F32)
    start_of = jnp.max(jnp.where(starts <= t_wide, starts, 0.0), axis=1, keepdims=True)
    t_col = t_wide[:, 0:1]
    into = t_col - start_of
    bias_row = jnp.zeros((8, 128), F32)
    rate_row = jnp.zeros((8, 128), F32)
    lane_256 = lax.broadcasted_iota(jnp.int32, (8, 256), 1)
    skip_row = jnp.zeros((8, 256), F32)
    for i in range(4):
        bias_row = jnp.where(lane8 == STEP0 + i, bias[4 * c + i], bias_row)
        rate_row = jnp.where(lane8 == STEP0 + i, rate[4 * c + i], rate_row)
        skip_row = jnp.where(lax.div(lane_256, 64) == i, skip[4 * c + i], skip_row)
    bias_row, rate_row, skip_row = bias_row[0:1], rate_row[0:1], skip_row[0:1]

    def at_x(q):
        return dev(x_=q)

    def at_y(q):
        return dev(y_=q)

    legs = [(x, at_x, y, at_y), (y, at_y, x, at_x)]
    def spread(h, q):
        a, to, _, _ = legs[h]
        mine = X.at[c, h, a, q]
        send(mine, mine, sem_x.at[h, a, q], to(m4(a + 1)))
        send(mine, mine, sem_x.at[h, a, q], to(m4(a - 1)))

    def relay(h, q):
        a, to, _, _ = legs[h]
        near = m4(a - sg)
        got = X.at[c, h, near, q]
        arrived(got, sem_x.at[h, near, q])
        send(got, got, sem_x.at[h, near, q], to(m4(a + sg)))

    def trailing(h, q):
        arrived(X.at[c, h, legs[h][0], q], sem_y.at[h, q])

    for h, (a, _, b, to) in enumerate(legs):
        for zt in range(4):
            arrived(X.at[c, h, a, b, zt], sem_a.at[4 * h + zt])
        mine = X.at[c, h, a, b]
        send(mine, mine, sem_y.at[h, b], to(m4(b + 1)))
        send(mine, mine, sem_y.at[h, b], to(m4(b - 1)))
    for h, (_, _, b, _) in enumerate(legs):
        spread(h, b)
    for h, (a, _, b, to) in enumerate(legs):
        near = X.at[c, h, a, m4(b - sg)]
        trailing(h, m4(b - sg))
        send(near, near, sem_y.at[h, m4(b - sg)], to(m4(b + sg)))
    for h, (_, _, b, _) in enumerate(legs):
        spread(h, m4(b - sg))
        trailing(h, m4(b + sg))
        spread(h, m4(b + sg))
    for h, (_, _, b, _) in enumerate(legs):
        relay(h, b)
    for h, (a, _, b, _) in enumerate(legs):
        trailing(h, m4(b + 2))
        spread(h, m4(b + 2))
        send(X.at[c, h, a], X.at[c, h, a], sem_s.at[h, a], sibling)
    arrived(WV.at[1 - c], sem_w.at[0])
    arrived(WG.at[1 - c], sem_w.at[1])

    lane_e = lax.broadcasted_iota(jnp.int32, (256, 128), 1)
    groups = [[a, m4(a - sg), m4(a + sg), m4(a + 2)] for a, _, _, _ in legs]

    def came(j):
        for h, (_, _, b, _) in enumerate(legs):
            q = groups[h][j]
            for at in range(4):
                if j > 1:
                    arrived(X.at[c, h, q, at], sem_x.at[h, q, at])
            send(X.at[c, h, q], X.at[c, h, q], sem_s.at[h, q], sibling)

    def product(g):
        for h in range(2):
            arrived(X.at[1 - c, h, groups[h][g]], sem_s.at[h, groups[h][g]])
            a = X[0, h, groups[h][g]].reshape(256, 512)
            b = X[1, h, groups[h][g]].reshape(256, 512)
            p = dot(a, WV[0]) + dot(b, WV[1])
            PG[g, h] = (dot(a, WG[0]) + dot(b, WG[1])).reshape(4, 4, 16, 256)
            a, b = a.astype(F32), b.astype(F32)
            squares = jnp.sum(a * a + b * b, axis=1, keepdims=True)
            PV[g, h, :, :, :, 0:256] = p[:, 0:256].reshape(4, 4, 16, 256)
            PV[g, h, :, :, :, 256:384] = (p[:, 256:384] + jnp.where(lane_e == SQ, squares, 0.0)).reshape(4, 4, 16, 128)

    rings = [
        (0, 1, "all", S0L, S0S, R0L, R0S),
        (1, 1, "values", S1L, S1S, R1L, R1S),
        (2, 1, "values", S2L, S2S, R2L, R2S),
        (3, 1, "values", S3L, S3S, R3L, R3S),
        (1, 3, "gate", S4L, S4S, R4L, R4S),
    ]

    def pieces(r, d):
        g, n, kind = rings[r][:3]
        d_up, d_at = lax.div(d, 4), lax.rem(d, 4)
        got = []
        if kind != "gate":
            got.append((0, 384, PV[pl.ds(g, n), d_up, :, d_at]))
        if kind != "values":
            got.append((got[0][1] if got else 0, 256, PG[pl.ds(g, n), d_up, :, d_at]))
        return got

    def hop(r, k):
        out_l, out_s, in_l, in_s = rings[r][3:]
        if k:
            arrived(in_l.at[k - 1], sem_l.at[r, k - 1])
        for lo, wide, v in pieces(r, m8(z + (4 - k) * sg)):
            if k:
                v = v + in_l[k - 1, :, :, :, lo : lo + wide].astype(F32)
            out_l[k, :, :, :, lo : lo + wide] = v.astype(BF16)
        send(out_l.at[k], in_l.at[k], sem_l.at[r, k], dev(z_=m8(z + sg)))
        if k < 3:
            if k:
                arrived(in_s.at[k - 1], sem_sh.at[r, k - 1])
            for lo, wide, v in pieces(r, m8(z - (3 - k) * sg)):
                if k:
                    v = v + in_s[k - 1, :, :, :, lo : lo + wide].astype(F32)
                out_s[k, :, :, :, lo : lo + wide] = v.astype(BF16)
            send(out_s.at[k], in_s.at[k], sem_sh.at[r, k], dev(z_=m8(z - sg)))

    def last(r):
        g, n, kind, _, _, in_l, in_s = rings[r]
        arrived(in_l.at[3], sem_l.at[r, 3])
        arrived(in_s.at[2], sem_sh.at[r, 2])
        for lo, wide, v in pieces(r, z):
            v = v + in_l[3, :, :, :, lo : lo + wide].astype(F32) + in_s[2, :, :, :, lo : lo + wide].astype(F32)
            ref = RV if wide == 384 else RG
            for j in range(n):
                a = groups[0][g + j] + upper * (groups[1][g + j] - groups[0][g + j])
                for i in range(4):
                    ref[a + upper * (i - a), i + upper * (a - i)] = v[j, i]

    product(0)
    hop(0, 0)
    for at in (-1, 1):
        for h in range(2):
            relay(h, m4(legs[h][2] + at * sg))
    hop(0, 1)
    for h in range(2):
        relay(h, m4(legs[h][2] + 2))
    came(1)
    came(2)
    product(1)
    hop(1, 0)
    product(2)
    hop(2, 0)
    hop(0, 2)
    hop(1, 1)
    hop(2, 1)
    hop(0, 3)
    came(3)
    product(3)
    hop(3, 0)
    hop(1, 2)
    hop(2, 2)
    hop(3, 1)
    hop(1, 3)
    hop(2, 3)
    hop(3, 2)
    last(0)
    last(1)
    hop(3, 3)
    last(2)
    hop(4, 0)
    last(3)

    scale = lax.rsqrt(RV[:, :, :, 256:384].reshape(256, 128)[:, SQ : SQ + 1] * (1.0 / 8192) + EPSILON)
    raw = (RV[...].reshape(256, 384) * scale).astype(BF16)
    HS[...] = raw[240:256]
    send(HS, HR, sem_h, dev(z_=m8(z + 1)))
    EXT[16:272] = raw.astype(F32)

    raw_step = RV[:, :, :, 256:384].reshape(256, 128) * scale + bias_row
    step = jnp.maximum(raw_step, 0.0) + jnp.log1p(jnp.exp(-jnp.abs(raw_step)))
    log_decay = -rate_row * step
    order_r = lax.broadcasted_iota(jnp.int32, (256, 256), 0)
    order_c = lax.broadcasted_iota(jnp.int32, (256, 256), 1)
    cum = dot((order_r >= order_c).astype(F32), log_decay, PRECISE)
    cum_rows = jnp.transpose(cum)
    end = cum[255:256]
    causal = (order_r >= order_c) & (first + order_c.astype(F32) >= start_of)
    start_last = start_of[255:256]
    low = lax.broadcasted_iota(jnp.int32, (1, 128), 1) < 64

    def expand(a):
        return jnp.concatenate(
            [
                jnp.where(low, a[:, STEP0 + 2 * i : STEP0 + 2 * i + 1], a[:, STEP0 + 2 * i + 1 : STEP0 + 2 * i + 2])
                for i in range(2)
            ],
            axis=1,
        )

    step_wide = expand(step)
    tail = expand(jnp.where(t_col >= start_last, jnp.exp(end - cum), 0.0))
    carried = expand(jnp.where(start_of < first, jnp.exp(cum), 0.0))
    passing = expand(jnp.where(start_last < first, jnp.exp(end), 0.0))

    arrived(HR, sem_h)
    EXT[0:16] = HR[...].astype(F32)
    hop(4, 1)

    def conv(lo, width, taps):
        acc = jnp.zeros((256, width), F32)
        for k in range(4):
            acc = acc + jnp.where(into >= 3 - k, EXT[13 + k : 269 + k, lo : lo + width], 0.0) * taps[k]
        return acc * jax.nn.sigmoid(acc)

    maps_cols = pl.ds(pl.multiple_of(128 * c, 128), 128)
    group_row = lax.broadcasted_iota(jnp.int32, (4, 128), 0) == x
    taps_s = [
        pltpu.roll(
            jnp.broadcast_to(
                jnp.sum(jnp.where(group_row, conv_s[k, :, maps_cols], 0.0), axis=0, keepdims=True), (8, 128)
            ),
            turn,
            1,
        )[0:1]
        for k in range(4)
    ]
    maps = jnp.transpose(conv(256, 128, taps_s))[0:32].astype(BF16)
    BC[c, y] = maps
    for dc, dy in peers:
        to_c = lax.rem(c + dc, 2)
        send(BC.at[c, y], BC.at[c, y], sem_bc.at[4 * c + y], dev(c_=to_c, y_=m4(y + dy)))

    own_cols = pl.ds(pl.multiple_of(256 * c, 256), 256)
    inputs = conv(0, 256, [conv_v[k : k + 1, own_cols] for k in range(4)]).astype(BF16).astype(F32)
    stepped = inputs * step_wide
    to_end = (stepped * tail).astype(BF16)
    stepped = stepped.astype(BF16)

    for dc, dy in peers:
        pc, py = lax.rem(c + dc, 2), m4(y + dy)
        arrived(BC.at[pc, py], sem_bc.at[4 * pc + py])
    hop(4, 2)
    b_rows = BC[0].reshape(128, 256)
    c_cols = jnp.transpose(BC[1].reshape(128, 256).astype(F32)).astype(BF16)

    state = dot(b_rows, to_end).astype(BF16)
    ST[:, 0:16] = state.reshape(8, 16, 256)
    ST[:, 16:32] = jnp.broadcast_to(passing.astype(BF16)[None], (8, 16, 256))
    for o in range(1, 8):
        k = m8(z + o)
        send(ST.at[k], SR.at[z], sem_st.at[z], dev(z_=k))
    SR[z] = ST[z]

    scores = dot(c_cols, b_rows)
    parts = []
    for i in range(4):
        gaps = cum[:, STEP0 + i : STEP0 + i + 1] - cum_rows[STEP0 + i : STEP0 + i + 1, :]
        mixing = (jnp.exp(jnp.where(causal, gaps, -1e30)) * scores).astype(BF16)
        parts.append(dot(mixing, stepped[:, 128 * (i // 2) : 128 * (i // 2) + 128]))
    intra = jnp.concatenate([jnp.where(low, parts[0], parts[1]), jnp.where(low, parts[2], parts[3])], axis=1)
    partly = intra + skip_row * inputs
    hop(4, 3)

    for o in range(1, 8):
        k = m8(z + o)
        arrived(SR.at[k], sem_st.at[k])
    incoming = jnp.zeros((16, 256), F32)
    for i in range(8):
        SO[i] = incoming.astype(BF16)
        incoming = SR[i, 16:32].astype(F32) * incoming + SR[i, 0:16].astype(F32)
    for o in range(1, 8):
        k = m8(z + o)
        send(SO.at[k], SI.at[z], sem_in.at[z], dev(z_=k))
    SI[z] = SO[z]
    last(4)
    gate = RG[...].reshape(256, 256) * scale
    gate = gate * jax.nn.sigmoid(gate)
    partly = partly * gate
    carried = carried * gate
    for o in range(1, 8):
        k = m8(z + o)
        arrived(SI.at[k], sem_in.at[k])
    gated = partly + dot(c_cols, SI[...].reshape(128, 256)) * carried
    GZ[c, z] = (gated * mix_gain[0:1, own_cols]).astype(BF16).reshape(PIECES, 256 // PIECES, 256)

    order = [z]
    for k in range(1, 4):
        order += [m8(z - k * sg), m8(z + k * sg)]
    order.append(m8(z + 4))
    for i in range(PIECES):
        block = GZ.at[c, z, i]
        send(block, block, sem_g.at[z, i], dev(z_=m8(z + sg)))
        send(block, block, sem_g.at[z, i], dev(z_=m8(z - sg)))
        send(block, block, sem_gs.at[z, i], sibling)

    own_sq = 2 * y + c
    SQB[own_sq] = lax.dot_general(
        jnp.ones((8, 256), F32), gated * gated, (((1,), (1,)), ((), ())), preferred_element_type=F32, precision=PRECISE
    )
    for dc, dy in peers:
        send(SQB.at[own_sq], SQB.at[own_sq], sem_sq.at[own_sq], dev(c_=lax.rem(c + dc, 2), y_=m4(y + dy)))
    def pass_on(o, i):
        zt = order[o]
        got = GZ.at[c, zt, i]
        arrived(got, sem_g.at[zt, i])
        if o in (1, 3, 5):
            send(got, got, sem_g.at[zt, i], dev(z_=m8(z + sg)))
        if o in (2, 4):
            send(got, got, sem_g.at[zt, i], dev(z_=m8(z - sg)))
        send(got, got, sem_gs.at[zt, i], sibling)

    def forward(o):
        for i in range(PIECES):
            pass_on(o, i)
            if o < 7:
                pass_on(o + 1, i)

    def take(o):
        zt = order[o]
        for i in range(PIECES):
            arrived(GZ.at[1 - c, zt, i], sem_gs.at[zt, i])
        if o:
            arrived(NZ.at[zt], sem_nz.at[zt])
        norm = jnp.transpose(jnp.concatenate([NZ[zt]] * 16, axis=0))[:, 0:1]
        T[o] = ((dot(GZ[0, zt].reshape(256, 256), out_w[0:256]) + dot(GZ[1, zt].reshape(256, 256), out_w[256:512])) * norm).reshape(4, 4, 16, 512)

    def along(o, level):
        over_x = (o % 2 == 0) == (level == 1)
        p = x if over_x else y

        def to(q):
            return dev(x_=q) if over_x else dev(y_=q)

        return p, to

    def quarter(o, q):
        return T[o, q] if o % 2 == 0 else T[o, :, q]

    straight = (6, 7)

    def first_out(o):
        p, to = along(o, 1)
        A1[o] = quarter(o, m4(p + 2)).astype(BF16)
        send(A1.at[o], RA1.at[o], sem_1.at[o, 0], to(m4(p + 2) if o in straight else m4(p + sg)))
        B1[o] = quarter(o, m4(p - sg)).astype(BF16)
        send(B1.at[o], RB1.at[o], sem_1.at[o, 1], to(m4(p - sg)))
        if o in straight:
            C1[o] = quarter(o, m4(p + sg)).astype(BF16)
            send(C1.at[o], RC1.at[o], sem_1.at[o, 2], to(m4(p + sg)))

    def first_relay(o):
        p, to = along(o, 1)
        arrived(RA1.at[o], sem_1.at[o, 0])
        C1[o] = (quarter(o, m4(p + sg)) + RA1[o].astype(F32)).astype(BF16)
        send(C1.at[o], RC1.at[o], sem_1.at[o, 2], to(m4(p + sg)))

    def second_out(o):
        p, _ = along(o, 1)
        arrived(RB1.at[o], sem_1.at[o, 1])
        arrived(RC1.at[o], sem_1.at[o, 2])
        summed = quarter(o, p) + RB1[o].astype(F32) + RC1[o].astype(F32)
        if o in straight:
            arrived(RA1.at[o], sem_1.at[o, 0])
            summed = summed + RA1[o].astype(F32)
        Q[o] = summed
        p, to = along(o, 2)
        for i, (out_b, in_b, q) in enumerate(((A2, RA2, m4(p + 2)), (B2, RB2, m4(p - sg)), (C2, RC2, m4(p + sg)))):
            out_b[o] = Q[o, q].astype(BF16)
            send(out_b.at[o], in_b.at[o], sem_2.at[o, i], to(q))

    block_at = f
    row_block = lax.rem(block_at, 8)
    to_core = lax.div(block_at, 8)

    def finish(o):
        p, _ = along(o, 2)
        for i, in_b in enumerate((RA2, RB2, RC2)):
            arrived(in_b.at[o], sem_2.at[o, i])
        FO[o] = (Q[o, p] + RA2[o].astype(F32) + RB2[o].astype(F32) + RC2[o].astype(F32)).astype(BF16)
        to = (2 * order[o] + to_core, s)
        own = (to[0] == s) & (s == f) if o == 0 else None
        if own is None:
            send(FO.at[o], FR.at[row_block], sem_f.at[row_block], to)
        else:
            send_or_keep(own, FO.at[o], FR.at[row_block], sem_f.at[row_block], to)

    forward(1)
    for dc, dy in peers:
        k = 2 * m4(y + dy) + lax.rem(c + dc, 2)
        arrived(SQB.at[k], sem_sq.at[k])
    NZ[z] = lax.rsqrt(jnp.sum(SQB[...], axis=0) * (1.0 / 2048) + EPSILON)
    for o in range(1, 8):
        send(NZ.at[z], NZ.at[z], sem_nz.at[z], dev(z_=m8(z + o)))
    take(0)
    first_out(0)
    forward(3)
    for o in (1, 2):
        take(o)
        first_out(o)
    first_relay(0)
    forward(5)
    for o in (3, 4):
        take(o)
        first_out(o)
    first_relay(1)
    first_relay(2)
    second_out(0)
    forward(7)
    for o in (5, 6):
        take(o)
        first_out(o)
    first_relay(3)
    first_relay(4)
    take(7)
    first_out(7)
    second_out(1)
    second_out(2)
    first_relay(5)
    second_out(3)
    second_out(4)
    for o in range(3):
        finish(o)
    second_out(6)
    second_out(5)
    second_out(7)
    for o in (3, 4, 6, 5, 7):
        finish(o)

    for i in range(8):
        arrived(FR.at[i], sem_f.at[i])
    out[...] = (tok[...].astype(F32) + FR[...].reshape(128, 512).astype(F32)).astype(BF16)

    wrap_up()


def local(
    tokens, norm_gain, gate_proj, value_proj, step_proj, state_proj, conv_value, conv_state, step_bias, decay_rate,
    skip_gain, mix_gain, out_proj, doc_lengths,
):
    vmem = pl.BlockSpec(memory_space=pltpu.VMEM)
    smem = pl.BlockSpec(memory_space=pltpu.SMEM)

    def buf(*shape, dtype=BF16):
        return pltpu.VMEM(shape, dtype)

    def dma(*shape):
        return pltpu.SemaphoreType.DMA(shape)

    return pl.pallas_call(
        body,
        out_shape=jax.ShapeDtypeStruct((128, 512), BF16),
        in_specs=[pl.BlockSpec(memory_space=pl.ANY)] * 10 + [smem] * 4,
        out_specs=vmem,
        scratch_shapes=[
            buf(128, 512),
            buf(1, 8192, dtype=F32),
            buf(512, 512),
            buf(512, 512),
            buf(512, 4, 256),
            buf(8, 512),
            buf(4, 512, dtype=F32),
            buf(4, 4, 256, dtype=F32),
            buf(1, 512, dtype=F32),
            buf(512, 512),
            buf(512, 256),
            buf(8, 16, 512),
            buf(2, 2, 4, 4, 4, 16, 512),
            buf(2, 512, 384),
            buf(2, 512, 256),
            buf(512, 384),
            buf(512, 256),
            buf(4, 2, 4, 4, 16, 384, dtype=F32),
            buf(4, 2, 4, 4, 16, 256, dtype=F32),
        ]
        + [buf(k, n, 4, 16, w) for n, w in ((1, 640), (1, 384), (1, 384), (1, 384), (3, 256)) for k in (4, 3, 4, 3)]
        + [
            buf(4, 4, 16, 384, dtype=F32),
            buf(4, 4, 16, 256, dtype=F32),
            buf(16, 384),
            buf(16, 384),
            buf(272, 384, dtype=F32),
            buf(2, 4, 32, 256),
            buf(8, 32, 256),
            buf(8, 32, 256),
            buf(8, 16, 256),
            buf(8, 16, 256),
            buf(8, 8, 256, dtype=F32),
            buf(8, 8, 256, dtype=F32),
            buf(2, 8, PIECES, 256 // PIECES, 256),
            buf(8, 4, 4, 16, 512, dtype=F32),
            buf(8, 4, 16, 512, dtype=F32),
        ]
        + [buf(8, 4, 16, 512)] * 6
        + [buf(8, 16, 512)] * 6
        + [buf(8, 16, 512)] * 2
        + [
            dma(10), dma(SENDS), dma(8), dma(8), dma(2, 4), dma(2, 4, 4), dma(2, 4), dma(2), dma(5, 4), dma(5, 3), dma(), dma(8),
            dma(8), dma(8), dma(8), dma(8), dma(8, PIECES), dma(8, PIECES), dma(8, 3), dma(8, 3), dma(8),
        ],
        compiler_params=pltpu.CompilerParams(collective_id=0, has_side_effects=True, vmem_limit_bytes=56 * 2**20),
        name="mixer",
    )(
        tokens, norm_gain.reshape(1, -1), gate_proj, value_proj, state_proj, step_proj.T, conv_value, conv_state, mix_gain.reshape(1, -1),
        out_proj, step_bias, decay_rate, skip_gain, doc_lengths,
    )


def solution(mesh):
    return jax.shard_map(
        local,
        mesh=mesh,
        in_specs=(
            P("seq", "fsdp"), P(), P("seq", "fsdp"), P("seq", "fsdp"), P("seq", "fsdp"), P("seq", None, None),
            P(None, "fsdp"), P(), P("fsdp"), P("fsdp"), P("fsdp"), P("fsdp"), P("fsdp", "seq"), P(),
        ),
        out_specs=P("seq", "fsdp"),
        check_vma=False,
    )
```

```python
import jax
import jax.numpy as jnp
from jax import lax
from jax.experimental import pallas as pl
from jax.experimental.pallas import tpu as pltpu
from jax.sharding import PartitionSpec as P

N = 128
EPSILON = 1e-05
PRECISE = lax.Precision.HIGHEST
MESH = pl.DeviceIdType.MESH
F32 = jnp.float32
BF16 = jnp.bfloat16
WIDE = 640
STEP0 = 32
SQ = 40
SENDS = 400
PIECES = 4


def dot(a, b, precision=None):
    return jnp.dot(a, b, preferred_element_type=F32, precision=precision)


def body(
    tok_h, gain_h, gate_h, value_h, maps_h, step_h, conv_v_h, conv_s_h, mix_gain_h, out_w_h,
    bias, rate, skip, docs,
    out,
    tok, gain, gate_w, value_w, all_maps, step_w, conv_v, conv_s, mix_gain, out_w, maps_w,
    XI, X, WV, WG, SV, SG, PV, PG, S0L, S0S, R0L, R0S, S1L, S1S, R1L, R1S, S2L, S2S, R2L, R2S, S3L, S3S, R3L, R3S, S4L, S4S, R4L, R4S, RV, RG,
    HS, HR, EXT, BC, ST, SR, PB, SO, SI, SQB, NZ, GZ, T, Q, A1, B1, C1, RA1, RB1, RC1,
    A2, B2, C2, RA2, RB2, RC2, FO, FR,
    sem_load, sem_send, sem_i, sem_a, sem_y, sem_x, sem_s, sem_w, sem_l, sem_sh, sem_h, sem_bc, sem_st, sem_in, sem_sq,
    sem_p, sem_nz, sem_g, sem_gs, sem_1, sem_2, sem_f,
):
    s = lax.axis_index("seq")
    f = lax.axis_index("fsdp")
    z, c = lax.div(s, 2), lax.rem(s, 2)
    x, y = lax.div(f, 4), lax.rem(f, 4)
    sg = 1 - 2 * c

    def m4(v):
        return lax.rem(v + 8, 4)

    def m8(v):
        return lax.rem(v + 16, 8)

    def dev(z_=z, c_=c, x_=x, y_=y):
        return (2 * z_ + c_, 4 * x_ + y_)

    sibling = dev(c_=1 - c)
    peers = [(dc, dy) for dc in range(2) for dy in range(4) if (dc, dy) != (0, 0)]
    started = []

    def send(src, dst, sem, to):
        copy = pltpu.make_async_remote_copy(
            src_ref=src, dst_ref=dst, send_sem=sem_send.at[len(started)], recv_sem=sem,
            device_id=to, device_id_type=MESH,
        )
        copy.start()
        started.append((copy, None))

    def arrived(dst, sem):
        pltpu.make_async_remote_copy(
            src_ref=dst, dst_ref=dst, send_sem=sem_send.at[0], recv_sem=sem,
            device_id=sibling, device_id_type=MESH,
        ).wait_recv()

    def send_or_keep(own, src, dst, sem, to):
        copy = pltpu.make_async_remote_copy(
            src_ref=src, dst_ref=dst, send_sem=sem_send.at[len(started)], recv_sem=sem,
            device_id=to, device_id_type=MESH,
        )
        away = jnp.logical_not(own)

        @pl.when(away)
        def _():
            copy.start()

        @pl.when(own)
        def _():
            pltpu.make_async_copy(src, dst, sem).start()

        started.append((copy, away))

    def wrap_up():
        for copy, away in started:
            if away is None:
                copy.wait_send()
            else:

                @pl.when(away)
                def _(copy=copy):
                    copy.wait_send()

        assert len(started) <= SENDS

    barrier = pltpu.get_barrier_semaphore()
    own_leg = (lax.rem(f, 2) == c) & (lax.div(x, 2) == c)

    def greet(to):
        pl.semaphore_signal(barrier, inc=1, device_id=to, device_id_type=MESH)

    for o in (4, 3, 5, 2, 6, 1, 7):
        greet(dev(z_=m8(z + o)))
    for i in range(8):
        for to, at in (((2 * z + lax.rem(f, 2), 8 * c + i), 8 * c + i), ((2 * z + lax.div(x, 2), 2 * i + c), 2 * i + c)):

            @pl.when(jnp.logical_not(own_leg & (f == at)))
            def _(to=to):
                greet(to)

    for dc, dy in peers:
        greet(dev(c_=lax.rem(c + dc, 2), y_=m4(y + dy)))
    greet(dev(x_=m4(x + 1)))
    greet(dev(x_=m4(x - 1)))

    loads = [
        pltpu.make_async_copy(src, dst, sem_load.at[i])
        for i, (src, dst) in enumerate(
            (
                (tok_h, tok), (gain_h, gain), (value_h, value_w), (maps_h, all_maps), (step_h, step_w), (gate_h, gate_w),
                (conv_v_h, conv_v), (conv_s_h, conv_s), (mix_gain_h, mix_gain), (out_w_h, out_w),
            )
        )
    ]
    for load in loads:
        load.start()
    loads[0].wait()
    pl.semaphore_wait(barrier, 32 - 2 * own_leg.astype(jnp.int32))

    for i in range(8):
        send_or_keep(
            own_leg & (f == 8 * c + i),
            tok.at[pl.ds(16 * i, 16)], XI.at[lax.div(f, 2)], sem_i.at[lax.div(f, 2)],
            (2 * z + lax.rem(f, 2), 8 * c + i),
        )
    upper = lax.div(z, 4)
    lead, trail = x + upper * (y - x), y + upper * (x - y)
    for o in (4, 3, 5, 2, 6, 1, 7):
        to = m8(z + o)
        arrived(XI.at[to], sem_i.at[to])
        send(XI.at[to], X.at[c, upper, lead, trail, lax.rem(z, 4)], sem_a.at[z], dev(z_=to))
    arrived(XI.at[z], sem_i.at[z])
    pltpu.make_async_copy(XI.at[z], X.at[c, upper, lead, trail, lax.rem(z, 4)], sem_a.at[z]).start()

    loads[1].wait()

    gain_col = jnp.transpose(
        jnp.broadcast_to(gain[0:1, pl.ds(pl.multiple_of(512 * s, 512), 512)], (128, 512))
    )[:, 0:1]
    lane_w = lax.broadcasted_iota(jnp.int32, (512, 128), 1)
    turn = lax.rem(128 - 32 * y, 128)

    def rows_of(half, ref_v, ref_g):
        cols = pl.ds(pl.multiple_of(256 * half, 256), 256)
        ref_v[:, 0:256] = (value_w[:, cols].astype(F32) * gain_col).astype(BF16)
        maps = pltpu.roll(maps_w[:, pl.ds(pl.multiple_of(128 * half, 128), 128)].astype(F32), turn, 1)
        steps = pltpu.roll(step_w[...].astype(F32), lax.rem(8 - 4 * half, 8), 0)
        steps = jnp.concatenate([jnp.zeros((32, 512), F32), steps, jnp.zeros((88, 512), F32)], axis=0)
        extra = jnp.where(lane_w < 32, maps, 0.0) + jnp.transpose(steps)
        ref_v[:, 256:384] = (extra * gain_col).astype(BF16)
        ref_g[...] = (gate_w[:, cols].astype(F32) * gain_col).astype(BF16)

    for load in loads[2:]:
        load.wait()
    for k in range(4):

        @pl.when(x == k)
        def _(k=k):
            maps_w[...] = all_maps[:, k, :]

    rows_of(1 - c, SV, SG)
    send(SV, WV.at[c], sem_w.at[0], sibling)
    send(SG, WG.at[c], sem_w.at[1], sibling)
    rows_of(c, WV.at[c], WG.at[c])

    lane8 = lax.broadcasted_iota(jnp.int32, (8, 128), 1)
    starts = jnp.full((8, 128), 1 << 20, jnp.int32)
    total = jnp.int32(0)
    for i in range(32):
        starts = jnp.where(lane8 == i, total, starts)
        total = total + docs[i]
    starts = starts.astype(F32)[0:1]
    first = (256 * z).astype(F32)
    t_wide = first + lax.broadcasted_iota(jnp.int32, (256, 128), 0).astype(F32)
    start_of = jnp.max(jnp.where(starts <= t_wide, starts, 0.0), axis=1, keepdims=True)
    t_col = t_wide[:, 0:1]
    into = t_col - start_of
    bias_row = jnp.zeros((8, 128), F32)
    rate_row = jnp.zeros((8, 128), F32)
    lane_256 = lax.broadcasted_iota(jnp.int32, (8, 256), 1)
    skip_row = jnp.zeros((8, 256), F32)
    for i in range(4):
        bias_row = jnp.where(lane8 == STEP0 + i, bias[4 * c + i], bias_row)
        rate_row = jnp.where(lane8 == STEP0 + i, rate[4 * c + i], rate_row)
        skip_row = jnp.where(lax.div(lane_256, 64) == i, skip[4 * c + i], skip_row)
    bias_row, rate_row, skip_row = bias_row[0:1], rate_row[0:1], skip_row[0:1]

    def at_x(q):
        return dev(x_=q)

    def at_y(q):
        return dev(y_=q)

    legs = [(x, at_x, y, at_y), (y, at_y, x, at_x)]
    def spread(h, q):
        a, to, _, _ = legs[h]
        mine = X.at[c, h, a, q]
        send(mine, mine, sem_x.at[h, a, q], to(m4(a + 1)))
        send(mine, mine, sem_x.at[h, a, q], to(m4(a - 1)))

    def relay(h, q):
        a, to, _, _ = legs[h]
        near = m4(a - sg)
        got = X.at[c, h, near, q]
        arrived(got, sem_x.at[h, near, q])
        send(got, got, sem_x.at[h, near, q], to(m4(a + sg)))

    def trailing(h, q):
        arrived(X.at[c, h, legs[h][0], q], sem_y.at[h, q])

    for h, (a, _, b, to) in enumerate(legs):
        for zt in range(4):
            arrived(X.at[c, h, a, b, zt], sem_a.at[4 * h + zt])
        mine = X.at[c, h, a, b]
        send(mine, mine, sem_y.at[h, b], to(m4(b + 1)))
        send(mine, mine, sem_y.at[h, b], to(m4(b - 1)))
        spread(h, b)
    for h, (a, _, b, to) in enumerate(legs):
        near = X.at[c, h, a, m4(b - sg)]
        trailing(h, m4(b - sg))
        send(near, near, sem_y.at[h, m4(b - sg)], to(m4(b + sg)))
        spread(h, m4(b - sg))
        trailing(h, m4(b + sg))
        spread(h, m4(b + sg))
    for h, (_, _, b, _) in enumerate(legs):
        relay(h, b)
    for h, (a, _, b, _) in enumerate(legs):
        trailing(h, m4(b + 2))
        spread(h, m4(b + 2))
        send(X.at[c, h, a], X.at[c, h, a], sem_s.at[h, a], sibling)
    arrived(WV.at[1 - c], sem_w.at[0])
    arrived(WG.at[1 - c], sem_w.at[1])

    lane_e = lax.broadcasted_iota(jnp.int32, (256, 128), 1)
    groups = [[a, m4(a - sg), m4(a + sg), m4(a + 2)] for a, _, _, _ in legs]

    def came(j):
        for h, (_, _, b, _) in enumerate(legs):
            q = groups[h][j]
            for at in range(4):
                if j > 1:
                    arrived(X.at[c, h, q, at], sem_x.at[h, q, at])
            send(X.at[c, h, q], X.at[c, h, q], sem_s.at[h, q], sibling)

    def product(g):
        for h in range(2):
            arrived(X.at[1 - c, h, groups[h][g]], sem_s.at[h, groups[h][g]])
            a = X[0, h, groups[h][g]].reshape(256, 512)
            b = X[1, h, groups[h][g]].reshape(256, 512)
            p = dot(a, WV[0]) + dot(b, WV[1])
            PG[g, h] = (dot(a, WG[0]) + dot(b, WG[1])).reshape(4, 4, 16, 256)
            a, b = a.astype(F32), b.astype(F32)
            squares = jnp.sum(a * a + b * b, axis=1, keepdims=True)
            PV[g, h, :, :, :, 0:256] = p[:, 0:256].reshape(4, 4, 16, 256)
            PV[g, h, :, :, :, 256:384] = (p[:, 256:384] + jnp.where(lane_e == SQ, squares, 0.0)).reshape(4, 4, 16, 128)

    rings = [
        (0, 1, "all", S0L, S0S, R0L, R0S),
        (1, 1, "values", S1L, S1S, R1L, R1S),
        (2, 1, "values", S2L, S2S, R2L, R2S),
        (3, 1, "values", S3L, S3S, R3L, R3S),
        (1, 3, "gate", S4L, S4S, R4L, R4S),
    ]

    def pieces(r, d):
        g, n, kind = rings[r][:3]
        d_up, d_at = lax.div(d, 4), lax.rem(d, 4)
        got = []
        if kind != "gate":
            got.append((0, 384, PV[pl.ds(g, n), d_up, :, d_at]))
        if kind != "values":
            got.append((got[0][1] if got else 0, 256, PG[pl.ds(g, n), d_up, :, d_at]))
        return got

    def hop(r, k):
        out_l, out_s, in_l, in_s = rings[r][3:]
        if k:
            arrived(in_l.at[k - 1], sem_l.at[r, k - 1])
        for lo, wide, v in pieces(r, m8(z + (4 - k) * sg)):
            if k:
                v = v + in_l[k - 1, :, :, :, lo : lo + wide].astype(F32)
            out_l[k, :, :, :, lo : lo + wide] = v.astype(BF16)
        send(out_l.at[k], in_l.at[k], sem_l.at[r, k], dev(z_=m8(z + sg)))
        if k < 3:
            if k:
                arrived(in_s.at[k - 1], sem_sh.at[r, k - 1])
            for lo, wide, v in pieces(r, m8(z - (3 - k) * sg)):
                if k:
                    v = v + in_s[k - 1, :, :, :, lo : lo + wide].astype(F32)
                out_s[k, :, :, :, lo : lo + wide] = v.astype(BF16)
            send(out_s.at[k], in_s.at[k], sem_sh.at[r, k], dev(z_=m8(z - sg)))

    def last(r):
        g, n, kind, _, _, in_l, in_s = rings[r]
        arrived(in_l.at[3], sem_l.at[r, 3])
        arrived(in_s.at[2], sem_sh.at[r, 2])
        for lo, wide, v in pieces(r, z):
            v = v + in_l[3, :, :, :, lo : lo + wide].astype(F32) + in_s[2, :, :, :, lo : lo + wide].astype(F32)
            ref = RV if wide == 384 else RG
            for j in range(n):
                a = groups[0][g + j] + upper * (groups[1][g + j] - groups[0][g + j])
                for i in range(4):
                    ref[a + upper * (i - a), i + upper * (a - i)] = v[j, i]

    product(0)
    hop(0, 0)
    for at in (-1, 1):
        for h in range(2):
            relay(h, m4(legs[h][2] + at * sg))
    hop(0, 1)
    for h in range(2):
        relay(h, m4(legs[h][2] + 2))
    came(1)
    came(2)
    product(1)
    hop(1, 0)
    product(2)
    hop(2, 0)
    hop(0, 2)
    hop(1, 1)
    hop(2, 1)
    hop(0, 3)
    came(3)
    product(3)
    hop(3, 0)
    hop(1, 2)
    hop(2, 2)
    hop(3, 1)
    hop(1, 3)
    hop(2, 3)
    hop(3, 2)
    last(0)
    last(1)
    hop(3, 3)
    last(2)
    hop(4, 0)
    last(3)

    scale = lax.rsqrt(RV[:, :, :, 256:384].reshape(256, 128)[:, SQ : SQ + 1] * (1.0 / 8192) + EPSILON)
    HS[...] = (RV[3, 3] * scale[240:256]).astype(BF16)
    send(HS, HR, sem_h, dev(z_=m8(z + 1)))
    raw = (RV[...].reshape(256, 384) * scale).astype(BF16)
    EXT[16:272] = raw.astype(F32)

    raw_step = RV[:, :, :, 256:384].reshape(256, 128) * scale + bias_row
    step = jnp.maximum(raw_step, 0.0) + jnp.log1p(jnp.exp(-jnp.abs(raw_step)))
    log_decay = -rate_row * step
    order_r = lax.broadcasted_iota(jnp.int32, (256, 256), 0)
    order_c = lax.broadcasted_iota(jnp.int32, (256, 256), 1)
    cum = dot((order_r >= order_c).astype(F32), log_decay, PRECISE)
    cum_rows = jnp.transpose(cum)
    end = cum[255:256]
    causal = (order_r >= order_c) & (first + order_c.astype(F32) >= start_of)
    start_last = start_of[255:256]
    low = lax.broadcasted_iota(jnp.int32, (1, 128), 1) < 64

    def expand(a):
        return jnp.concatenate(
            [
                jnp.where(low, a[:, STEP0 + 2 * i : STEP0 + 2 * i + 1], a[:, STEP0 + 2 * i + 1 : STEP0 + 2 * i + 2])
                for i in range(2)
            ],
            axis=1,
        )

    step_wide = expand(step)
    tail = expand(jnp.where(t_col >= start_last, jnp.exp(end - cum), 0.0))
    carried = expand(jnp.where(start_of < first, jnp.exp(cum), 0.0))
    PB[z] = jnp.broadcast_to(expand(jnp.where(start_last < first, jnp.exp(end), 0.0)), (8, 256))
    for o in range(1, 8):
        send(PB.at[z], PB.at[z], sem_p.at[z], dev(z_=m8(z + o)))

    arrived(HR, sem_h)
    EXT[0:16] = HR[...].astype(F32)
    hop(4, 1)

    def conv(lo, width, taps):
        acc = jnp.zeros((256, width), F32)
        for k in range(4):
            acc = acc + jnp.where(into >= 3 - k, EXT[13 + k : 269 + k, lo : lo + width], 0.0) * taps[k]
        return acc * jax.nn.sigmoid(acc)

    maps_cols = pl.ds(pl.multiple_of(128 * c, 128), 128)
    group_row = lax.broadcasted_iota(jnp.int32, (4, 128), 0) == x
    taps_s = [
        pltpu.roll(
            jnp.broadcast_to(
                jnp.sum(jnp.where(group_row, conv_s[k, :, maps_cols], 0.0), axis=0, keepdims=True), (8, 128)
            ),
            turn,
            1,
        )[0:1]
        for k in range(4)
    ]
    maps = jnp.transpose(conv(256, 128, taps_s))[0:32].astype(BF16)
    BC[c, y] = maps
    for dc, dy in peers:
        to_c = lax.rem(c + dc, 2)
        send(BC.at[c, y], BC.at[c, y], sem_bc.at[4 * c + y], dev(c_=to_c, y_=m4(y + dy)))

    own_cols = pl.ds(pl.multiple_of(256 * c, 256), 256)
    inputs = conv(0, 256, [conv_v[k : k + 1, own_cols] for k in range(4)]).astype(BF16).astype(F32)
    stepped = inputs * step_wide
    to_end = (stepped * tail).astype(BF16)
    stepped = stepped.astype(BF16)

    for dc, dy in peers:
        pc, py = lax.rem(c + dc, 2), m4(y + dy)
        arrived(BC.at[pc, py], sem_bc.at[4 * pc + py])
    hop(4, 2)
    b_rows = BC[0].reshape(128, 256)
    c_cols = jnp.transpose(BC[1].reshape(128, 256).astype(F32)).astype(BF16)

    state = dot(b_rows, to_end).astype(BF16)
    ST[...] = state.reshape(8, 16, 256)
    for o in range(1, 8):
        k = m8(z + o)
        send(ST.at[k], SR.at[z], sem_st.at[z], dev(z_=k))
    SR[z] = ST[z]

    scores = dot(c_cols, b_rows)
    parts = []
    for i in range(4):
        gaps = cum[:, STEP0 + i : STEP0 + i + 1] - cum_rows[STEP0 + i : STEP0 + i + 1, :]
        mixing = (jnp.exp(jnp.where(causal, gaps, -1e30)) * scores).astype(BF16)
        parts.append(dot(mixing, stepped[:, 128 * (i // 2) : 128 * (i // 2) + 128]))
    intra = jnp.concatenate([jnp.where(low, parts[0], parts[1]), jnp.where(low, parts[2], parts[3])], axis=1)
    partly = intra + skip_row * inputs
    hop(4, 3)

    for o in range(1, 8):
        k = m8(z + o)
        arrived(SR.at[k], sem_st.at[k])
        arrived(PB.at[k], sem_p.at[k])
    incoming = jnp.zeros((16, 256), F32)
    for i in range(8):
        SO[i] = incoming.astype(BF16)
        incoming = PB[i, 0:1] * incoming + SR[i].astype(F32)
    for o in range(1, 8):
        k = m8(z + o)
        send(SO.at[k], SI.at[z], sem_in.at[z], dev(z_=k))
    SI[z] = SO[z]
    last(4)
    gate = RG[...].reshape(256, 256) * scale
    gate = gate * jax.nn.sigmoid(gate)
    partly = partly * gate
    carried = carried * gate
    for o in range(1, 8):
        k = m8(z + o)
        arrived(SI.at[k], sem_in.at[k])
    gated = partly + dot(c_cols, SI[...].reshape(128, 256)) * carried
    GZ[c, z] = (gated * mix_gain[0:1, own_cols]).astype(BF16).reshape(PIECES, 256 // PIECES, 256)

    order = [z]
    for k in range(1, 4):
        order += [m8(z - k * sg), m8(z + k * sg)]
    order.append(m8(z + 4))
    for i in range(PIECES):
        block = GZ.at[c, z, i]
        send(block, block, sem_g.at[z, i], dev(z_=m8(z + sg)))
        send(block, block, sem_g.at[z, i], dev(z_=m8(z - sg)))
        send(block, block, sem_gs.at[z, i], sibling)

    own_sq = 2 * y + c
    SQB[own_sq] = lax.dot_general(
        jnp.ones((8, 256), F32), gated * gated, (((1,), (1,)), ((), ())), preferred_element_type=F32, precision=PRECISE
    )
    for dc, dy in peers:
        send(SQB.at[own_sq], SQB.at[own_sq], sem_sq.at[own_sq], dev(c_=lax.rem(c + dc, 2), y_=m4(y + dy)))
    def pass_on(o, i):
        zt = order[o]
        got = GZ.at[c, zt, i]
        arrived(got, sem_g.at[zt, i])
        if o in (1, 3, 5):
            send(got, got, sem_g.at[zt, i], dev(z_=m8(z + sg)))
        if o in (2, 4):
            send(got, got, sem_g.at[zt, i], dev(z_=m8(z - sg)))
        send(got, got, sem_gs.at[zt, i], sibling)

    def forward(o):
        for i in range(PIECES):
            pass_on(o, i)
            if o < 7:
                pass_on(o + 1, i)

    def take(o):
        zt = order[o]
        for i in range(PIECES):
            arrived(GZ.at[1 - c, zt, i], sem_gs.at[zt, i])
        if o:
            arrived(NZ.at[zt], sem_nz.at[zt])
        norm = jnp.transpose(jnp.concatenate([NZ[zt]] * 16, axis=0))[:, 0:1]
        T[o] = ((dot(GZ[0, zt].reshape(256, 256), out_w[0:256]) + dot(GZ[1, zt].reshape(256, 256), out_w[256:512])) * norm).reshape(4, 4, 16, 512)

    def along(o, level):
        over_x = (o % 2 == 0) == (level == 1)
        p = x if over_x else y

        def to(q):
            return dev(x_=q) if over_x else dev(y_=q)

        return p, to

    def quarter(o, q):
        return T[o, q] if o % 2 == 0 else T[o, :, q]

    straight = (6, 7)

    def first_out(o):
        p, to = along(o, 1)
        A1[o] = quarter(o, m4(p + 2)).astype(BF16)
        send(A1.at[o], RA1.at[o], sem_1.at[o, 0], to(m4(p + 2) if o in straight else m4(p + sg)))
        B1[o] = quarter(o, m4(p - sg)).astype(BF16)
        send(B1.at[o], RB1.at[o], sem_1.at[o, 1], to(m4(p - sg)))
        if o in straight:
            C1[o] = quarter(o, m4(p + sg)).astype(BF16)
            send(C1.at[o], RC1.at[o], sem_1.at[o, 2], to(m4(p + sg)))

    def first_relay(o):
        p, to = along(o, 1)
        arrived(RA1.at[o], sem_1.at[o, 0])
        C1[o] = (quarter(o, m4(p + sg)) + RA1[o].astype(F32)).astype(BF16)
        send(C1.at[o], RC1.at[o], sem_1.at[o, 2], to(m4(p + sg)))

    def second_out(o):
        p, _ = along(o, 1)
        arrived(RB1.at[o], sem_1.at[o, 1])
        arrived(RC1.at[o], sem_1.at[o, 2])
        summed = quarter(o, p) + RB1[o].astype(F32) + RC1[o].astype(F32)
        if o in straight:
            arrived(RA1.at[o], sem_1.at[o, 0])
            summed = summed + RA1[o].astype(F32)
        Q[o] = summed
        p, to = along(o, 2)
        for i, (out_b, in_b, q) in enumerate(((A2, RA2, m4(p + 2)), (B2, RB2, m4(p - sg)), (C2, RC2, m4(p + sg)))):
            out_b[o] = Q[o, q].astype(BF16)
            send(out_b.at[o], in_b.at[o], sem_2.at[o, i], to(q))

    block_at = f
    row_block = lax.rem(block_at, 8)
    to_core = lax.div(block_at, 8)

    def finish(o):
        p, _ = along(o, 2)
        for i, in_b in enumerate((RA2, RB2, RC2)):
            arrived(in_b.at[o], sem_2.at[o, i])
        FO[o] = (Q[o, p] + RA2[o].astype(F32) + RB2[o].astype(F32) + RC2[o].astype(F32)).astype(BF16)
        to = (2 * order[o] + to_core, s)
        own = (to[0] == s) & (s == f) if o == 0 else None
        if own is None:
            send(FO.at[o], FR.at[row_block], sem_f.at[row_block], to)
        else:
            send_or_keep(own, FO.at[o], FR.at[row_block], sem_f.at[row_block], to)

    forward(1)
    for dc, dy in peers:
        k = 2 * m4(y + dy) + lax.rem(c + dc, 2)
        arrived(SQB.at[k], sem_sq.at[k])
    NZ[z] = lax.rsqrt(jnp.sum(SQB[...], axis=0) * (1.0 / 2048) + EPSILON)
    for o in range(1, 8):
        send(NZ.at[z], NZ.at[z], sem_nz.at[z], dev(z_=m8(z + o)))
    take(0)
    first_out(0)
    forward(3)
    for o in (1, 2):
        take(o)
        first_out(o)
    first_relay(0)
    forward(5)
    for o in (3, 4):
        take(o)
        first_out(o)
    first_relay(1)
    first_relay(2)
    second_out(0)
    forward(7)
    for o in (5, 6):
        take(o)
        first_out(o)
    first_relay(3)
    first_relay(4)
    take(7)
    first_out(7)
    second_out(1)
    second_out(2)
    first_relay(5)
    second_out(3)
    second_out(4)
    for o in range(3):
        finish(o)
    second_out(6)
    second_out(5)
    second_out(7)
    for o in (3, 4, 6, 5, 7):
        finish(o)

    for i in range(8):
        arrived(FR.at[i], sem_f.at[i])
    out[...] = (tok[...].astype(F32) + FR[...].reshape(128, 512).astype(F32)).astype(BF16)

    wrap_up()


def local(
    tokens, norm_gain, gate_proj, value_proj, step_proj, state_proj, conv_value, conv_state, step_bias, decay_rate,
    skip_gain, mix_gain, out_proj, doc_lengths,
):
    vmem = pl.BlockSpec(memory_space=pltpu.VMEM)
    smem = pl.BlockSpec(memory_space=pltpu.SMEM)

    def buf(*shape, dtype=BF16):
        return pltpu.VMEM(shape, dtype)

    def dma(*shape):
        return pltpu.SemaphoreType.DMA(shape)

    return pl.pallas_call(
        body,
        out_shape=jax.ShapeDtypeStruct((128, 512), BF16),
        in_specs=[pl.BlockSpec(memory_space=pl.ANY)] * 10 + [smem] * 4,
        out_specs=vmem,
        scratch_shapes=[
            buf(128, 512),
            buf(1, 8192, dtype=F32),
            buf(512, 512),
            buf(512, 512),
            buf(512, 4, 256),
            buf(8, 512),
            buf(4, 512, dtype=F32),
            buf(4, 4, 256, dtype=F32),
            buf(1, 512, dtype=F32),
            buf(512, 512),
            buf(512, 256),
            buf(8, 16, 512),
            buf(2, 2, 4, 4, 4, 16, 512),
            buf(2, 512, 384),
            buf(2, 512, 256),
            buf(512, 384),
            buf(512, 256),
            buf(4, 2, 4, 4, 16, 384, dtype=F32),
            buf(4, 2, 4, 4, 16, 256, dtype=F32),
        ]
        + [buf(k, n, 4, 16, w) for n, w in ((1, 640), (1, 384), (1, 384), (1, 384), (3, 256)) for k in (4, 3, 4, 3)]
        + [
            buf(4, 4, 16, 384, dtype=F32),
            buf(4, 4, 16, 256, dtype=F32),
            buf(16, 384),
            buf(16, 384),
            buf(272, 384, dtype=F32),
            buf(2, 4, 32, 256),
            buf(8, 16, 256),
            buf(8, 16, 256),
            buf(8, 8, 256, dtype=F32),
            buf(8, 16, 256),
            buf(8, 16, 256),
            buf(8, 8, 256, dtype=F32),
            buf(8, 8, 256, dtype=F32),
            buf(2, 8, PIECES, 256 // PIECES, 256),
            buf(8, 4, 4, 16, 512, dtype=F32),
            buf(8, 4, 16, 512, dtype=F32),
        ]
        + [buf(8, 4, 16, 512)] * 6
        + [buf(8, 16, 512)] * 6
        + [buf(8, 16, 512)] * 2
        + [
            dma(10), dma(SENDS), dma(8), dma(8), dma(2, 4), dma(2, 4, 4), dma(2, 4), dma(2), dma(5, 4), dma(5, 3), dma(), dma(8),
            dma(8), dma(8), dma(8), dma(8), dma(8), dma(8, PIECES), dma(8, PIECES), dma(8, 3), dma(8, 3), dma(8),
        ],
        compiler_params=pltpu.CompilerParams(collective_id=0, has_side_effects=True, vmem_limit_bytes=56 * 2**20),
        name="mixer",
    )(
        tokens, norm_gain.reshape(1, -1), gate_proj, value_proj, state_proj, step_proj.T, conv_value, conv_state, mix_gain.reshape(1, -1),
        out_proj, step_bias, decay_rate, skip_gain, doc_lengths,
    )


def solution(mesh):
    return jax.shard_map(
        local,
        mesh=mesh,
        in_specs=(
            P("seq", "fsdp"), P(), P("seq", "fsdp"), P("seq", "fsdp"), P("seq", "fsdp"), P("seq", None, None),
            P(None, "fsdp"), P(), P("fsdp"), P("fsdp"), P("fsdp"), P("fsdp"), P("fsdp", "seq"), P(),
        ),
        out_specs=P("seq", "fsdp"),
        check_vma=False,
    )
```

```python
import jax
import jax.numpy as jnp
from jax import lax
from jax.experimental import pallas as pl
from jax.experimental.pallas import tpu as pltpu
from jax.sharding import PartitionSpec as P

N = 128
EPSILON = 1e-05
PRECISE = lax.Precision.HIGHEST
MESH = pl.DeviceIdType.MESH
F32 = jnp.float32
BF16 = jnp.bfloat16
WIDE = 640
STEP0 = 32
SQ = 40
SENDS = 400
PIECES = 4


def dot(a, b, precision=None):
    return jnp.dot(a, b, preferred_element_type=F32, precision=precision)


def body(
    tok_h, gain_h, gate_h, value_h, maps_h, step_h, conv_v_h, conv_s_h, mix_gain_h, out_w_h,
    bias, rate, skip, docs,
    out,
    tok, gain, gate_w, value_w, all_maps, step_w, conv_v, conv_s, mix_gain, out_w, maps_w,
    XI, X, WV, WG, SV, SG, PV, PG, S0L, S0S, R0L, R0S, S1L, S1S, R1L, R1S, S2L, S2S, R2L, R2S, S3L, S3S, R3L, R3S, S4L, S4S, R4L, R4S, RV, RG,
    HS, HR, EXT, BC, BP, ST, SR, PB, SO, SI, SQB, NZ, GZ, T, Q, A1, B1, C1, RA1, RB1, RC1,
    A2, B2, C2, RA2, RB2, RC2, FO, FR,
    sem_load, sem_send, sem_i, sem_a, sem_y, sem_x, sem_s, sem_w, sem_l, sem_sh, sem_h, sem_bc, sem_st, sem_in, sem_sq,
    sem_p, sem_bp, sem_nz, sem_g, sem_gs, sem_1, sem_2, sem_f,
):
    s = lax.axis_index("seq")
    f = lax.axis_index("fsdp")
    z, c = lax.div(s, 2), lax.rem(s, 2)
    x, y = lax.div(f, 4), lax.rem(f, 4)
    sg = 1 - 2 * c

    def m4(v):
        return lax.rem(v + 8, 4)

    def m8(v):
        return lax.rem(v + 16, 8)

    def dev(z_=z, c_=c, x_=x, y_=y):
        return (2 * z_ + c_, 4 * x_ + y_)

    sibling = dev(c_=1 - c)
    peers = [(dc, dy) for dc in range(2) for dy in range(4) if (dc, dy) != (0, 0)]
    started = []

    def send(src, dst, sem, to):
        copy = pltpu.make_async_remote_copy(
            src_ref=src, dst_ref=dst, send_sem=sem_send.at[len(started)], recv_sem=sem,
            device_id=to, device_id_type=MESH,
        )
        copy.start()
        started.append((copy, None))

    def arrived(dst, sem):
        pltpu.make_async_remote_copy(
            src_ref=dst, dst_ref=dst, send_sem=sem_send.at[0], recv_sem=sem,
            device_id=sibling, device_id_type=MESH,
        ).wait_recv()

    def send_or_keep(own, src, dst, sem, to):
        copy = pltpu.make_async_remote_copy(
            src_ref=src, dst_ref=dst, send_sem=sem_send.at[len(started)], recv_sem=sem,
            device_id=to, device_id_type=MESH,
        )
        away = jnp.logical_not(own)

        @pl.when(away)
        def _():
            copy.start()

        @pl.when(own)
        def _():
            pltpu.make_async_copy(src, dst, sem).start()

        started.append((copy, away))

    def wrap_up():
        for copy, away in started:
            if away is None:
                copy.wait_send()
            else:

                @pl.when(away)
                def _(copy=copy):
                    copy.wait_send()

        assert len(started) <= SENDS

    barrier = pltpu.get_barrier_semaphore()
    own_leg = (lax.rem(f, 2) == c) & (lax.div(x, 2) == c)

    def greet(to):
        pl.semaphore_signal(barrier, inc=1, device_id=to, device_id_type=MESH)

    for o in (4, 3, 5, 2, 6, 1, 7):
        greet(dev(z_=m8(z + o)))
    for i in range(8):
        for to, at in (((2 * z + lax.rem(f, 2), 8 * c + i), 8 * c + i), ((2 * z + lax.div(x, 2), 2 * i + c), 2 * i + c)):

            @pl.when(jnp.logical_not(own_leg & (f == at)))
            def _(to=to):
                greet(to)

    for dc, dy in peers:
        greet(dev(c_=lax.rem(c + dc, 2), y_=m4(y + dy)))
    greet(dev(x_=m4(x + 1)))
    greet(dev(x_=m4(x - 1)))

    loads = [
        pltpu.make_async_copy(src, dst, sem_load.at[i])
        for i, (src, dst) in enumerate(
            (
                (tok_h, tok), (gain_h, gain), (value_h, value_w), (maps_h, all_maps), (step_h, step_w), (gate_h, gate_w),
                (conv_v_h, conv_v), (conv_s_h, conv_s), (mix_gain_h, mix_gain), (out_w_h, out_w),
            )
        )
    ]
    for load in loads:
        load.start()
    loads[0].wait()
    pl.semaphore_wait(barrier, 32 - 2 * own_leg.astype(jnp.int32))

    for i in range(8):
        send_or_keep(
            own_leg & (f == 8 * c + i),
            tok.at[pl.ds(16 * i, 16)], XI.at[lax.div(f, 2)], sem_i.at[lax.div(f, 2)],
            (2 * z + lax.rem(f, 2), 8 * c + i),
        )
    upper = lax.div(z, 4)
    lead, trail = x + upper * (y - x), y + upper * (x - y)
    for o in (4, 3, 5, 2, 6, 1, 7):
        to = m8(z + o)
        arrived(XI.at[to], sem_i.at[to])
        send(XI.at[to], X.at[c, upper, lead, trail, lax.rem(z, 4)], sem_a.at[z], dev(z_=to))
    arrived(XI.at[z], sem_i.at[z])
    pltpu.make_async_copy(XI.at[z], X.at[c, upper, lead, trail, lax.rem(z, 4)], sem_a.at[z]).start()

    loads[1].wait()

    gain_col = jnp.transpose(
        jnp.broadcast_to(gain[0:1, pl.ds(pl.multiple_of(512 * s, 512), 512)], (128, 512))
    )[:, 0:1]
    lane_w = lax.broadcasted_iota(jnp.int32, (512, 128), 1)
    turn = lax.rem(128 - 32 * y, 128)

    def rows_of(half, ref_v, ref_g):
        cols = pl.ds(pl.multiple_of(256 * half, 256), 256)
        ref_v[:, 0:256] = (value_w[:, cols].astype(F32) * gain_col).astype(BF16)
        maps = pltpu.roll(maps_w[:, pl.ds(pl.multiple_of(128 * half, 128), 128)].astype(F32), turn, 1)
        steps = pltpu.roll(step_w[...].astype(F32), lax.rem(8 - 4 * half, 8), 0)
        steps = jnp.concatenate([jnp.zeros((32, 512), F32), steps, jnp.zeros((88, 512), F32)], axis=0)
        extra = jnp.where(lane_w < 32, maps, 0.0) + jnp.transpose(steps)
        ref_v[:, 256:384] = (extra * gain_col).astype(BF16)
        ref_g[...] = (gate_w[:, cols].astype(F32) * gain_col).astype(BF16)

    for load in loads[2:]:
        load.wait()
    for k in range(4):

        @pl.when(x == k)
        def _(k=k):
            maps_w[...] = all_maps[:, k, :]

    rows_of(1 - c, SV, SG)
    send(SV, WV.at[c], sem_w.at[0], sibling)
    send(SG, WG.at[c], sem_w.at[1], sibling)
    rows_of(c, WV.at[c], WG.at[c])

    lane8 = lax.broadcasted_iota(jnp.int32, (8, 128), 1)
    starts = jnp.full((8, 128), 1 << 20, jnp.int32)
    total = jnp.int32(0)
    for i in range(32):
        starts = jnp.where(lane8 == i, total, starts)
        total = total + docs[i]
    starts = starts.astype(F32)[0:1]
    first = (256 * z).astype(F32)
    t_wide = first + lax.broadcasted_iota(jnp.int32, (256, 128), 0).astype(F32)
    start_of = jnp.max(jnp.where(starts <= t_wide, starts, 0.0), axis=1, keepdims=True)
    t_col = t_wide[:, 0:1]
    into = t_col - start_of
    into_row = jnp.transpose(jnp.broadcast_to(into, (256, 128)))[0:1]
    group_row = lax.broadcasted_iota(jnp.int32, (4, 256), 0) == x
    tap_row = lax.broadcasted_iota(jnp.int32, (128, 256), 0)
    map_taps = jnp.zeros((128, 256), F32)
    for k in range(4):
        own_taps = jnp.sum(jnp.where(group_row, conv_s[k], 0.0), axis=0, keepdims=True)
        map_taps = jnp.where(tap_row == k, own_taps, map_taps)
    map_taps = jnp.transpose(map_taps)
    bias_row = jnp.zeros((8, 128), F32)
    rate_row = jnp.zeros((8, 128), F32)
    lane_256 = lax.broadcasted_iota(jnp.int32, (8, 256), 1)
    skip_row = jnp.zeros((8, 256), F32)
    for i in range(4):
        bias_row = jnp.where(lane8 == STEP0 + i, bias[4 * c + i], bias_row)
        rate_row = jnp.where(lane8 == STEP0 + i, rate[4 * c + i], rate_row)
        skip_row = jnp.where(lax.div(lane_256, 64) == i, skip[4 * c + i], skip_row)
    bias_row, rate_row, skip_row = bias_row[0:1], rate_row[0:1], skip_row[0:1]

    def at_x(q):
        return dev(x_=q)

    def at_y(q):
        return dev(y_=q)

    legs = [(x, at_x, y, at_y), (y, at_y, x, at_x)]
    def spread(h, q):
        a, to, _, _ = legs[h]
        mine = X.at[c, h, a, q]
        send(mine, mine, sem_x.at[h, a, q], to(m4(a + 1)))
        send(mine, mine, sem_x.at[h, a, q], to(m4(a - 1)))

    def relay(h, q):
        a, to, _, _ = legs[h]
        near = m4(a - sg)
        got = X.at[c, h, near, q]
        arrived(got, sem_x.at[h, near, q])
        send(got, got, sem_x.at[h, near, q], to(m4(a + sg)))

    def trailing(h, q):
        arrived(X.at[c, h, legs[h][0], q], sem_y.at[h, q])

    for h, (a, _, b, to) in enumerate(legs):
        for zt in range(4):
            arrived(X.at[c, h, a, b, zt], sem_a.at[4 * h + zt])
        mine = X.at[c, h, a, b]
        send(mine, mine, sem_y.at[h, b], to(m4(b + 1)))
        send(mine, mine, sem_y.at[h, b], to(m4(b - 1)))
        spread(h, b)
    for h, (a, _, b, to) in enumerate(legs):
        near = X.at[c, h, a, m4(b - sg)]
        trailing(h, m4(b - sg))
        send(near, near, sem_y.at[h, m4(b - sg)], to(m4(b + sg)))
        spread(h, m4(b - sg))
        trailing(h, m4(b + sg))
        spread(h, m4(b + sg))
    for h, (_, _, b, _) in enumerate(legs):
        relay(h, b)
    for h, (a, _, b, _) in enumerate(legs):
        trailing(h, m4(b + 2))
        spread(h, m4(b + 2))
        send(X.at[c, h, a], X.at[c, h, a], sem_s.at[h, a], sibling)
    arrived(WV.at[1 - c], sem_w.at[0])
    arrived(WG.at[1 - c], sem_w.at[1])

    lane_e = lax.broadcasted_iota(jnp.int32, (256, 128), 1)
    groups = [[a, m4(a - sg), m4(a + sg), m4(a + 2)] for a, _, _, _ in legs]

    def came(j):
        for h, (_, _, b, _) in enumerate(legs):
            q = groups[h][j]
            for at in range(4):
                if j > 1:
                    arrived(X.at[c, h, q, at], sem_x.at[h, q, at])
            send(X.at[c, h, q], X.at[c, h, q], sem_s.at[h, q], sibling)

    def product(g):
        for h in range(2):
            arrived(X.at[1 - c, h, groups[h][g]], sem_s.at[h, groups[h][g]])
            a = X[0, h, groups[h][g]].reshape(256, 512)
            b = X[1, h, groups[h][g]].reshape(256, 512)
            p = dot(a, WV[0]) + dot(b, WV[1])
            PG[g, h] = (dot(a, WG[0]) + dot(b, WG[1])).reshape(4, 4, 16, 256)
            a, b = a.astype(F32), b.astype(F32)
            squares = jnp.sum(a * a + b * b, axis=1, keepdims=True)
            PV[g, h, :, :, :, 0:256] = p[:, 0:256].reshape(4, 4, 16, 256)
            PV[g, h, :, :, :, 256:384] = (p[:, 256:384] + jnp.where(lane_e == SQ, squares, 0.0)).reshape(4, 4, 16, 128)

    rings = [
        (0, 1, "all", S0L, S0S, R0L, R0S),
        (1, 1, "values", S1L, S1S, R1L, R1S),
        (2, 1, "values", S2L, S2S, R2L, R2S),
        (3, 1, "values", S3L, S3S, R3L, R3S),
        (1, 3, "gate", S4L, S4S, R4L, R4S),
    ]

    def pieces(r, d):
        g, n, kind = rings[r][:3]
        d_up, d_at = lax.div(d, 4), lax.rem(d, 4)
        got = []
        if kind != "gate":
            got.append((0, 384, PV[pl.ds(g, n), d_up, :, d_at]))
        if kind != "values":
            got.append((got[0][1] if got else 0, 256, PG[pl.ds(g, n), d_up, :, d_at]))
        return got

    def hop(r, k):
        out_l, out_s, in_l, in_s = rings[r][3:]
        if k:
            arrived(in_l.at[k - 1], sem_l.at[r, k - 1])
        for lo, wide, v in pieces(r, m8(z + (4 - k) * sg)):
            if k:
                v = v + in_l[k - 1, :, :, :, lo : lo + wide].astype(F32)
            out_l[k, :, :, :, lo : lo + wide] = v.astype(BF16)
        send(out_l.at[k], in_l.at[k], sem_l.at[r, k], dev(z_=m8(z + sg)))
        if k < 3:
            if k:
                arrived(in_s.at[k - 1], sem_sh.at[r, k - 1])
            for lo, wide, v in pieces(r, m8(z - (3 - k) * sg)):
                if k:
                    v = v + in_s[k - 1, :, :, :, lo : lo + wide].astype(F32)
                out_s[k, :, :, :, lo : lo + wide] = v.astype(BF16)
            send(out_s.at[k], in_s.at[k], sem_sh.at[r, k], dev(z_=m8(z - sg)))

    def last(r):
        g, n, kind, _, _, in_l, in_s = rings[r]
        arrived(in_l.at[3], sem_l.at[r, 3])
        arrived(in_s.at[2], sem_sh.at[r, 2])
        for lo, wide, v in pieces(r, z):
            v = v + in_l[3, :, :, :, lo : lo + wide].astype(F32) + in_s[2, :, :, :, lo : lo + wide].astype(F32)
            ref = RV if wide == 384 else RG
            for j in range(n):
                a = groups[0][g + j] + upper * (groups[1][g + j] - groups[0][g + j])
                for i in range(4):
                    ref[a + upper * (i - a), i + upper * (a - i)] = v[j, i]

    product(0)
    hop(0, 0)
    for at in (-1, 1):
        for h in range(2):
            relay(h, m4(legs[h][2] + at * sg))
    hop(0, 1)
    for h in range(2):
        relay(h, m4(legs[h][2] + 2))
    came(1)
    came(2)
    product(1)
    hop(1, 0)
    product(2)
    hop(2, 0)
    hop(0, 2)
    hop(1, 1)
    hop(2, 1)
    hop(0, 3)
    came(3)
    product(3)
    hop(3, 0)
    hop(1, 2)
    hop(2, 2)
    hop(3, 1)
    hop(1, 3)
    hop(2, 3)
    hop(3, 2)
    last(0)
    last(1)
    hop(3, 3)
    last(2)
    hop(4, 0)
    last(3)

    scale = lax.rsqrt(RV[:, :, :, 256:384].reshape(256, 128)[:, SQ : SQ + 1] * (1.0 / 8192) + EPSILON)
    HS[...] = (RV[3, 3, :, 0:256] * scale[240:256]).astype(BF16)
    send(HS, HR, sem_h, dev(z_=m8(z + 1)))
    extra = RV[:, :, :, 256:384].reshape(256, 128) * scale
    BC[c, y] = jnp.transpose(extra)[0:32].astype(BF16)
    for dc, dy in [(0, 0)] + peers:
        to_c, to_y = lax.rem(c + dc, 2), m4(y + dy)
        end_of = BC.at[c, y, :, pl.ds(128, 128)]
        send(end_of, BP.at[c, y], sem_bp.at[4 * c + y], dev(z_=m8(z + 1), c_=to_c, y_=to_y))
        if (dc, dy) != (0, 0):
            send(BC.at[c, y], BC.at[c, y], sem_bc.at[4 * c + y], dev(c_=to_c, y_=to_y))
    EXT[16:272] = (RV[:, :, :, 0:256].reshape(256, 256) * scale).astype(BF16).astype(F32)

    raw_step = extra + bias_row
    step = jnp.maximum(raw_step, 0.0) + jnp.log1p(jnp.exp(-jnp.abs(raw_step)))
    log_decay = -rate_row * step
    order_r = lax.broadcasted_iota(jnp.int32, (256, 256), 0)
    order_c = lax.broadcasted_iota(jnp.int32, (256, 256), 1)
    cum = dot((order_r >= order_c).astype(F32), log_decay, PRECISE)
    cum_rows = jnp.transpose(cum)
    end = cum[255:256]
    causal = (order_r >= order_c) & (first + order_c.astype(F32) >= start_of)
    start_last = start_of[255:256]
    low = lax.broadcasted_iota(jnp.int32, (1, 128), 1) < 64

    def expand(a):
        return jnp.concatenate(
            [
                jnp.where(low, a[:, STEP0 + 2 * i : STEP0 + 2 * i + 1], a[:, STEP0 + 2 * i + 1 : STEP0 + 2 * i + 2])
                for i in range(2)
            ],
            axis=1,
        )

    step_wide = expand(step)
    tail = expand(jnp.where(t_col >= start_last, jnp.exp(end - cum), 0.0))
    carried = expand(jnp.where(start_of < first, jnp.exp(cum), 0.0))
    PB[z] = jnp.broadcast_to(expand(jnp.where(start_last < first, jnp.exp(end), 0.0)), (8, 256))
    for o in range(1, 8):
        send(PB.at[z], PB.at[z], sem_p.at[z], dev(z_=m8(z + o)))

    arrived(HR, sem_h)
    EXT[0:16] = HR[...].astype(F32)
    hop(4, 1)

    def conv(lo, width, taps):
        acc = jnp.zeros((256, width), F32)
        for k in range(4):
            acc = acc + jnp.where(into >= 3 - k, EXT[13 + k : 269 + k, lo : lo + width], 0.0) * taps[k]
        return acc * jax.nn.sigmoid(acc)

    own_cols = pl.ds(pl.multiple_of(256 * c, 256), 256)
    inputs = conv(0, 256, [conv_v[k : k + 1, own_cols] for k in range(4)]).astype(BF16).astype(F32)
    stepped = inputs * step_wide
    to_end = (stepped * tail).astype(BF16)
    stepped = stepped.astype(BF16)

    for dc, dy in peers:
        pc, py = lax.rem(c + dc, 2), m4(y + dy)
        arrived(BC.at[pc, py], sem_bc.at[4 * pc + py])
    hop(4, 2)
    for at in range(8):
        arrived(BP.at[at // 4, at % 4], sem_bp.at[at])
    before = jnp.concatenate([BP[...].reshape(256, 128), BC[...].reshape(256, 256)], axis=1).astype(F32)
    acc = jnp.zeros((256, 256), F32)
    for k in range(4):
        moved = before if k == 3 else pltpu.roll(before, 3 - k, 1)
        acc = acc + jnp.where(into_row >= 3 - k, moved[:, 128:384], 0.0) * map_taps[:, k : k + 1]
    maps = (acc * jax.nn.sigmoid(acc)).astype(BF16)
    b_rows = maps[0:128]
    c_cols = jnp.transpose(maps[128:256].astype(F32)).astype(BF16)

    state = dot(b_rows, to_end).astype(BF16)
    ST[...] = state.reshape(8, 16, 256)
    for o in range(1, 8):
        k = m8(z + o)
        send(ST.at[k], SR.at[z], sem_st.at[z], dev(z_=k))
    SR[z] = ST[z]

    scores = dot(c_cols, b_rows)
    parts = []
    for i in range(4):
        gaps = cum[:, STEP0 + i : STEP0 + i + 1] - cum_rows[STEP0 + i : STEP0 + i + 1, :]
        mixing = (jnp.exp(jnp.where(causal, gaps, -1e30)) * scores).astype(BF16)
        parts.append(dot(mixing, stepped[:, 128 * (i // 2) : 128 * (i // 2) + 128]))
    intra = jnp.concatenate([jnp.where(low, parts[0], parts[1]), jnp.where(low, parts[2], parts[3])], axis=1)
    partly = intra + skip_row * inputs
    hop(4, 3)

    for o in range(1, 8):
        k = m8(z + o)
        arrived(SR.at[k], sem_st.at[k])
        arrived(PB.at[k], sem_p.at[k])
    incoming = jnp.zeros((16, 256), F32)
    for i in range(8):
        SO[i] = incoming.astype(BF16)
        incoming = PB[i, 0:1] * incoming + SR[i].astype(F32)
    for o in range(1, 8):
        k = m8(z + o)
        send(SO.at[k], SI.at[z], sem_in.at[z], dev(z_=k))
    SI[z] = SO[z]
    last(4)
    gate = RG[...].reshape(256, 256) * scale
    gate = gate * jax.nn.sigmoid(gate)
    partly = partly * gate
    carried = carried * gate
    for o in range(1, 8):
        k = m8(z + o)
        arrived(SI.at[k], sem_in.at[k])
    gated = partly + dot(c_cols, SI[...].reshape(128, 256)) * carried
    GZ[c, z] = (gated * mix_gain[0:1, own_cols]).astype(BF16).reshape(PIECES, 256 // PIECES, 256)

    order = [z]
    for k in range(1, 4):
        order += [m8(z - k * sg), m8(z + k * sg)]
    order.append(m8(z + 4))
    for i in range(PIECES):
        block = GZ.at[c, z, i]
        send(block, block, sem_g.at[z, i], dev(z_=m8(z + sg)))
        send(block, block, sem_g.at[z, i], dev(z_=m8(z - sg)))
        send(block, block, sem_gs.at[z, i], sibling)

    own_sq = 2 * y + c
    SQB[own_sq] = lax.dot_general(
        jnp.ones((8, 256), F32), gated * gated, (((1,), (1,)), ((), ())), preferred_element_type=F32, precision=PRECISE
    )
    for dc, dy in peers:
        send(SQB.at[own_sq], SQB.at[own_sq], sem_sq.at[own_sq], dev(c_=lax.rem(c + dc, 2), y_=m4(y + dy)))
    def pass_on(o, i):
        zt = order[o]
        got = GZ.at[c, zt, i]
        arrived(got, sem_g.at[zt, i])
        if o in (1, 3, 5):
            send(got, got, sem_g.at[zt, i], dev(z_=m8(z + sg)))
        if o in (2, 4):
            send(got, got, sem_g.at[zt, i], dev(z_=m8(z - sg)))
        send(got, got, sem_gs.at[zt, i], sibling)

    def forward(o):
        for i in range(PIECES):
            pass_on(o, i)
            if o < 7:
                pass_on(o + 1, i)

    def take(o):
        zt = order[o]
        for i in range(PIECES):
            arrived(GZ.at[1 - c, zt, i], sem_gs.at[zt, i])
        if o:
            arrived(NZ.at[zt], sem_nz.at[zt])
        norm = jnp.transpose(jnp.concatenate([NZ[zt]] * 16, axis=0))[:, 0:1]
        T[o] = ((dot(GZ[0, zt].reshape(256, 256), out_w[0:256]) + dot(GZ[1, zt].reshape(256, 256), out_w[256:512])) * norm).reshape(4, 4, 16, 512)

    def along(o, level):
        over_x = (o % 2 == 0) == (level == 1)
        p = x if over_x else y

        def to(q):
            return dev(x_=q) if over_x else dev(y_=q)

        return p, to

    def quarter(o, q):
        return T[o, q] if o % 2 == 0 else T[o, :, q]

    straight = (6, 7)

    def first_out(o):
        p, to = along(o, 1)
        A1[o] = quarter(o, m4(p + 2)).astype(BF16)
        send(A1.at[o], RA1.at[o], sem_1.at[o, 0], to(m4(p + 2) if o in straight else m4(p + sg)))
        B1[o] = quarter(o, m4(p - sg)).astype(BF16)
        send(B1.at[o], RB1.at[o], sem_1.at[o, 1], to(m4(p - sg)))
        if o in straight:
            C1[o] = quarter(o, m4(p + sg)).astype(BF16)
            send(C1.at[o], RC1.at[o], sem_1.at[o, 2], to(m4(p + sg)))

    def first_relay(o):
        p, to = along(o, 1)
        arrived(RA1.at[o], sem_1.at[o, 0])
        C1[o] = (quarter(o, m4(p + sg)) + RA1[o].astype(F32)).astype(BF16)
        send(C1.at[o], RC1.at[o], sem_1.at[o, 2], to(m4(p + sg)))

    def second_out(o):
        p, _ = along(o, 1)
        arrived(RB1.at[o], sem_1.at[o, 1])
        arrived(RC1.at[o], sem_1.at[o, 2])
        summed = quarter(o, p) + RB1[o].astype(F32) + RC1[o].astype(F32)
        if o in straight:
            arrived(RA1.at[o], sem_1.at[o, 0])
            summed = summed + RA1[o].astype(F32)
        Q[o] = summed
        p, to = along(o, 2)
        for i, (out_b, in_b, q) in enumerate(((A2, RA2, m4(p + 2)), (B2, RB2, m4(p - sg)), (C2, RC2, m4(p + sg)))):
            out_b[o] = Q[o, q].astype(BF16)
            send(out_b.at[o], in_b.at[o], sem_2.at[o, i], to(q))

    block_at = f
    row_block = lax.rem(block_at, 8)
    to_core = lax.div(block_at, 8)

    def finish(o):
        p, _ = along(o, 2)
        for i, in_b in enumerate((RA2, RB2, RC2)):
            arrived(in_b.at[o], sem_2.at[o, i])
        FO[o] = (Q[o, p] + RA2[o].astype(F32) + RB2[o].astype(F32) + RC2[o].astype(F32)).astype(BF16)
        to = (2 * order[o] + to_core, s)
        own = (to[0] == s) & (s == f) if o == 0 else None
        if own is None:
            send(FO.at[o], FR.at[row_block], sem_f.at[row_block], to)
        else:
            send_or_keep(own, FO.at[o], FR.at[row_block], sem_f.at[row_block], to)

    forward(1)
    for dc, dy in peers:
        k = 2 * m4(y + dy) + lax.rem(c + dc, 2)
        arrived(SQB.at[k], sem_sq.at[k])
    NZ[z] = lax.rsqrt(jnp.sum(SQB[...], axis=0) * (1.0 / 2048) + EPSILON)
    for o in range(1, 8):
        send(NZ.at[z], NZ.at[z], sem_nz.at[z], dev(z_=m8(z + o)))
    take(0)
    first_out(0)
    forward(3)
    for o in (1, 2):
        take(o)
        first_out(o)
    first_relay(0)
    forward(5)
    for o in (3, 4):
        take(o)
        first_out(o)
    first_relay(1)
    first_relay(2)
    second_out(0)
    forward(7)
    for o in (5, 6):
        take(o)
        first_out(o)
    first_relay(3)
    first_relay(4)
    take(7)
    first_out(7)
    second_out(1)
    second_out(2)
    first_relay(5)
    second_out(3)
    second_out(4)
    for o in range(3):
        finish(o)
    second_out(6)
    second_out(5)
    second_out(7)
    for o in (3, 4, 6, 5, 7):
        finish(o)

    for i in range(8):
        arrived(FR.at[i], sem_f.at[i])
    out[...] = (tok[...].astype(F32) + FR[...].reshape(128, 512).astype(F32)).astype(BF16)

    wrap_up()


def local(
    tokens, norm_gain, gate_proj, value_proj, step_proj, state_proj, conv_value, conv_state, step_bias, decay_rate,
    skip_gain, mix_gain, out_proj, doc_lengths,
):
    vmem = pl.BlockSpec(memory_space=pltpu.VMEM)
    smem = pl.BlockSpec(memory_space=pltpu.SMEM)

    def buf(*shape, dtype=BF16):
        return pltpu.VMEM(shape, dtype)

    def dma(*shape):
        return pltpu.SemaphoreType.DMA(shape)

    return pl.pallas_call(
        body,
        out_shape=jax.ShapeDtypeStruct((128, 512), BF16),
        in_specs=[pl.BlockSpec(memory_space=pl.ANY)] * 10 + [smem] * 4,
        out_specs=vmem,
        scratch_shapes=[
            buf(128, 512),
            buf(1, 8192, dtype=F32),
            buf(512, 512),
            buf(512, 512),
            buf(512, 4, 256),
            buf(8, 512),
            buf(4, 512, dtype=F32),
            buf(4, 4, 256, dtype=F32),
            buf(1, 512, dtype=F32),
            buf(512, 512),
            buf(512, 256),
            buf(8, 16, 512),
            buf(2, 2, 4, 4, 4, 16, 512),
            buf(2, 512, 384),
            buf(2, 512, 256),
            buf(512, 384),
            buf(512, 256),
            buf(4, 2, 4, 4, 16, 384, dtype=F32),
            buf(4, 2, 4, 4, 16, 256, dtype=F32),
        ]
        + [buf(k, n, 4, 16, w) for n, w in ((1, 640), (1, 384), (1, 384), (1, 384), (3, 256)) for k in (4, 3, 4, 3)]
        + [
            buf(4, 4, 16, 384, dtype=F32),
            buf(4, 4, 16, 256, dtype=F32),
            buf(16, 256),
            buf(16, 256),
            buf(272, 256, dtype=F32),
            buf(2, 4, 32, 256),
            buf(2, 4, 32, 128),
            buf(8, 16, 256),
            buf(8, 16, 256),
            buf(8, 8, 256, dtype=F32),
            buf(8, 16, 256),
            buf(8, 16, 256),
            buf(8, 8, 256, dtype=F32),
            buf(8, 8, 256, dtype=F32),
            buf(2, 8, PIECES, 256 // PIECES, 256),
            buf(8, 4, 4, 16, 512, dtype=F32),
            buf(8, 4, 16, 512, dtype=F32),
        ]
        + [buf(8, 4, 16, 512)] * 6
        + [buf(8, 16, 512)] * 6
        + [buf(8, 16, 512)] * 2
        + [
            dma(10), dma(SENDS), dma(8), dma(8), dma(2, 4), dma(2, 4, 4), dma(2, 4), dma(2), dma(5, 4), dma(5, 3), dma(), dma(8),
            dma(8), dma(8), dma(8), dma(8), dma(8), dma(8), dma(8, PIECES), dma(8, PIECES), dma(8, 3), dma(8, 3), dma(8),
        ],
        compiler_params=pltpu.CompilerParams(collective_id=0, has_side_effects=True, vmem_limit_bytes=56 * 2**20),
        name="mixer",
    )(
        tokens, norm_gain.reshape(1, -1), gate_proj, value_proj, state_proj, step_proj.T, conv_value, conv_state, mix_gain.reshape(1, -1),
        out_proj, step_bias, decay_rate, skip_gain, doc_lengths,
    )


def solution(mesh):
    return jax.shard_map(
        local,
        mesh=mesh,
        in_specs=(
            P("seq", "fsdp"), P(), P("seq", "fsdp"), P("seq", "fsdp"), P("seq", "fsdp"), P("seq", None, None),
            P(None, "fsdp"), P(), P("fsdp"), P("fsdp"), P("fsdp"), P("fsdp"), P("fsdp", "seq"), P(),
        ),
        out_specs=P("seq", "fsdp"),
        check_vma=False,
    )
```

```python
import jax
import jax.numpy as jnp
from jax import lax
from jax.experimental import pallas as pl
from jax.experimental.pallas import tpu as pltpu
from jax.sharding import PartitionSpec as P

N = 128
EPSILON = 1e-05
PRECISE = lax.Precision.HIGHEST
MESH = pl.DeviceIdType.MESH
F32 = jnp.float32
BF16 = jnp.bfloat16
WIDE = 640
STEP0 = 32
SQ = 40
SENDS = 400
PIECES = 4


def dot(a, b, precision=None):
    return jnp.dot(a, b, preferred_element_type=F32, precision=precision)


def body(
    tok_h, gain_h, gate_h, value_h, maps_h, step_h, conv_v_h, conv_s_h, mix_gain_h, out_w_h,
    bias, rate, skip, docs,
    out,
    tok, gain, gate_w, value_w, all_maps, step_w, conv_v, conv_s, mix_gain, out_w, maps_w,
    XI, X, WV, WG, SV, SG, PV, PG, S0L, S0S, R0L, R0S, S1L, S1S, R1L, R1S, S2L, S2S, R2L, R2S, S3L, S3S, R3L, R3S, S4L, S4S, R4L, R4S, RV, RG,
    HS, HR, EXT, BC, BP, ST, SR, PB, SO, SI, SQB, NZ, GZ, T, Q, A1, B1, C1, RA1, RB1, RC1,
    A2, B2, C2, RA2, RB2, RC2, FO, FR,
    sem_load, sem_send, sem_i, sem_a, sem_y, sem_x, sem_s, sem_w, sem_l, sem_sh, sem_h, sem_bc, sem_st, sem_in, sem_sq,
    sem_p, sem_bp, sem_nz, sem_g, sem_gs, sem_1, sem_2, sem_f,
):
    s = lax.axis_index("seq")
    f = lax.axis_index("fsdp")
    z, c = lax.div(s, 2), lax.rem(s, 2)
    x, y = lax.div(f, 4), lax.rem(f, 4)
    sg = 1 - 2 * c

    def m4(v):
        return lax.rem(v + 8, 4)

    def m8(v):
        return lax.rem(v + 16, 8)

    def dev(z_=z, c_=c, x_=x, y_=y):
        return (2 * z_ + c_, 4 * x_ + y_)

    sibling = dev(c_=1 - c)
    peers = [(dc, dy) for dc in range(2) for dy in range(4) if (dc, dy) != (0, 0)]
    started = []

    def send(src, dst, sem, to):
        copy = pltpu.make_async_remote_copy(
            src_ref=src, dst_ref=dst, send_sem=sem_send.at[len(started)], recv_sem=sem,
            device_id=to, device_id_type=MESH,
        )
        copy.start()
        started.append((copy, None))

    def arrived(dst, sem):
        pltpu.make_async_remote_copy(
            src_ref=dst, dst_ref=dst, send_sem=sem_send.at[0], recv_sem=sem,
            device_id=sibling, device_id_type=MESH,
        ).wait_recv()

    def send_or_keep(own, src, dst, sem, to):
        copy = pltpu.make_async_remote_copy(
            src_ref=src, dst_ref=dst, send_sem=sem_send.at[len(started)], recv_sem=sem,
            device_id=to, device_id_type=MESH,
        )
        away = jnp.logical_not(own)

        @pl.when(away)
        def _():
            copy.start()

        @pl.when(own)
        def _():
            pltpu.make_async_copy(src, dst, sem).start()

        started.append((copy, away))

    def wrap_up():
        for copy, away in started:
            if away is None:
                copy.wait_send()
            else:

                @pl.when(away)
                def _(copy=copy):
                    copy.wait_send()

        assert len(started) <= SENDS

    barrier = pltpu.get_barrier_semaphore()
    own_leg = (lax.rem(f, 2) == c) & (lax.div(x, 2) == c)

    def greet(to):
        pl.semaphore_signal(barrier, inc=1, device_id=to, device_id_type=MESH)

    for o in (4, 3, 5, 2, 6, 1, 7):
        greet(dev(z_=m8(z + o)))
    for i in range(8):
        for to, at in (((2 * z + lax.rem(f, 2), 8 * c + i), 8 * c + i), ((2 * z + lax.div(x, 2), 2 * i + c), 2 * i + c)):

            @pl.when(jnp.logical_not(own_leg & (f == at)))
            def _(to=to):
                greet(to)

    for dc, dy in peers:
        greet(dev(c_=lax.rem(c + dc, 2), y_=m4(y + dy)))
    greet(dev(x_=m4(x + 1)))
    greet(dev(x_=m4(x - 1)))

    loads = [
        pltpu.make_async_copy(src, dst, sem_load.at[i])
        for i, (src, dst) in enumerate(
            (
                (tok_h, tok), (gain_h, gain), (value_h, value_w), (maps_h, all_maps), (step_h, step_w), (gate_h, gate_w),
                (conv_v_h, conv_v), (conv_s_h, conv_s), (mix_gain_h, mix_gain), (out_w_h, out_w),
            )
        )
    ]
    for load in loads:
        load.start()
    loads[0].wait()
    pl.semaphore_wait(barrier, 32 - 2 * own_leg.astype(jnp.int32))

    for i in range(8):
        send_or_keep(
            own_leg & (f == 8 * c + i),
            tok.at[pl.ds(16 * i, 16)], XI.at[lax.div(f, 2)], sem_i.at[lax.div(f, 2)],
            (2 * z + lax.rem(f, 2), 8 * c + i),
        )
    upper = lax.div(z, 4)
    lead, trail = x + upper * (y - x), y + upper * (x - y)
    for o in (4, 3, 5, 2, 6, 1, 7):
        to = m8(z + o)
        arrived(XI.at[to], sem_i.at[to])
        send(XI.at[to], X.at[c, upper, lead, trail, lax.rem(z, 4)], sem_a.at[z], dev(z_=to))
    arrived(XI.at[z], sem_i.at[z])
    pltpu.make_async_copy(XI.at[z], X.at[c, upper, lead, trail, lax.rem(z, 4)], sem_a.at[z]).start()

    loads[1].wait()

    gain_col = jnp.transpose(
        jnp.broadcast_to(gain[0:1, pl.ds(pl.multiple_of(512 * s, 512), 512)], (128, 512))
    )[:, 0:1]
    lane_w = lax.broadcasted_iota(jnp.int32, (512, 128), 1)
    turn = lax.rem(128 - 32 * y, 128)

    def rows_of(half, ref_v, ref_g):
        cols = pl.ds(pl.multiple_of(256 * half, 256), 256)
        ref_v[:, 0:256] = (value_w[:, cols].astype(F32) * gain_col).astype(BF16)
        maps = pltpu.roll(maps_w[:, pl.ds(pl.multiple_of(128 * half, 128), 128)].astype(F32), turn, 1)
        steps = pltpu.roll(step_w[...].astype(F32), lax.rem(8 - 4 * half, 8), 0)
        steps = jnp.concatenate([jnp.zeros((32, 512), F32), steps, jnp.zeros((88, 512), F32)], axis=0)
        extra = jnp.where(lane_w < 32, maps, 0.0) + jnp.transpose(steps)
        ref_v[:, 256:384] = (extra * gain_col).astype(BF16)
        ref_g[...] = (gate_w[:, cols].astype(F32) * gain_col).astype(BF16)

    for load in loads[2:]:
        load.wait()
    for k in range(4):

        @pl.when(x == k)
        def _(k=k):
            maps_w[...] = all_maps[:, k, :]

    rows_of(1 - c, SV, SG)
    send(SV, WV.at[c], sem_w.at[0], sibling)
    send(SG, WG.at[c], sem_w.at[1], sibling)
    rows_of(c, WV.at[c], WG.at[c])

    lane8 = lax.broadcasted_iota(jnp.int32, (8, 128), 1)
    starts = jnp.full((8, 128), 1 << 20, jnp.int32)
    total = jnp.int32(0)
    for i in range(32):
        starts = jnp.where(lane8 == i, total, starts)
        total = total + docs[i]
    starts = starts.astype(F32)[0:1]
    first = (256 * z).astype(F32)
    t_wide = first + lax.broadcasted_iota(jnp.int32, (256, 128), 0).astype(F32)
    start_of = jnp.max(jnp.where(starts <= t_wide, starts, 0.0), axis=1, keepdims=True)
    t_col = t_wide[:, 0:1]
    into = t_col - start_of
    into_row = jnp.transpose(jnp.broadcast_to(into, (256, 128)))[0:1]
    group_row = lax.broadcasted_iota(jnp.int32, (4, 256), 0) == x
    tap_row = lax.broadcasted_iota(jnp.int32, (128, 256), 0)
    map_taps = jnp.zeros((128, 256), F32)
    for k in range(4):
        own_taps = jnp.sum(jnp.where(group_row, conv_s[k], 0.0), axis=0, keepdims=True)
        map_taps = jnp.where(tap_row == k, own_taps, map_taps)
    map_taps = jnp.transpose(map_taps)
    bias_row = jnp.zeros((8, 128), F32)
    rate_row = jnp.zeros((8, 128), F32)
    lane_256 = lax.broadcasted_iota(jnp.int32, (8, 256), 1)
    skip_row = jnp.zeros((8, 256), F32)
    for i in range(4):
        bias_row = jnp.where(lane8 == STEP0 + i, bias[4 * c + i], bias_row)
        rate_row = jnp.where(lane8 == STEP0 + i, rate[4 * c + i], rate_row)
        skip_row = jnp.where(lax.div(lane_256, 64) == i, skip[4 * c + i], skip_row)
    bias_row, rate_row, skip_row = bias_row[0:1], rate_row[0:1], skip_row[0:1]

    def at_x(q):
        return dev(x_=q)

    def at_y(q):
        return dev(y_=q)

    legs = [(x, at_x, y, at_y), (y, at_y, x, at_x)]
    def spread(h, q):
        a, to, _, _ = legs[h]
        mine = X.at[c, h, a, q]
        send(mine, mine, sem_x.at[h, a, q], to(m4(a + 1)))
        send(mine, mine, sem_x.at[h, a, q], to(m4(a - 1)))

    def relay(h, q):
        a, to, _, _ = legs[h]
        near = m4(a - sg)
        got = X.at[c, h, near, q]
        arrived(got, sem_x.at[h, near, q])
        send(got, got, sem_x.at[h, near, q], to(m4(a + sg)))

    def trailing(h, q):
        arrived(X.at[c, h, legs[h][0], q], sem_y.at[h, q])

    for h, (a, _, b, to) in enumerate(legs):
        for zt in range(4):
            arrived(X.at[c, h, a, b, zt], sem_a.at[4 * h + zt])
        mine = X.at[c, h, a, b]
        send(mine, mine, sem_y.at[h, b], to(m4(b + 1)))
        send(mine, mine, sem_y.at[h, b], to(m4(b - 1)))
        spread(h, b)
    for h, (a, _, b, to) in enumerate(legs):
        near = X.at[c, h, a, m4(b - sg)]
        trailing(h, m4(b - sg))
        send(near, near, sem_y.at[h, m4(b - sg)], to(m4(b + sg)))
        spread(h, m4(b - sg))
        trailing(h, m4(b + sg))
        spread(h, m4(b + sg))
    for h, (_, _, b, _) in enumerate(legs):
        relay(h, b)
    for h, (a, _, b, _) in enumerate(legs):
        trailing(h, m4(b + 2))
        spread(h, m4(b + 2))
        send(X.at[c, h, a], X.at[c, h, a], sem_s.at[h, a], sibling)
    arrived(WV.at[1 - c], sem_w.at[0])
    arrived(WG.at[1 - c], sem_w.at[1])

    lane_e = lax.broadcasted_iota(jnp.int32, (256, 128), 1)
    groups = [[a, m4(a - sg), m4(a + sg), m4(a + 2)] for a, _, _, _ in legs]

    def came(j):
        for h, (_, _, b, _) in enumerate(legs):
            q = groups[h][j]
            for at in range(4):
                if j > 1:
                    arrived(X.at[c, h, q, at], sem_x.at[h, q, at])
            send(X.at[c, h, q], X.at[c, h, q], sem_s.at[h, q], sibling)

    def product(g):
        for h in range(2):
            arrived(X.at[1 - c, h, groups[h][g]], sem_s.at[h, groups[h][g]])
            a = X[0, h, groups[h][g]].reshape(256, 512)
            b = X[1, h, groups[h][g]].reshape(256, 512)
            p = dot(a, WV[0]) + dot(b, WV[1])
            PG[g, h] = (dot(a, WG[0]) + dot(b, WG[1])).reshape(4, 4, 16, 256)
            a, b = a.astype(F32), b.astype(F32)
            squares = jnp.sum(a * a + b * b, axis=1, keepdims=True)
            PV[g, h, :, :, :, 0:256] = p[:, 0:256].reshape(4, 4, 16, 256)
            PV[g, h, :, :, :, 256:384] = (p[:, 256:384] + jnp.where(lane_e == SQ, squares, 0.0)).reshape(4, 4, 16, 128)

    rings = [
        (0, 1, "all", S0L, S0S, R0L, R0S),
        (1, 1, "all", S1L, S1S, R1L, R1S),
        (2, 1, "all", S2L, S2S, R2L, R2S),
        (3, 1, "values", S3L, S3S, R3L, R3S),
        (3, 1, "gate", S4L, S4S, R4L, R4S),
    ]

    def pieces(r, d):
        g, n, kind = rings[r][:3]
        d_up, d_at = lax.div(d, 4), lax.rem(d, 4)
        got = []
        if kind != "gate":
            got.append((0, 384, PV[pl.ds(g, n), d_up, :, d_at]))
        if kind != "values":
            got.append((got[0][1] if got else 0, 256, PG[pl.ds(g, n), d_up, :, d_at]))
        return got

    def hop(r, k):
        out_l, out_s, in_l, in_s = rings[r][3:]
        if k:
            arrived(in_l.at[k - 1], sem_l.at[r, k - 1])
        for lo, wide, v in pieces(r, m8(z + (4 - k) * sg)):
            if k:
                v = v + in_l[k - 1, :, :, :, lo : lo + wide].astype(F32)
            out_l[k, :, :, :, lo : lo + wide] = v.astype(BF16)
        send(out_l.at[k], in_l.at[k], sem_l.at[r, k], dev(z_=m8(z + sg)))
        if k < 3:
            if k:
                arrived(in_s.at[k - 1], sem_sh.at[r, k - 1])
            for lo, wide, v in pieces(r, m8(z - (3 - k) * sg)):
                if k:
                    v = v + in_s[k - 1, :, :, :, lo : lo + wide].astype(F32)
                out_s[k, :, :, :, lo : lo + wide] = v.astype(BF16)
            send(out_s.at[k], in_s.at[k], sem_sh.at[r, k], dev(z_=m8(z - sg)))

    def last(r):
        g, n, kind, _, _, in_l, in_s = rings[r]
        arrived(in_l.at[3], sem_l.at[r, 3])
        arrived(in_s.at[2], sem_sh.at[r, 2])
        for lo, wide, v in pieces(r, z):
            v = v + in_l[3, :, :, :, lo : lo + wide].astype(F32) + in_s[2, :, :, :, lo : lo + wide].astype(F32)
            ref = RV if wide == 384 else RG
            for j in range(n):
                a = groups[0][g + j] + upper * (groups[1][g + j] - groups[0][g + j])
                for i in range(4):
                    ref[a + upper * (i - a), i + upper * (a - i)] = v[j, i]

    product(0)
    hop(0, 0)
    for at in (-1, 1):
        for h in range(2):
            relay(h, m4(legs[h][2] + at * sg))
    hop(0, 1)
    for h in range(2):
        relay(h, m4(legs[h][2] + 2))
    came(1)
    came(2)
    product(1)
    hop(1, 0)
    product(2)
    hop(2, 0)
    hop(0, 2)
    hop(1, 1)
    hop(2, 1)
    hop(0, 3)
    came(3)
    product(3)
    hop(3, 0)
    hop(1, 2)
    hop(2, 2)
    hop(3, 1)
    hop(4, 0)
    hop(1, 3)
    hop(2, 3)
    hop(3, 2)
    hop(4, 1)
    last(0)
    last(1)
    hop(3, 3)
    hop(4, 2)
    last(2)
    last(3)

    scale = lax.rsqrt(RV[:, :, :, 256:384].reshape(256, 128)[:, SQ : SQ + 1] * (1.0 / 8192) + EPSILON)
    HS[...] = (RV[3, 3, :, 0:256] * scale[240:256]).astype(BF16)
    send(HS, HR, sem_h, dev(z_=m8(z + 1)))
    extra = RV[:, :, :, 256:384].reshape(256, 128) * scale
    BC[c, y] = jnp.transpose(extra)[0:32].astype(BF16)
    for dc, dy in [(0, 0)] + peers:
        to_c, to_y = lax.rem(c + dc, 2), m4(y + dy)
        end_of = BC.at[c, y, :, pl.ds(128, 128)]
        send(end_of, BP.at[c, y], sem_bp.at[4 * c + y], dev(z_=m8(z + 1), c_=to_c, y_=to_y))
        if (dc, dy) != (0, 0):
            send(BC.at[c, y], BC.at[c, y], sem_bc.at[4 * c + y], dev(c_=to_c, y_=to_y))
    EXT[16:272] = (RV[:, :, :, 0:256].reshape(256, 256) * scale).astype(BF16).astype(F32)

    raw_step = extra + bias_row
    step = jnp.maximum(raw_step, 0.0) + jnp.log1p(jnp.exp(-jnp.abs(raw_step)))
    log_decay = -rate_row * step
    order_r = lax.broadcasted_iota(jnp.int32, (256, 256), 0)
    order_c = lax.broadcasted_iota(jnp.int32, (256, 256), 1)
    cum = dot((order_r >= order_c).astype(F32), log_decay, PRECISE)
    cum_rows = jnp.transpose(cum)
    end = cum[255:256]
    causal = (order_r >= order_c) & (first + order_c.astype(F32) >= start_of)
    start_last = start_of[255:256]
    low = lax.broadcasted_iota(jnp.int32, (1, 128), 1) < 64

    def expand(a):
        return jnp.concatenate(
            [
                jnp.where(low, a[:, STEP0 + 2 * i : STEP0 + 2 * i + 1], a[:, STEP0 + 2 * i + 1 : STEP0 + 2 * i + 2])
                for i in range(2)
            ],
            axis=1,
        )

    step_wide = expand(step)
    tail = expand(jnp.where(t_col >= start_last, jnp.exp(end - cum), 0.0))
    carried = expand(jnp.where(start_of < first, jnp.exp(cum), 0.0))
    PB[z] = jnp.broadcast_to(expand(jnp.where(start_last < first, jnp.exp(end), 0.0)), (8, 256))
    for o in range(1, 8):
        send(PB.at[z], PB.at[z], sem_p.at[z], dev(z_=m8(z + o)))

    arrived(HR, sem_h)
    EXT[0:16] = HR[...].astype(F32)
    hop(4, 3)

    def conv(lo, width, taps):
        acc = jnp.zeros((256, width), F32)
        for k in range(4):
            acc = acc + jnp.where(into >= 3 - k, EXT[13 + k : 269 + k, lo : lo + width], 0.0) * taps[k]
        return acc * jax.nn.sigmoid(acc)

    own_cols = pl.ds(pl.multiple_of(256 * c, 256), 256)
    inputs = conv(0, 256, [conv_v[k : k + 1, own_cols] for k in range(4)]).astype(BF16).astype(F32)
    stepped = inputs * step_wide
    to_end = (stepped * tail).astype(BF16)
    stepped = stepped.astype(BF16)

    for dc, dy in peers:
        pc, py = lax.rem(c + dc, 2), m4(y + dy)
        arrived(BC.at[pc, py], sem_bc.at[4 * pc + py])
    for at in range(8):
        arrived(BP.at[at // 4, at % 4], sem_bp.at[at])
    before = jnp.concatenate([BP[...].reshape(256, 128), BC[...].reshape(256, 256)], axis=1).astype(F32)
    acc = jnp.zeros((256, 256), F32)
    for k in range(4):
        moved = before if k == 3 else pltpu.roll(before, 3 - k, 1)
        acc = acc + jnp.where(into_row >= 3 - k, moved[:, 128:384], 0.0) * map_taps[:, k : k + 1]
    maps = (acc * jax.nn.sigmoid(acc)).astype(BF16)
    b_rows = maps[0:128]
    c_cols = jnp.transpose(maps[128:256].astype(F32)).astype(BF16)

    state = dot(b_rows, to_end).astype(BF16)
    ST[...] = state.reshape(8, 16, 256)
    for o in range(1, 8):
        k = m8(z + o)
        send(ST.at[k], SR.at[z], sem_st.at[z], dev(z_=k))
    SR[z] = ST[z]

    scores = dot(c_cols, b_rows)
    parts = []
    for i in range(4):
        gaps = cum[:, STEP0 + i : STEP0 + i + 1] - cum_rows[STEP0 + i : STEP0 + i + 1, :]
        mixing = (jnp.exp(jnp.where(causal, gaps, -1e30)) * scores).astype(BF16)
        parts.append(dot(mixing, stepped[:, 128 * (i // 2) : 128 * (i // 2) + 128]))
    intra = jnp.concatenate([jnp.where(low, parts[0], parts[1]), jnp.where(low, parts[2], parts[3])], axis=1)
    partly = intra + skip_row * inputs

    for o in range(1, 8):
        k = m8(z + o)
        arrived(SR.at[k], sem_st.at[k])
        arrived(PB.at[k], sem_p.at[k])
    incoming = jnp.zeros((16, 256), F32)
    for i in range(8):
        SO[i] = incoming.astype(BF16)
        incoming = PB[i, 0:1] * incoming + SR[i].astype(F32)
    for o in range(1, 8):
        k = m8(z + o)
        send(SO.at[k], SI.at[z], sem_in.at[z], dev(z_=k))
    SI[z] = SO[z]
    last(4)
    gate = RG[...].reshape(256, 256) * scale
    gate = gate * jax.nn.sigmoid(gate)
    partly = partly * gate
    carried = carried * gate
    for o in range(1, 8):
        k = m8(z + o)
        arrived(SI.at[k], sem_in.at[k])
    gated = partly + dot(c_cols, SI[...].reshape(128, 256)) * carried
    GZ[c, z] = (gated * mix_gain[0:1, own_cols]).astype(BF16).reshape(PIECES, 256 // PIECES, 256)

    order = [z]
    for k in range(1, 4):
        order += [m8(z - k * sg), m8(z + k * sg)]
    order.append(m8(z + 4))
    for i in range(PIECES):
        block = GZ.at[c, z, i]
        send(block, block, sem_g.at[z, i], dev(z_=m8(z + sg)))
        send(block, block, sem_g.at[z, i], dev(z_=m8(z - sg)))
        send(block, block, sem_gs.at[z, i], sibling)

    own_sq = 2 * y + c
    SQB[own_sq] = lax.dot_general(
        jnp.ones((8, 256), F32), gated * gated, (((1,), (1,)), ((), ())), preferred_element_type=F32, precision=PRECISE
    )
    for dc, dy in peers:
        send(SQB.at[own_sq], SQB.at[own_sq], sem_sq.at[own_sq], dev(c_=lax.rem(c + dc, 2), y_=m4(y + dy)))
    def pass_on(o, i):
        zt = order[o]
        got = GZ.at[c, zt, i]
        arrived(got, sem_g.at[zt, i])
        if o in (1, 3, 5):
            send(got, got, sem_g.at[zt, i], dev(z_=m8(z + sg)))
        if o in (2, 4):
            send(got, got, sem_g.at[zt, i], dev(z_=m8(z - sg)))
        send(got, got, sem_gs.at[zt, i], sibling)

    def forward(o):
        for i in range(PIECES):
            pass_on(o, i)
            if o < 7:
                pass_on(o + 1, i)

    def take(o):
        zt = order[o]
        for i in range(PIECES):
            arrived(GZ.at[1 - c, zt, i], sem_gs.at[zt, i])
        if o:
            arrived(NZ.at[zt], sem_nz.at[zt])
        norm = jnp.transpose(jnp.concatenate([NZ[zt]] * 16, axis=0))[:, 0:1]
        T[o] = ((dot(GZ[0, zt].reshape(256, 256), out_w[0:256]) + dot(GZ[1, zt].reshape(256, 256), out_w[256:512])) * norm).reshape(4, 4, 16, 512)

    def along(o, level):
        over_x = (o % 2 == 0) == (level == 1)
        p = x if over_x else y

        def to(q):
            return dev(x_=q) if over_x else dev(y_=q)

        return p, to

    def quarter(o, q):
        return T[o, q] if o % 2 == 0 else T[o, :, q]

    straight = (6, 7)

    def first_out(o):
        p, to = along(o, 1)
        A1[o] = quarter(o, m4(p + 2)).astype(BF16)
        send(A1.at[o], RA1.at[o], sem_1.at[o, 0], to(m4(p + 2) if o in straight else m4(p + sg)))
        B1[o] = quarter(o, m4(p - sg)).astype(BF16)
        send(B1.at[o], RB1.at[o], sem_1.at[o, 1], to(m4(p - sg)))
        if o in straight:
            C1[o] = quarter(o, m4(p + sg)).astype(BF16)
            send(C1.at[o], RC1.at[o], sem_1.at[o, 2], to(m4(p + sg)))

    def first_relay(o):
        p, to = along(o, 1)
        arrived(RA1.at[o], sem_1.at[o, 0])
        C1[o] = (quarter(o, m4(p + sg)) + RA1[o].astype(F32)).astype(BF16)
        send(C1.at[o], RC1.at[o], sem_1.at[o, 2], to(m4(p + sg)))

    def second_out(o):
        p, _ = along(o, 1)
        arrived(RB1.at[o], sem_1.at[o, 1])
        arrived(RC1.at[o], sem_1.at[o, 2])
        summed = quarter(o, p) + RB1[o].astype(F32) + RC1[o].astype(F32)
        if o in straight:
            arrived(RA1.at[o], sem_1.at[o, 0])
            summed = summed + RA1[o].astype(F32)
        Q[o] = summed
        p, to = along(o, 2)
        for i, (out_b, in_b, q) in enumerate(((A2, RA2, m4(p + 2)), (B2, RB2, m4(p - sg)), (C2, RC2, m4(p + sg)))):
            out_b[o] = Q[o, q].astype(BF16)
            send(out_b.at[o], in_b.at[o], sem_2.at[o, i], to(q))

    block_at = f
    row_block = lax.rem(block_at, 8)
    to_core = lax.div(block_at, 8)

    def finish(o):
        p, _ = along(o, 2)
        for i, in_b in enumerate((RA2, RB2, RC2)):
            arrived(in_b.at[o], sem_2.at[o, i])
        FO[o] = (Q[o, p] + RA2[o].astype(F32) + RB2[o].astype(F32) + RC2[o].astype(F32)).astype(BF16)
        to = (2 * order[o] + to_core, s)
        own = (to[0] == s) & (s == f) if o == 0 else None
        if own is None:
            send(FO.at[o], FR.at[row_block], sem_f.at[row_block], to)
        else:
            send_or_keep(own, FO.at[o], FR.at[row_block], sem_f.at[row_block], to)

    forward(1)
    for dc, dy in peers:
        k = 2 * m4(y + dy) + lax.rem(c + dc, 2)
        arrived(SQB.at[k], sem_sq.at[k])
    NZ[z] = lax.rsqrt(jnp.sum(SQB[...], axis=0) * (1.0 / 2048) + EPSILON)
    for o in range(1, 8):
        send(NZ.at[z], NZ.at[z], sem_nz.at[z], dev(z_=m8(z + o)))
    take(0)
    first_out(0)
    forward(3)
    for o in (1, 2):
        take(o)
        first_out(o)
    first_relay(0)
    forward(5)
    for o in (3, 4):
        take(o)
        first_out(o)
    first_relay(1)
    first_relay(2)
    second_out(0)
    forward(7)
    for o in (5, 6):
        take(o)
        first_out(o)
    first_relay(3)
    first_relay(4)
    take(7)
    first_out(7)
    second_out(1)
    second_out(2)
    first_relay(5)
    second_out(3)
    second_out(4)
    for o in range(3):
        finish(o)
    second_out(6)
    second_out(5)
    second_out(7)
    for o in (3, 4, 6, 5, 7):
        finish(o)

    for i in range(8):
        arrived(FR.at[i], sem_f.at[i])
    out[...] = (tok[...].astype(F32) + FR[...].reshape(128, 512).astype(F32)).astype(BF16)

    wrap_up()


def local(
    tokens, norm_gain, gate_proj, value_proj, step_proj, state_proj, conv_value, conv_state, step_bias, decay_rate,
    skip_gain, mix_gain, out_proj, doc_lengths,
):
    vmem = pl.BlockSpec(memory_space=pltpu.VMEM)
    smem = pl.BlockSpec(memory_space=pltpu.SMEM)

    def buf(*shape, dtype=BF16):
        return pltpu.VMEM(shape, dtype)

    def dma(*shape):
        return pltpu.SemaphoreType.DMA(shape)

    return pl.pallas_call(
        body,
        out_shape=jax.ShapeDtypeStruct((128, 512), BF16),
        in_specs=[pl.BlockSpec(memory_space=pl.ANY)] * 10 + [smem] * 4,
        out_specs=vmem,
        scratch_shapes=[
            buf(128, 512),
            buf(1, 8192, dtype=F32),
            buf(512, 512),
            buf(512, 512),
            buf(512, 4, 256),
            buf(8, 512),
            buf(4, 512, dtype=F32),
            buf(4, 4, 256, dtype=F32),
            buf(1, 512, dtype=F32),
            buf(512, 512),
            buf(512, 256),
            buf(8, 16, 512),
            buf(2, 2, 4, 4, 4, 16, 512),
            buf(2, 512, 384),
            buf(2, 512, 256),
            buf(512, 384),
            buf(512, 256),
            buf(4, 2, 4, 4, 16, 384, dtype=F32),
            buf(4, 2, 4, 4, 16, 256, dtype=F32),
        ]
        + [buf(k, n, 4, 16, w) for n, w in ((1, 640), (1, 640), (1, 640), (1, 384), (1, 256)) for k in (4, 3, 4, 3)]
        + [
            buf(4, 4, 16, 384, dtype=F32),
            buf(4, 4, 16, 256, dtype=F32),
            buf(16, 256),
            buf(16, 256),
            buf(272, 256, dtype=F32),
            buf(2, 4, 32, 256),
            buf(2, 4, 32, 128),
            buf(8, 16, 256),
            buf(8, 16, 256),
            buf(8, 8, 256, dtype=F32),
            buf(8, 16, 256),
            buf(8, 16, 256),
            buf(8, 8, 256, dtype=F32),
            buf(8, 8, 256, dtype=F32),
            buf(2, 8, PIECES, 256 // PIECES, 256),
            buf(8, 4, 4, 16, 512, dtype=F32),
            buf(8, 4, 16, 512, dtype=F32),
        ]
        + [buf(8, 4, 16, 512)] * 6
        + [buf(8, 16, 512)] * 6
        + [buf(8, 16, 512)] * 2
        + [
            dma(10), dma(SENDS), dma(8), dma(8), dma(2, 4), dma(2, 4, 4), dma(2, 4), dma(2), dma(5, 4), dma(5, 3), dma(), dma(8),
            dma(8), dma(8), dma(8), dma(8), dma(8), dma(8), dma(8, PIECES), dma(8, PIECES), dma(8, 3), dma(8, 3), dma(8),
        ],
        compiler_params=pltpu.CompilerParams(collective_id=0, has_side_effects=True, vmem_limit_bytes=56 * 2**20),
        name="mixer",
    )(
        tokens, norm_gain.reshape(1, -1), gate_proj, value_proj, state_proj, step_proj.T, conv_value, conv_state, mix_gain.reshape(1, -1),
        out_proj, step_bias, decay_rate, skip_gain, doc_lengths,
    )


def solution(mesh):
    return jax.shard_map(
        local,
        mesh=mesh,
        in_specs=(
            P("seq", "fsdp"), P(), P("seq", "fsdp"), P("seq", "fsdp"), P("seq", "fsdp"), P("seq", None, None),
            P(None, "fsdp"), P(), P("fsdp"), P("fsdp"), P("fsdp"), P("fsdp"), P("fsdp", "seq"), P(),
        ),
        out_specs=P("seq", "fsdp"),
        check_vma=False,
    )
```
